32 devices in a mesh: row: 8 (over y, x, core), col: 4 (over z).
Axes of the slice: x: 2, y: 2, z: 4, core: 2. Of those that a mesh axis runs over, the one named last changes fastest.
Arguments:
- trailing_in: float32 [2, 8, 256, 4, 4, 256], P(None, 'row', None, None, 'col'), may hold values from 0 to 4, as said below
Outputs:
- factored: float32 [2, 8, 256, 4, 4, 256], P(None, 'row', None, None, 'col')
The draws below stay inside these ranges and needn't reach their ends.
Inputs may be any that keep to these rules, and one draw needn't show every extreme that they name: `trailing_in`: the matrix is symmetric and positive definite.
All inputs are finite; a program needn't handle non-finite values.
Results may differ from the reference program's by a relative error of at most 0.0003.
Values sent between devices are 32-bit elements; how exact they have to be, the bound alone decides.
No kernel may reach another device: no remote copies, remote signals or barrier semaphores. Data moves between devices by JAX's collectives and lax.ppermute only.
A program may use at most 64 MiB of HBM per device.

```python
import jax
import jax.numpy as jnp
from jax import lax

NB = 256
LR = 2
LC = 4
N_ROW = 8
N_COL = 4


def draw_trailing_in(key, part):
    key = jax.random.fold_in(key, 11)
    matrix_order = LR * N_ROW * NB
    key_points, key_noise = jax.random.split(key)
    located = jax.random.normal(key_points, (matrix_order, 8), jnp.float32)
    noise_var = jnp.exp(jax.random.uniform(key_noise, (matrix_order,), jnp.float32, jnp.log(0.3), jnp.log(3.0)))
    col_ids = jnp.arange(matrix_order, dtype=jnp.int32)

    def tile_rows(tile_index):
        start = tile_index * NB
        block = lax.dynamic_slice_in_dim(located, start, NB, 0)
        block_noise = lax.dynamic_slice_in_dim(noise_var, start, NB, 0)
        differ = block[:, None, :] - located[None, :, :]
        distance = jnp.sum(differ * differ, axis=-1)
        row_ids = start + jnp.arange(NB, dtype=jnp.int32)
        on_diagonal = row_ids[:, None] == col_ids[None, :]
        return jnp.exp(-0.25 * distance) + jnp.where(on_diagonal, block_noise[:, None], jnp.float32(0.0))
    whole = lax.map(tile_rows, jnp.arange(matrix_order // NB, dtype=jnp.int32))
    return whole.reshape(LR, N_ROW, NB, LC, N_COL, NB).astype(jnp.float32)


def setup_inputs(seed: int = 0) -> dict:
    splits = jax.random.split(jax.random.key(seed), 2)
    trailing_in = draw_trailing_in(jax.random.fold_in(splits[1], 71), 0)
    return {"trailing_in": trailing_in}


HIGHEST_PRECISION = lax.Precision.HIGHEST

def solve_panel(factor_diag, column):
    return jax.scipy.linalg.solve_triangular(factor_diag, column.T, lower=True).T

def reference(trailing_in):
    matrix_order = LR * N_ROW * NB
    kernel = trailing_in.reshape(matrix_order, matrix_order)
    tile_count = matrix_order // NB
    first_col = kernel[:, :NB]
    factor_zero = jnp.linalg.cholesky(first_col[:NB])
    panel_zero = solve_panel(factor_zero, first_col)
    panel_zero = panel_zero.at[:NB].set(factor_zero)
    second_col = kernel[:, NB:2 * NB] - jnp.dot(panel_zero.astype(jnp.float32), panel_zero[NB:2 * NB].T.astype(jnp.float32), precision=HIGHEST_PRECISION, preferred_element_type=jnp.float32)
    factor_one = jnp.linalg.cholesky(second_col[NB:2 * NB])
    panel_one = solve_panel(factor_one, second_col)
    panel_one = panel_one.at[:NB].set(jnp.float32(0.0)).at[NB:2 * NB].set(factor_one)
    panels = jnp.concatenate([panel_zero, panel_one], axis=1)
    col_tiles = jnp.arange(matrix_order, dtype=jnp.int32) // NB

    def final_rows(tile_index):
        start = tile_index * NB
        kernel_block = lax.dynamic_slice_in_dim(kernel, start, NB, 0)
        panel_block = lax.dynamic_slice_in_dim(panels, start, NB, 0)
        updated = kernel_block - jnp.dot(panel_block.astype(jnp.float32), panels.T.astype(jnp.float32), precision=HIGHEST_PRECISION, preferred_element_type=jnp.float32)
        values = jnp.concatenate([panel_block, updated[:, 2 * NB:]], axis=1)
        keep = col_tiles <= tile_index
        return jnp.where(keep[None, :], values, jnp.float32(0.0))
    result = lax.map(final_rows, jnp.arange(tile_count, dtype=jnp.int32))
    return result.reshape(LR, N_ROW, NB, LC, N_COL, NB)
```

```python
import functools

import jax
import jax.numpy as jnp
from jax import lax
from jax.experimental import pallas as pl
from jax.experimental.pallas import tpu as pltpu
from jax.sharding import PartitionSpec as P

NB = 256
HALF = 128
SUB = 8
HIGHEST = lax.Precision.HIGHEST
HIGH = lax.Precision.HIGH


def mm(a, b, precision=HIGHEST):
    return lax.dot_general(
        a, b, (((1,), (0,)), ((), ())), precision=precision, preferred_element_type=jnp.float32
    )


def mm_t(a, b, precision=HIGHEST):
    return lax.dot_general(
        a, b, (((1,), (1,)), ((), ())), precision=precision, preferred_element_type=jnp.float32
    )


def t_mm(a, b, precision=HIGHEST):
    return lax.dot_general(
        a, b, (((0,), (0,)), ((), ())), precision=precision, preferred_element_type=jnp.float32
    )


def spread(x):
    return jnp.broadcast_to(x, (SUB, HALF))


def factor_half(s):
    groups = HALF // SUB
    rows = [s[SUB * g : SUB * (g + 1), :] for g in range(groups)]
    lane = lax.broadcasted_iota(jnp.int32, (SUB, HALF), 1)
    sub = lax.broadcasted_iota(jnp.int32, (SUB, HALF), 0)
    eyes = [jnp.where(lane == sub + SUB * g, 1.0, 0.0).astype(jnp.float32) for g in range(groups)]
    out_u, out_x = [], []
    for g in range(groups):
        base = SUB * g
        own = rows[g]
        own_x = eyes[g]
        a = {}
        for i in range(SUB):
            for j in range(i, SUB):
                a[i, j] = spread(own[i : i + 1, base + j : base + j + 1])
        near = None
        if g + 1 < groups:
            near = [spread(rows[g + 1][:, base + j : base + j + 1]) for j in range(SUB)]
        u = [spread(own[i : i + 1, :]) for i in range(SUB)]
        x = [spread(own_x[i : i + 1, :]) for i in range(SUB)]
        r = [None] * SUB
        l = {}
        for k in range(SUB):
            r[k] = lax.rsqrt(a[k, k])
            for j in range(k + 1, SUB):
                l[k, j] = a[k, j] * r[k]
            for i in range(k + 1, SUB):
                for j in range(i, SUB):
                    a[i, j] = a[i, j] - l[k, i] * l[k, j]
            u[k] = u[k] * r[k]
            x[k] = x[k] * r[k]
            if near is not None:
                near[k] = near[k] * r[k]
            for i in range(k + 1, SUB):
                u[i] = u[i] - l[k, i] * u[k]
                x[i] = x[i] - l[k, i] * x[k]
                if near is not None:
                    near[i] = near[i] - l[k, i] * near[k]
        final_u, final_x = u[0], x[0]
        for i in range(1, SUB):
            final_u = jnp.where(sub == i, u[i], final_u)
            final_x = jnp.where(sub == i, x[i], final_x)
        out_u.append(jnp.where(lane >= sub + base, final_u, 0.0))
        out_x.append(final_x)
        if near is not None:
            nxt, nxt_x = rows[g + 1], eyes[g + 1]
            for k in range(SUB):
                nxt = nxt - near[k] * u[k]
                nxt_x = nxt_x - near[k] * x[k]
        if g + 2 < groups:
            v, vx = list(u), list(x)
            for i in reversed(range(SUB)):
                for j in range(i + 1, SUB):
                    v[i] = v[i] - l[i, j] * v[j]
                    vx[i] = vx[i] - l[i, j] * vx[j]
                v[i] = v[i] * r[i]
                vx[i] = vx[i] * r[i]
            for h in range(g + 2, groups):
                far, far_x = rows[h], eyes[h]
                for j in range(SUB):
                    c = spread(rows[h][:, base + j : base + j + 1])
                    far = far - c * v[j]
                    far_x = far_x - c * vx[j]
                rows[h], eyes[h] = far, far_x
        if near is not None:
            rows[g + 1], eyes[g + 1] = nxt, nxt_x
    return jnp.concatenate(out_u, axis=0), jnp.concatenate(out_x, axis=0)


def factor_tile(s, u_ref, x_ref):
    zero = jnp.zeros((HALF, HALF), jnp.float32)
    u11, x11 = factor_half(s[:HALF, :HALF])
    u12 = mm(x11, s[:HALF, HALF:])
    u22, x22 = factor_half(s[HALF:, HALF:] - t_mm(u12, u12))
    x21 = -mm(x22, t_mm(u12, x11))
    u_ref[:HALF, :HALF] = u11
    u_ref[:HALF, HALF:] = u12
    u_ref[HALF:, :HALF] = zero
    u_ref[HALF:, HALF:] = u22
    x_ref[:HALF, :HALF] = x11
    x_ref[:HALF, HALF:] = zero
    x_ref[HALF:, :HALF] = x21
    x_ref[HALF:, HALF:] = x22


def tile_from(ref, start, stride):
    return jnp.concatenate(
        [ref[pl.ds(start, NB, stride=stride), :], ref[pl.ds(start + 1, NB, stride=stride), :]], axis=1
    )


def first_kernel(a_ref, u_ref, x_ref):
    factor_tile(tile_from(a_ref, 0, 2), u_ref, x_ref)


def second_kernel(x0_ref, a01_ref, a11_ref, u_ref, x_ref, w_ref):
    x0 = x0_ref[...]
    u01 = mm(x0, tile_from(a01_ref, 0, 2))
    factor_tile(tile_from(a11_ref, 0, 2) - t_mm(u01, u01), u_ref, x_ref)
    w_ref[...] = -mm(x_ref[...], t_mm(u01, x0))


def last_kernel(loc_rows, loc_cols, pos, own, r0, r1, c0, c1, u0, x0, u1, x1, w, out):
    stride = 2 * loc_cols
    prows = []
    for a in range(loc_rows):
        b0, b1 = tile_from(r0, a * 2 * NB, 2), tile_from(r1, a * 2 * NB, 2)
        prows.append(
            (mm_t(b0, x0[...], HIGH), mm_t(b0, w[...], HIGH) + mm_t(b1, x1[...], HIGH))
        )
    for b in range(loc_cols):
        tile_col = pos[1] + b * pos[3]
        d0, d1 = tile_from(c0, 2 * b, stride), tile_from(c1, 2 * b, stride)
        q0 = mm(x0[...], d0, HIGH)
        q1 = mm(w[...], d0, HIGH) + mm(x1[...], d1, HIGH)
        for a in range(loc_rows):
            tile_row = pos[0] + a * pos[2]
            start = a * NB * stride + 2 * b

            def put(value, start=start):
                out[pl.ds(start, NB, stride=stride), :] = value[:, :HALF]
                out[pl.ds(start + 1, NB, stride=stride), :] = value[:, HALF:]

            @pl.when(tile_row < tile_col)
            def _():
                put(jnp.zeros((NB, NB), jnp.float32))

            @pl.when((tile_row >= tile_col) & (tile_col >= 2))
            def _():
                put(
                    tile_from(own, start, stride)
                    - (mm(prows[a][0], q0, HIGH) + mm(prows[a][1], q1, HIGH))
                )

            if b == 0:

                @pl.when((tile_row > 0) & (tile_col == 0))
                def _():
                    put(prows[a][0])

                @pl.when((tile_row > 1) & (tile_col == 1))
                def _():
                    put(prows[a][1])

                if a == 0:

                    @pl.when((tile_row == 0) & (tile_col == 0))
                    def _():
                        put(u0[...].T)

                    @pl.when((tile_row == 1) & (tile_col == 1))
                    def _():
                        put(u1[...].T)


VMEM = pl.BlockSpec(memory_space=pltpu.VMEM)
SMEM = pl.BlockSpec(memory_space=pltpu.SMEM)
TILE = jax.ShapeDtypeStruct((NB, NB), jnp.float32)


def call(kernel, out_shape, flops, *args, smem=0):
    return pl.pallas_call(
        kernel,
        out_shape=out_shape,
        in_specs=[SMEM] * smem + [VMEM] * (len(args) - smem),
        out_specs=jax.tree.map(lambda _: VMEM, out_shape),
        compiler_params=pltpu.CompilerParams(vmem_limit_bytes=48 * 2**20),
        cost_estimate=pl.CostEstimate(flops=flops, bytes_accessed=2**22, transcendentals=0),
    )(*args)


def on_device(n_row, n_col, trailing_in):
    row = lax.axis_index("row")
    col = lax.axis_index("col")
    loc_rows, _, _, loc_cols, _, _ = trailing_in.shape
    halves = 2 * loc_cols
    x = trailing_in.reshape(loc_rows, NB, halves, HALF)

    def send(value, pairs):
        flat = [(s[0] * n_col + s[1], d[0] * n_col + d[1]) for s, d in pairs]
        return lax.ppermute(value, ("row", "col"), flat)

    corner = x[0, :, :2, :]
    planes = range(n_col)
    evens = range(2, n_row, 2)

    a00 = jnp.where(
        col == 0, corner, sum(send(corner, [((0, 0), (0, z))]) for z in range(1, n_col))
    )
    a00 = jnp.where(row == 0, a00, sum(send(a00, [((0, z), (r, z)) for z in planes]) for r in evens))
    other = send(a00, [((r, z), (r + 1, z)) for z in planes for r in range(0, n_row, 2)])
    a00 = jnp.where(row % 2 == 0, a00, other)

    pair = jnp.where(
        col == 1,
        corner,
        sum(send(corner, [((i, 1), (i, z)) for i in (0, 1)]) for z in planes if z != 1),
    )
    pair = jnp.where(
        row < 2,
        pair,
        sum(send(pair, [((i, z), (r + i, z)) for z in planes for i in (0, 1)]) for r in evens),
    )
    swap = [((r, z), (r ^ 1, z)) for z in planes for r in range(n_row)]
    other = send(pair, swap)
    a01 = jnp.where(row % 2 == 0, pair, other)
    a11 = jnp.where(row % 2 == 0, other, pair)

    bits = [1 << k for k in range(1, (n_row - 1).bit_length())]
    top = x[0]
    holders = ([0], [1])
    for first, second in zip(bits, bits[::-1]):
        pairs = []
        for mine, bit in zip(holders, (first, second)):
            new = [(h, h ^ bit) for h in mine]
            mine.extend(d for _, d in new)
            pairs += new
        got = send(top, [((s, z), (d, z)) for z in planes for s, d in pairs])
        targets = jnp.array([d for _, d in pairs], jnp.int32)
        top = jnp.where(jnp.any(targets == row), got, top)
    other = send(top, swap)
    c0 = jnp.where(row % 2 == 0, top, other)
    c1 = jnp.where(row % 2 == 0, other, top)

    left = x[:, :, :2, :]
    rows = range(n_row)
    back = send(left, [((r, 1), (r, 0)) for r in rows])
    steps, here = [], left
    for k in range(n_col - 1):
        hops = [(k, k + 1)] + ([(k + 1, k + 2)] if k + 2 < n_col else [])
        here = send(here, [((r, s), (r, d)) for r in rows for s, d in hops])
        steps.append(here)
    r0 = jnp.where(col == 0, left, steps[0])
    for k in range(1, n_col - 1):
        r0 = jnp.where(col == k + 1, steps[k], r0)
    r1 = jnp.where(col == 0, back, left)
    for k in range(n_col - 2):
        r1 = jnp.where(col == k + 2, steps[k], r1)

    def flat(value):
        return value.reshape(-1, HALF)

    u0, x0 = call(first_kernel, [TILE] * 2, 2 * 10**9, flat(a00))
    u1, x1, w = call(second_kernel, [TILE] * 3, 2 * 10**9, x0, flat(a01), flat(a11))
    pos = jnp.stack([row, col, jnp.int32(n_row), jnp.int32(n_col)]).astype(jnp.int32)
    own = flat(x)
    out = call(
        functools.partial(last_kernel, loc_rows, loc_cols),
        jax.ShapeDtypeStruct(own.shape, jnp.float32),
        4 * 10**9,
        pos, own, flat(r0), flat(r1), flat(c0), flat(c1), u0, x0, u1, x1, w,
        smem=1,
    )
    return out.reshape(trailing_in.shape)


def solution(mesh):
    return jax.shard_map(
        functools.partial(on_device, mesh.shape["row"], mesh.shape["col"]),
        mesh=mesh,
        in_specs=(P(None, "row", None, None, "col", None),),
        out_specs=P(None, "row", None, None, "col", None),
        check_vma=False,
    )
```

```python
import functools

import jax
import jax.numpy as jnp
from jax import lax
from jax.experimental import pallas as pl
from jax.experimental.pallas import tpu as pltpu
from jax.sharding import PartitionSpec as P

NB = 256
HALF = 128
SUB = 8
HIGHEST = lax.Precision.HIGHEST
HIGH = lax.Precision.HIGH


def mm(a, b, precision=HIGHEST):
    return lax.dot_general(
        a, b, (((1,), (0,)), ((), ())), precision=precision, preferred_element_type=jnp.float32
    )


def mm_t(a, b, precision=HIGHEST):
    return lax.dot_general(
        a, b, (((1,), (1,)), ((), ())), precision=precision, preferred_element_type=jnp.float32
    )


def t_mm(a, b, precision=HIGHEST):
    return lax.dot_general(
        a, b, (((0,), (0,)), ((), ())), precision=precision, preferred_element_type=jnp.float32
    )


def spread(x):
    return jnp.broadcast_to(x, (SUB, HALF))


def factor_half(s):
    groups = HALF // SUB
    rows = [s[SUB * g : SUB * (g + 1), :] for g in range(groups)]
    lane = lax.broadcasted_iota(jnp.int32, (SUB, HALF), 1)
    sub = lax.broadcasted_iota(jnp.int32, (SUB, HALF), 0)
    eyes = [jnp.where(lane == sub + SUB * g, 1.0, 0.0).astype(jnp.float32) for g in range(groups)]
    out_u, out_x = [], []
    for g in range(groups):
        base = SUB * g
        own = rows[g]
        own_x = eyes[g]
        a = {}
        for i in range(SUB):
            for j in range(i, SUB):
                a[i, j] = spread(own[i : i + 1, base + j : base + j + 1])
        near = None
        if g + 1 < groups:
            near = [spread(rows[g + 1][:, base + j : base + j + 1]) for j in range(SUB)]
        u = [spread(own[i : i + 1, :]) for i in range(SUB)]
        x = [spread(own_x[i : i + 1, :]) for i in range(SUB)]
        r = [None] * SUB
        l = {}
        for k in range(SUB):
            r[k] = lax.rsqrt(a[k, k])
            for j in range(k + 1, SUB):
                l[k, j] = a[k, j] * r[k]
            for i in range(k + 1, SUB):
                for j in range(i, SUB):
                    a[i, j] = a[i, j] - l[k, i] * l[k, j]
            u[k] = u[k] * r[k]
            x[k] = x[k] * r[k]
            if near is not None:
                near[k] = near[k] * r[k]
            for i in range(k + 1, SUB):
                u[i] = u[i] - l[k, i] * u[k]
                x[i] = x[i] - l[k, i] * x[k]
                if near is not None:
                    near[i] = near[i] - l[k, i] * near[k]
        final_u, final_x = u[0], x[0]
        for i in range(1, SUB):
            final_u = jnp.where(sub == i, u[i], final_u)
            final_x = jnp.where(sub == i, x[i], final_x)
        out_u.append(jnp.where(lane >= sub + base, final_u, 0.0))
        out_x.append(final_x)
        if near is not None:
            nxt, nxt_x = rows[g + 1], eyes[g + 1]
            for k in range(SUB):
                nxt = nxt - near[k] * u[k]
                nxt_x = nxt_x - near[k] * x[k]
        if g + 2 < groups:
            v, vx = list(u), list(x)
            for i in reversed(range(SUB)):
                for j in range(i + 1, SUB):
                    v[i] = v[i] - l[i, j] * v[j]
                    vx[i] = vx[i] - l[i, j] * vx[j]
                v[i] = v[i] * r[i]
                vx[i] = vx[i] * r[i]
            for h in range(g + 2, groups):
                far, far_x = rows[h], eyes[h]
                for j in range(SUB):
                    c = spread(rows[h][:, base + j : base + j + 1])
                    far = far - c * v[j]
                    far_x = far_x - c * vx[j]
                rows[h], eyes[h] = far, far_x
        if near is not None:
            rows[g + 1], eyes[g + 1] = nxt, nxt_x
    return jnp.concatenate(out_u, axis=0), jnp.concatenate(out_x, axis=0)


def factor_blocks(s11, s12, s22, u_ref, x_ref):
    zero = jnp.zeros((HALF, HALF), jnp.float32)
    u11, x11 = factor_half(s11)
    u12 = mm(x11, s12)
    u22, x22 = factor_half(s22 - t_mm(u12, u12))
    x21 = -mm(x22, t_mm(u12, x11))
    u_ref[:HALF, :HALF] = u11
    u_ref[:HALF, HALF:] = u12
    u_ref[HALF:, :HALF] = zero
    u_ref[HALF:, HALF:] = u22
    x_ref[:HALF, :HALF] = x11
    x_ref[:HALF, HALF:] = zero
    x_ref[HALF:, :HALF] = x21
    x_ref[HALF:, HALF:] = x22


def tile_from(ref, start, stride):
    return jnp.concatenate(
        [ref[pl.ds(start, NB, stride=stride), :], ref[pl.ds(start + 1, NB, stride=stride), :]], axis=1
    )


def square_iotas():
    return (
        lax.broadcasted_iota(jnp.int32, (HALF, HALF), 0),
        lax.broadcasted_iota(jnp.int32, (HALF, HALF), 1),
    )


def pack_kernel(loc_rows, loc_cols, own, packed, corner, left, top):
    stride = 2 * loc_cols
    for a in range(loc_rows):
        tile = tile_from(own, a * NB * stride, stride)
        left[a * NB : (a + 1) * NB, :] = tile
        if a == 0:
            corner[...] = tile
            i, j = square_iotas()
            lower = tile[HALF:, HALF:]
            packed[:HALF, :] = jnp.where(i >= j, tile[:HALF, :HALF], lower)
            packed[HALF:NB, :] = tile[:HALF, HALF:]
            diagonal = jnp.sum(jnp.where(i == j, lower, 0.0), axis=0, keepdims=True)
            packed[NB:, :] = jnp.broadcast_to(diagonal, (SUB, HALF))
    top[...] = own[: NB * stride, :]


def unpack(p):
    i, j = square_iotas()
    mixed = p[:HALF, :]
    turned = mixed.T
    b11 = jnp.where(i >= j, mixed, turned)
    diagonal = jnp.broadcast_to(p[NB : NB + 1, :], (HALF, HALF))
    b22 = jnp.where(i == j, diagonal, jnp.where(i < j, mixed, turned))
    return b11, p[HALF:NB, :], b22


def first_kernel(pos, mine, other, u_ref, x_ref):
    b11, b12, b22 = unpack(jnp.where(pos[0] % 2 == 0, mine[...], other[...]))
    factor_blocks(b11, b12, b22, u_ref, x_ref)


def second_kernel(pos, x0_ref, mine, other, u_ref, x_ref, w_ref):
    even = pos[0] % 2 == 0
    x0 = x0_ref[...]
    u01 = mm(x0, jnp.where(even, mine[...], other[...]))
    s = jnp.where(even, other[...], mine[...]) - t_mm(u01, u01)
    factor_blocks(s[:HALF, :HALF], s[:HALF, HALF:], s[HALF:, HALF:], u_ref, x_ref)
    w_ref[...] = -mm(x_ref[...], t_mm(u01, x0))


def last_kernel(
    loc_rows, loc_cols, n_steps, pos, own, mine, other, u0, x0, u1, x1, w, left, back, *rest
):
    steps, out, r0, r1 = rest[:n_steps], rest[n_steps], rest[n_steps + 1], rest[n_steps + 2]
    stride = 2 * loc_cols
    even = pos[0] % 2 == 0

    def choose(col, first, second):
        @pl.when(pos[1] == col)
        def _():
            r0[...] = first[...]
            r1[...] = second[...]

    choose(0, left, back)
    choose(1, steps[0], left)
    for k in range(2, n_steps + 1):
        choose(k, steps[k - 1], steps[k - 2])

    prows = []
    for a in range(loc_rows):
        b0, b1 = r0[a * NB : (a + 1) * NB, :], r1[a * NB : (a + 1) * NB, :]
        prows.append(
            (mm_t(b0, x0[...], HIGH), mm_t(b0, w[...], HIGH) + mm_t(b1, x1[...], HIGH))
        )
    for b in range(loc_cols):
        tile_col = pos[1] + b * pos[3]
        e, o = tile_from(mine, 2 * b, stride), tile_from(other, 2 * b, stride)
        d0, d1 = jnp.where(even, e, o), jnp.where(even, o, e)
        q0 = mm(x0[...], d0, HIGH)
        q1 = mm(w[...], d0, HIGH) + mm(x1[...], d1, HIGH)
        for a in range(loc_rows):
            tile_row = pos[0] + a * pos[2]
            start = a * NB * stride + 2 * b

            def put(value, start=start):
                out[pl.ds(start, NB, stride=stride), :] = value[:, :HALF]
                out[pl.ds(start + 1, NB, stride=stride), :] = value[:, HALF:]

            @pl.when(tile_row < tile_col)
            def _():
                put(jnp.zeros((NB, NB), jnp.float32))

            @pl.when((tile_row >= tile_col) & (tile_col >= 2))
            def _():
                put(
                    tile_from(own, start, stride)
                    - (mm(prows[a][0], q0, HIGH) + mm(prows[a][1], q1, HIGH))
                )

            if b == 0:

                @pl.when((tile_row > 0) & (tile_col == 0))
                def _():
                    put(prows[a][0])

                @pl.when((tile_row > 1) & (tile_col == 1))
                def _():
                    put(prows[a][1])

                if a == 0:

                    @pl.when((tile_row == 0) & (tile_col == 0))
                    def _():
                        put(u0[...].T)

                    @pl.when((tile_row == 1) & (tile_col == 1))
                    def _():
                        put(u1[...].T)


VMEM = pl.BlockSpec(memory_space=pltpu.VMEM)
SMEM = pl.BlockSpec(memory_space=pltpu.SMEM)


def shape(*dims):
    return jax.ShapeDtypeStruct(dims, jnp.float32)


def call(kernel, out_shape, flops, *args, smem=0, scratch=()):
    return pl.pallas_call(
        kernel,
        out_shape=out_shape,
        in_specs=[SMEM] * smem + [VMEM] * (len(args) - smem),
        out_specs=jax.tree.map(lambda _: VMEM, out_shape),
        scratch_shapes=list(scratch),
        compiler_params=pltpu.CompilerParams(vmem_limit_bytes=40 * 2**20),
        cost_estimate=pl.CostEstimate(flops=flops, bytes_accessed=2**22, transcendentals=0),
    )(*args)


def on_device(n_row, n_col, trailing_in):
    row = lax.axis_index("row")
    col = lax.axis_index("col")
    loc_rows, _, _, loc_cols, _, _ = trailing_in.shape
    stride = 2 * loc_cols
    own = trailing_in.reshape(loc_rows * NB * stride, HALF)
    pos = jnp.stack([row, col, jnp.int32(n_row), jnp.int32(n_col)]).astype(jnp.int32)

    def send(value, pairs):
        flat = [(s[0] * n_col + s[1], d[0] * n_col + d[1]) for s, d in pairs]
        return lax.ppermute(value, ("row", "col"), flat)

    def pick(index, values):
        out = values[0]
        for k, value in enumerate(values[1:], 1):
            out = jnp.where(index == k, value, out)
        return out

    packed, corner, left, top = call(
        functools.partial(pack_kernel, loc_rows, loc_cols),
        [shape(NB + SUB, HALF), shape(NB, NB), shape(loc_rows * NB, NB), shape(NB * stride, HALF)],
        10**8,
        own,
    )
    planes = range(n_col)
    rows = range(n_row)
    chips = n_row // 2
    swap = [((r, z), (r ^ 1, z)) for z in planes for r in rows]

    got = [send(packed, [((0, 0), (0, z))]) for z in planes if z > 0]
    packed = pick(col, [packed] + got)
    got = {z: send(corner, [((i, 1), (i, z)) for i in (0, 1)]) for z in planes if z != 1}
    corner = pick(col, [got[z] if z != 1 else corner for z in planes])
    got = [send(packed, [((0, z), (2 * k, z)) for z in planes]) for k in range(1, chips)]
    packed = pick(row // 2, [packed] + got)
    packed_other = send(packed, [((r, z), (r + 1, z)) for z in planes for r in range(0, n_row, 2)])
    near = [
        send(corner, [((i, z), (2 * k + i, z)) for z in planes for i in (0, 1)])
        for k in range(1, chips)
    ]

    hops = [
        [((r, s), (r, s + 1)) for r in rows for s in (k, k + 1) if s + 1 < n_col]
        for k in range(n_col - 1)
    ]
    steps = [send(left, hops[0])]
    packed_other, steps[0] = lax.optimization_barrier((packed_other, steps[0]))
    u0, x0 = call(
        first_kernel, [shape(NB, NB)] * 2, 10**10, pos, packed, packed_other, smem=1
    )
    for k in range(1, n_col - 1):
        here = steps[-1]
        if k > 1:
            here, x0 = lax.optimization_barrier((here, x0))
        steps.append(send(here, hops[k]))
    if n_col > 2:
        x0, steps[1] = lax.optimization_barrier((x0, steps[1]))
    late, x0 = lax.optimization_barrier((left, x0))
    back = send(late, [((r, 1), (r, 0)) for r in rows])
    near, x0 = lax.optimization_barrier((near, x0))
    corner = pick(row // 2, [corner] + near)
    corner_other = send(corner, swap)
    stage = packed
    bits = [1 << k for k in range(1, (n_row - 1).bit_length())]
    holders = ([0], [1])
    for first, second in zip(bits, bits[::-1]):
        pairs = []
        for mine, bit in zip(holders, (first, second)):
            new = [(h, h ^ bit) for h in mine]
            mine.extend(d for _, d in new)
            pairs += new
        top, stage = lax.optimization_barrier((top, stage))
        arrived = send(top, [((s, z), (d, z)) for z in planes for s, d in pairs])
        stage = x0
        is_target = functools.reduce(jnp.logical_or, [row == d for _, d in pairs])
        top = jnp.where(is_target, arrived, top)
    u1, x1, w = call(
        second_kernel, [shape(NB, NB)] * 3, 10**10, pos, x0, corner, corner_other, smem=1
    )
    top, u1, back, steps = lax.optimization_barrier((top, u1, back, steps))
    top_other = send(top, swap)
    out = call(
        functools.partial(last_kernel, loc_rows, loc_cols, len(steps)),
        shape(*own.shape),
        4 * 10**9,
        pos, own, top, top_other, u0, x0, u1, x1, w, left, back, *steps,
        smem=1,
        scratch=[pltpu.VMEM(left.shape, jnp.float32)] * 2,
    )
    return out.reshape(trailing_in.shape)


def solution(mesh):
    return jax.shard_map(
        functools.partial(on_device, mesh.shape["row"], mesh.shape["col"]),
        mesh=mesh,
        in_specs=(P(None, "row", None, None, "col", None),),
        out_specs=P(None, "row", None, None, "col", None),
        check_vma=False,
    )
```

```python
import functools

import jax
import jax.numpy as jnp
from jax import lax
from jax.experimental import pallas as pl
from jax.experimental.pallas import tpu as pltpu
from jax.sharding import PartitionSpec as P

NB = 256
HALF = 128
SUB = 8
HIGHEST = lax.Precision.HIGHEST
HIGH = lax.Precision.HIGH


def mm(a, b, precision=HIGHEST):
    return lax.dot_general(
        a, b, (((1,), (0,)), ((), ())), precision=precision, preferred_element_type=jnp.float32
    )


def mm_t(a, b, precision=HIGHEST):
    return lax.dot_general(
        a, b, (((1,), (1,)), ((), ())), precision=precision, preferred_element_type=jnp.float32
    )


def t_mm(a, b, precision=HIGHEST):
    return lax.dot_general(
        a, b, (((0,), (0,)), ((), ())), precision=precision, preferred_element_type=jnp.float32
    )


def spread(x):
    return jnp.broadcast_to(x, (SUB, HALF))


def factor_half(s):
    groups = HALF // SUB
    rows = [s[SUB * g : SUB * (g + 1), :] for g in range(groups)]
    lane = lax.broadcasted_iota(jnp.int32, (SUB, HALF), 1)
    sub = lax.broadcasted_iota(jnp.int32, (SUB, HALF), 0)
    eyes = [jnp.where(lane == sub + SUB * g, 1.0, 0.0).astype(jnp.float32) for g in range(groups)]
    out_u, out_x = [], []
    for g in range(groups):
        base = SUB * g
        own = rows[g]
        own_x = eyes[g]
        a = {}
        for i in range(SUB):
            for j in range(i, SUB):
                a[i, j] = spread(own[i : i + 1, base + j : base + j + 1])
        near = None
        if g + 1 < groups:
            near = [spread(rows[g + 1][:, base + j : base + j + 1]) for j in range(SUB)]
        u = [spread(own[i : i + 1, :]) for i in range(SUB)]
        x = [spread(own_x[i : i + 1, :]) for i in range(SUB)]
        r = [None] * SUB
        l = {}
        for k in range(SUB):
            r[k] = lax.rsqrt(a[k, k])
            for j in range(k + 1, SUB):
                l[k, j] = a[k, j] * r[k]
            for i in range(k + 1, SUB):
                for j in range(i, SUB):
                    a[i, j] = a[i, j] - l[k, i] * l[k, j]
            u[k] = u[k] * r[k]
            x[k] = x[k] * r[k]
            if near is not None:
                near[k] = near[k] * r[k]
            for i in range(k + 1, SUB):
                u[i] = u[i] - l[k, i] * u[k]
                x[i] = x[i] - l[k, i] * x[k]
                if near is not None:
                    near[i] = near[i] - l[k, i] * near[k]
        final_u, final_x = u[0], x[0]
        for i in range(1, SUB):
            final_u = jnp.where(sub == i, u[i], final_u)
            final_x = jnp.where(sub == i, x[i], final_x)
        out_u.append(jnp.where(lane >= sub + base, final_u, 0.0))
        out_x.append(final_x)
        if near is not None:
            nxt, nxt_x = rows[g + 1], eyes[g + 1]
            for k in range(SUB):
                nxt = nxt - near[k] * u[k]
                nxt_x = nxt_x - near[k] * x[k]
        if g + 2 < groups:
            v, vx = list(u), list(x)
            for i in reversed(range(SUB)):
                for j in range(i + 1, SUB):
                    v[i] = v[i] - l[i, j] * v[j]
                    vx[i] = vx[i] - l[i, j] * vx[j]
                v[i] = v[i] * r[i]
                vx[i] = vx[i] * r[i]
            for h in range(g + 2, groups):
                far, far_x = rows[h], eyes[h]
                for j in range(SUB):
                    c = spread(rows[h][:, base + j : base + j + 1])
                    far = far - c * v[j]
                    far_x = far_x - c * vx[j]
                rows[h], eyes[h] = far, far_x
        if near is not None:
            rows[g + 1], eyes[g + 1] = nxt, nxt_x
    return jnp.concatenate(out_u, axis=0), jnp.concatenate(out_x, axis=0)


def factor_blocks(s11, s12, s22, u_ref, x_ref):
    zero = jnp.zeros((HALF, HALF), jnp.float32)
    u11, x11 = factor_half(s11)
    u12 = mm(x11, s12)
    u22, x22 = factor_half(s22 - t_mm(u12, u12))
    x21 = -mm(x22, t_mm(u12, x11))
    u_ref[:HALF, :HALF] = u11
    u_ref[:HALF, HALF:] = u12
    u_ref[HALF:, :HALF] = zero
    u_ref[HALF:, HALF:] = u22
    x_ref[:HALF, :HALF] = x11
    x_ref[:HALF, HALF:] = zero
    x_ref[HALF:, :HALF] = x21
    x_ref[HALF:, HALF:] = x22


def tile_from(ref, start, stride):
    return jnp.concatenate(
        [ref[pl.ds(start, NB, stride=stride), :], ref[pl.ds(start + 1, NB, stride=stride), :]], axis=1
    )


def square_iotas():
    return (
        lax.broadcasted_iota(jnp.int32, (HALF, HALF), 0),
        lax.broadcasted_iota(jnp.int32, (HALF, HALF), 1),
    )


def pack_kernel(loc_rows, loc_cols, own, packed, corner, left, top):
    stride = 2 * loc_cols
    for a in range(loc_rows):
        tile = tile_from(own, a * NB * stride, stride)
        left[a * NB : (a + 1) * NB, :] = tile
        if a == 0:
            corner[...] = tile
            i, j = square_iotas()
            lower = tile[HALF:, HALF:]
            packed[:HALF, :] = jnp.where(i >= j, tile[:HALF, :HALF], lower)
            packed[HALF:NB, :] = tile[:HALF, HALF:]
            diagonal = jnp.sum(jnp.where(i == j, lower, 0.0), axis=0, keepdims=True)
            packed[NB:, :] = jnp.broadcast_to(diagonal, (SUB, HALF))
    top[...] = own[: NB * stride, :]


def unpack(p):
    i, j = square_iotas()
    mixed = p[:HALF, :]
    turned = mixed.T
    b11 = jnp.where(i >= j, mixed, turned)
    diagonal = jnp.broadcast_to(p[NB : NB + 1, :], (HALF, HALF))
    b22 = jnp.where(i == j, diagonal, jnp.where(i < j, mixed, turned))
    return b11, p[HALF:NB, :], b22


def first_kernel(pos, mine, other, u_ref, x_ref):
    b11, b12, b22 = unpack(jnp.where(pos[0] % 2 == 0, mine[...], other[...]))
    factor_blocks(b11, b12, b22, u_ref, x_ref)


def second_kernel(pos, x0_ref, mine, other, u_ref, x_ref, w_ref):
    even = pos[0] % 2 == 0
    x0 = x0_ref[...]
    u01 = mm(x0, jnp.where(even, mine[...], other[...]))
    s = jnp.where(even, other[...], mine[...]) - t_mm(u01, u01)
    factor_blocks(s[:HALF, :HALF], s[:HALF, HALF:], s[HALF:, HALF:], u_ref, x_ref)
    w_ref[...] = -mm(x_ref[...], t_mm(u01, x0))


def last_kernel(
    loc_rows, loc_cols, n_steps, pos, own, mine, other, u0, x0, u1, x1, w, left, back, *rest
):
    steps, out, r0, r1 = rest[:n_steps], rest[n_steps], rest[n_steps + 1], rest[n_steps + 2]
    stride = 2 * loc_cols
    even = pos[0] % 2 == 0

    def choose(col, first, second):
        @pl.when(pos[1] == col)
        def _():
            r0[...] = first[...]
            r1[...] = second[...]

    choose(0, left, back)
    choose(1, steps[0], left)
    for k in range(2, n_steps + 1):
        choose(k, steps[k - 1], steps[k - 2])

    prows = []
    for a in range(loc_rows):
        b0, b1 = r0[a * NB : (a + 1) * NB, :], r1[a * NB : (a + 1) * NB, :]
        prows.append(
            (mm_t(b0, x0[...], HIGH), mm_t(b0, w[...], HIGH) + mm_t(b1, x1[...], HIGH))
        )
    for b in range(loc_cols):
        tile_col = pos[1] + b * pos[3]
        e, o = tile_from(mine, 2 * b, stride), tile_from(other, 2 * b, stride)
        d0, d1 = jnp.where(even, e, o), jnp.where(even, o, e)
        q0 = mm(x0[...], d0, HIGH)
        q1 = mm(w[...], d0, HIGH) + mm(x1[...], d1, HIGH)
        for a in range(loc_rows):
            tile_row = pos[0] + a * pos[2]
            start = a * NB * stride + 2 * b

            def put(value, start=start):
                out[pl.ds(start, NB, stride=stride), :] = value[:, :HALF]
                out[pl.ds(start + 1, NB, stride=stride), :] = value[:, HALF:]

            @pl.when(tile_row < tile_col)
            def _():
                put(jnp.zeros((NB, NB), jnp.float32))

            @pl.when((tile_row >= tile_col) & (tile_col >= 2))
            def _():
                put(
                    tile_from(own, start, stride)
                    - (mm(prows[a][0], q0, HIGH) + mm(prows[a][1], q1, HIGH))
                )

            if b == 0:

                @pl.when((tile_row > 0) & (tile_col == 0))
                def _():
                    put(prows[a][0])

                @pl.when((tile_row > 1) & (tile_col == 1))
                def _():
                    put(prows[a][1])

                if a == 0:

                    @pl.when((tile_row == 0) & (tile_col == 0))
                    def _():
                        put(u0[...].T)

                    @pl.when((tile_row == 1) & (tile_col == 1))
                    def _():
                        put(u1[...].T)


VMEM = pl.BlockSpec(memory_space=pltpu.VMEM)
SMEM = pl.BlockSpec(memory_space=pltpu.SMEM)


def shape(*dims):
    return jax.ShapeDtypeStruct(dims, jnp.float32)


def call(kernel, out_shape, flops, *args, smem=0, scratch=(), vmem=16):
    return pl.pallas_call(
        kernel,
        out_shape=out_shape,
        in_specs=[SMEM] * smem + [VMEM] * (len(args) - smem),
        out_specs=jax.tree.map(lambda _: VMEM, out_shape),
        scratch_shapes=list(scratch),
        compiler_params=pltpu.CompilerParams(vmem_limit_bytes=vmem * 2**20),
        cost_estimate=pl.CostEstimate(flops=flops, bytes_accessed=2**22, transcendentals=0),
    )(*args)


def on_device(n_row, n_col, trailing_in):
    row = lax.axis_index("row")
    col = lax.axis_index("col")
    loc_rows, _, _, loc_cols, _, _ = trailing_in.shape
    stride = 2 * loc_cols
    own = trailing_in.reshape(loc_rows * NB * stride, HALF)
    pos = jnp.stack([row, col, jnp.int32(n_row), jnp.int32(n_col)]).astype(jnp.int32)

    def send(value, pairs):
        goes = {s[0] * n_col + s[1]: d[0] * n_col + d[1] for s, d in pairs}
        comes = {d: s for s, d in goes.items()}
        full = dict(goes)
        for last in range(n_row * n_col):
            if last not in goes:
                head = last
                while head in comes:
                    head = comes[head]
                full[last] = head
        return lax.ppermute(value, ("row", "col"), sorted(full.items()))

    def pick(index, values):
        out = values[0]
        for k, value in enumerate(values[1:], 1):
            out = jnp.where(index == k, value, out)
        return out

    packed, corner, left, top = call(
        functools.partial(pack_kernel, loc_rows, loc_cols),
        [shape(NB + SUB, HALF), shape(NB, NB), shape(loc_rows * NB, NB), shape(NB * stride, HALF)],
        10**8,
        own,
    )
    planes = range(n_col)
    rows = range(n_row)
    chips = n_row // 2
    swap = [((r, z), (r ^ 1, z)) for z in planes for r in rows]

    got = [send(packed, [((0, 0), (0, z))]) for z in planes if z > 0]
    packed = pick(col, [packed] + got)
    got = {z: send(corner, [((i, 1), (i, z)) for i in (0, 1)]) for z in planes if z != 1}
    corner = pick(col, [got[z] if z != 1 else corner for z in planes])
    got = [send(packed, [((0, z), (2 * k, z)) for z in planes]) for k in range(1, chips)]
    packed = pick(row // 2, [packed] + got)
    packed_other = send(packed, [((r, z), (r + 1, z)) for z in planes for r in range(0, n_row, 2)])
    near = [
        send(corner, [((i, z), (2 * k + i, z)) for z in planes for i in (0, 1)])
        for k in range(1, chips)
    ]

    hops = [
        [((r, s), (r, s + 1)) for r in rows for s in (k, k + 1) if s + 1 < n_col]
        for k in range(n_col - 1)
    ]
    steps = [send(left, hops[0])]
    packed_other, steps[0] = lax.optimization_barrier((packed_other, steps[0]))
    u0, x0 = call(
        first_kernel, [shape(NB, NB)] * 2, 10**10, pos, packed, packed_other, smem=1
    )
    for k in range(1, n_col - 1):
        here = steps[-1]
        if k > 1:
            here, x0 = lax.optimization_barrier((here, x0))
        steps.append(send(here, hops[k]))
    if n_col > 2:
        x0, steps[1] = lax.optimization_barrier((x0, steps[1]))
    late, x0 = lax.optimization_barrier((left, x0))
    back = send(late, [((r, 1), (r, 0)) for r in rows])
    near, x0 = lax.optimization_barrier((near, x0))
    corner = pick(row // 2, [corner] + near)
    corner_other = send(corner, swap)
    stage = packed
    bits = [1 << k for k in range(1, (n_row - 1).bit_length())]
    holders = ([0], [1])
    for first, second in zip(bits, bits[::-1]):
        pairs = []
        for mine, bit in zip(holders, (first, second)):
            new = [(h, h ^ bit) for h in mine]
            mine.extend(d for _, d in new)
            pairs += new
        top, stage = lax.optimization_barrier((top, stage))
        arrived = send(top, [((s, z), (d, z)) for z in planes for s, d in pairs])
        stage = x0
        is_target = functools.reduce(jnp.logical_or, [row == d for _, d in pairs])
        top = jnp.where(is_target, arrived, top)
    u1, x1, w = call(
        second_kernel, [shape(NB, NB)] * 3, 10**10, pos, x0, corner, corner_other, smem=1
    )
    top, u1, back, steps = lax.optimization_barrier((top, u1, back, steps))
    top_other = send(top, swap)
    out = call(
        functools.partial(last_kernel, loc_rows, loc_cols, len(steps)),
        shape(*own.shape),
        4 * 10**9,
        pos, own, top, top_other, u0, x0, u1, x1, w, left, back, *steps,
        smem=1,
        scratch=[pltpu.VMEM(left.shape, jnp.float32)] * 2,
        vmem=32,
    )
    return out.reshape(trailing_in.shape)


def solution(mesh):
    return jax.shard_map(
        functools.partial(on_device, mesh.shape["row"], mesh.shape["col"]),
        mesh=mesh,
        in_specs=(P(None, "row", None, None, "col", None),),
        out_specs=P(None, "row", None, None, "col", None),
        check_vma=False,
    )
```

```python
import functools

import jax
import jax.numpy as jnp
from jax import lax
from jax.experimental import pallas as pl
from jax.experimental.pallas import tpu as pltpu
from jax.sharding import PartitionSpec as P

NB = 256
HALF = 128
SUB = 8
HIGHEST = lax.Precision.HIGHEST
HIGH = lax.Precision.HIGH


def mm(a, b, precision=HIGHEST):
    return lax.dot_general(
        a, b, (((1,), (0,)), ((), ())), precision=precision, preferred_element_type=jnp.float32
    )


def mm_t(a, b, precision=HIGHEST):
    return lax.dot_general(
        a, b, (((1,), (1,)), ((), ())), precision=precision, preferred_element_type=jnp.float32
    )


def t_mm(a, b, precision=HIGHEST):
    return lax.dot_general(
        a, b, (((0,), (0,)), ((), ())), precision=precision, preferred_element_type=jnp.float32
    )


def spread(x):
    return jnp.broadcast_to(x, (SUB, HALF))


def factor_half(s):
    groups = HALF // SUB
    rows = [s[SUB * g : SUB * (g + 1), :] for g in range(groups)]
    lane = lax.broadcasted_iota(jnp.int32, (SUB, HALF), 1)
    sub = lax.broadcasted_iota(jnp.int32, (SUB, HALF), 0)
    eyes = [jnp.where(lane == sub + SUB * g, 1.0, 0.0).astype(jnp.float32) for g in range(groups)]
    out_u, out_x = [], []
    for g in range(groups):
        base = SUB * g
        own = rows[g]
        own_x = eyes[g]
        a = {}
        for i in range(SUB):
            for j in range(i, SUB):
                a[i, j] = spread(own[i : i + 1, base + j : base + j + 1])
        near = None
        if g + 1 < groups:
            near = [spread(rows[g + 1][:, base + j : base + j + 1]) for j in range(SUB)]
        u = [spread(own[i : i + 1, :]) for i in range(SUB)]
        x = [spread(own_x[i : i + 1, :]) for i in range(SUB)]
        r = [None] * SUB
        l = {}
        for k in range(SUB):
            r[k] = lax.rsqrt(a[k, k])
            for j in range(k + 1, SUB):
                l[k, j] = a[k, j] * r[k]
            for i in range(k + 1, SUB):
                for j in range(i, SUB):
                    a[i, j] = a[i, j] - l[k, i] * l[k, j]
            u[k] = u[k] * r[k]
            x[k] = x[k] * r[k]
            if near is not None:
                near[k] = near[k] * r[k]
            for i in range(k + 1, SUB):
                u[i] = u[i] - l[k, i] * u[k]
                x[i] = x[i] - l[k, i] * x[k]
                if near is not None:
                    near[i] = near[i] - l[k, i] * near[k]
        final_u, final_x = u[0], x[0]
        for i in range(1, SUB):
            final_u = jnp.where(sub == i, u[i], final_u)
            final_x = jnp.where(sub == i, x[i], final_x)
        out_u.append(jnp.where(lane >= sub + base, final_u, 0.0))
        out_x.append(final_x)
        if near is not None:
            nxt, nxt_x = rows[g + 1], eyes[g + 1]
            for k in range(SUB):
                nxt = nxt - near[k] * u[k]
                nxt_x = nxt_x - near[k] * x[k]
        if g + 2 < groups:
            v, vx = list(u), list(x)
            for i in reversed(range(SUB)):
                for j in range(i + 1, SUB):
                    v[i] = v[i] - l[i, j] * v[j]
                    vx[i] = vx[i] - l[i, j] * vx[j]
                v[i] = v[i] * r[i]
                vx[i] = vx[i] * r[i]
            for h in range(g + 2, groups):
                far, far_x = rows[h], eyes[h]
                for j in range(SUB):
                    c = spread(rows[h][:, base + j : base + j + 1])
                    far = far - c * v[j]
                    far_x = far_x - c * vx[j]
                rows[h], eyes[h] = far, far_x
        if near is not None:
            rows[g + 1], eyes[g + 1] = nxt, nxt_x
    return jnp.concatenate(out_u, axis=0), jnp.concatenate(out_x, axis=0)


def finish_blocks(u11, u12, x11, rest, u_ref, x_ref):
    zero = jnp.zeros((HALF, HALF), jnp.float32)
    u22, x22 = factor_half(rest)
    u_ref[:HALF, :HALF] = u11
    u_ref[:HALF, HALF:] = u12
    u_ref[HALF:, :HALF] = zero
    u_ref[HALF:, HALF:] = u22
    x_ref[:HALF, :HALF] = x11
    x_ref[:HALF, HALF:] = zero
    x_ref[HALF:, :HALF] = -mm(x22, t_mm(u12, x11))
    x_ref[HALF:, HALF:] = x22


def factor_blocks(s11, s12, s22, u_ref, x_ref):
    u11, x11 = factor_half(s11)
    u12 = mm(x11, s12)
    finish_blocks(u11, u12, x11, s22 - t_mm(u12, u12), u_ref, x_ref)


def tile_from(ref, start, stride):
    return jnp.concatenate(
        [ref[pl.ds(start, NB, stride=stride), :], ref[pl.ds(start + 1, NB, stride=stride), :]], axis=1
    )


def square_iotas():
    return (
        lax.broadcasted_iota(jnp.int32, (HALF, HALF), 0),
        lax.broadcasted_iota(jnp.int32, (HALF, HALF), 1),
    )


def pack_kernel(loc_rows, loc_cols, own, packed, corner, left, top_a, top_b):
    stride = 2 * loc_cols
    for a in range(loc_rows):
        tile = tile_from(own, a * NB * stride, stride)
        left[a * NB : (a + 1) * NB, :] = tile
        if a == 0:
            corner[...] = tile
            i, j = square_iotas()
            lower = tile[HALF:, HALF:]
            packed[:HALF, :] = jnp.where(i >= j, tile[:HALF, :HALF], lower)
            packed[HALF:NB, :] = tile[:HALF, HALF:]
            diagonal = jnp.sum(jnp.where(i == j, lower, 0.0), axis=0, keepdims=True)
            packed[NB:, :] = jnp.broadcast_to(diagonal, (SUB, HALF))
    half = HALF * stride
    top_a[...] = own[:half, :]
    top_b[...] = own[half : 2 * half, :]


def unpack(p):
    i, j = square_iotas()
    mixed = p[:HALF, :]
    turned = mixed.T
    b11 = jnp.where(i >= j, mixed, turned)
    diagonal = jnp.broadcast_to(p[NB : NB + 1, :], (HALF, HALF))
    b22 = jnp.where(i == j, diagonal, jnp.where(i < j, mixed, turned))
    return b11, p[HALF:NB, :], b22


def first_kernel(pos, mine, other, u_ref, x_ref, rest_ref):
    b11, b12, b22 = unpack(jnp.where(pos[0] % 2 == 0, mine[...], other[...]))
    u11, x11 = factor_half(b11)
    u12 = mm(x11, b12)
    u_ref[:HALF, :] = u11
    u_ref[HALF:, :] = u12
    x_ref[...] = x11
    rest_ref[...] = b22 - t_mm(u12, u12)


def middle_kernel(ua, xa, rest, u_ref, x_ref):
    finish_blocks(ua[:HALF, :], ua[HALF:, :], xa[...], rest[...], u_ref, x_ref)


def second_kernel(pos, x0_ref, mine, other, u_ref, x_ref, w_ref):
    even = pos[0] % 2 == 0
    x0 = x0_ref[...]
    u01 = mm(x0, jnp.where(even, mine[...], other[...]))
    s = jnp.where(even, other[...], mine[...]) - t_mm(u01, u01)
    factor_blocks(s[:HALF, :HALF], s[:HALF, HALF:], s[HALF:, HALF:], u_ref, x_ref)
    w_ref[...] = -mm(x_ref[...], t_mm(u01, x0))


def last_kernel(
    loc_rows, loc_cols, pos, own, mine_a, mine_b, other_a, other_b, u0, x0, u1, x1, w, left, right, out
):
    stride = 2 * loc_cols
    even = pos[0] % 2 == 0
    even_col = pos[1] % 2 == 0

    def top_tile(a, b, start):
        halves = [
            jnp.concatenate(
                [ref[pl.ds(start + k, HALF, stride=stride), :] for k in (0, 1)], axis=1
            )
            for ref in (a, b)
        ]
        return jnp.concatenate(halves, axis=0)

    prows = []
    for a in range(loc_rows):
        l, r = left[a * NB : (a + 1) * NB, :], right[a * NB : (a + 1) * NB, :]
        b0, b1 = jnp.where(even_col, l, r), jnp.where(even_col, r, l)
        prows.append(
            (mm_t(b0, x0[...], HIGH), mm_t(b0, w[...], HIGH) + mm_t(b1, x1[...], HIGH))
        )
    for b in range(loc_cols):
        tile_col = pos[1] + b * pos[3]
        e, o = top_tile(mine_a, mine_b, 2 * b), top_tile(other_a, other_b, 2 * b)
        d0, d1 = jnp.where(even, e, o), jnp.where(even, o, e)
        q0 = mm(x0[...], d0, HIGH)
        q1 = mm(w[...], d0, HIGH) + mm(x1[...], d1, HIGH)
        for a in range(loc_rows):
            tile_row = pos[0] + a * pos[2]
            start = a * NB * stride + 2 * b

            def put(value, start=start):
                out[pl.ds(start, NB, stride=stride), :] = value[:, :HALF]
                out[pl.ds(start + 1, NB, stride=stride), :] = value[:, HALF:]

            @pl.when(tile_row < tile_col)
            def _():
                put(jnp.zeros((NB, NB), jnp.float32))

            @pl.when((tile_row >= tile_col) & (tile_col >= 2))
            def _():
                put(
                    tile_from(own, start, stride)
                    - (mm(prows[a][0], q0, HIGH) + mm(prows[a][1], q1, HIGH))
                )

            if b == 0:

                @pl.when((tile_row > 0) & (tile_col == 0))
                def _():
                    put(prows[a][0])

                @pl.when((tile_row > 1) & (tile_col == 1))
                def _():
                    put(prows[a][1])

                if a == 0:

                    @pl.when((tile_row == 0) & (tile_col == 0))
                    def _():
                        put(u0[...].T)

                    @pl.when((tile_row == 1) & (tile_col == 1))
                    def _():
                        put(u1[...].T)


VMEM = pl.BlockSpec(memory_space=pltpu.VMEM)
SMEM = pl.BlockSpec(memory_space=pltpu.SMEM)


def shape(*dims):
    return jax.ShapeDtypeStruct(dims, jnp.float32)


def call(kernel, out_shape, flops, *args, smem=0, scratch=(), vmem=16):
    return pl.pallas_call(
        kernel,
        out_shape=out_shape,
        in_specs=[SMEM] * smem + [VMEM] * (len(args) - smem),
        out_specs=jax.tree.map(lambda _: VMEM, out_shape),
        scratch_shapes=list(scratch),
        compiler_params=pltpu.CompilerParams(vmem_limit_bytes=vmem * 2**20),
        cost_estimate=pl.CostEstimate(flops=flops, bytes_accessed=2**22, transcendentals=0),
    )(*args)


def on_device(n_row, n_col, trailing_in):
    row = lax.axis_index("row")
    col = lax.axis_index("col")
    loc_rows, _, _, loc_cols, _, _ = trailing_in.shape
    stride = 2 * loc_cols
    own = trailing_in.reshape(loc_rows * NB * stride, HALF)
    pos = jnp.stack([row, col, jnp.int32(n_row), jnp.int32(n_col)]).astype(jnp.int32)
    planes = range(n_col)
    row_bits = [1 << k for k in range(1, (n_row - 1).bit_length())]
    col_bits = [1 << k for k in range(1, (n_col - 1).bit_length())][::-1]
    after = lax.optimization_barrier

    def send(value, pairs):
        flat = [(s[0] * n_col + s[1], d[0] * n_col + d[1]) for s, d in pairs]
        return lax.ppermute(value, ("row", "col"), flat)

    def swap(value, axis, bit):
        size = n_row if axis == "row" else n_col
        return lax.ppermute(value, axis, [(i, i ^ bit) for i in range(size)])

    def spread(value, axis, bit):
        index = row if axis == "row" else col
        return jnp.where(index & bit != 0, swap(value, axis, bit), value)

    def pick(index, values):
        out = values[0]
        for k, value in enumerate(values[1:], 1):
            out = jnp.where(index == k, value, out)
        return out

    packed, corner, left, top_a, top_b = call(
        functools.partial(pack_kernel, loc_rows, loc_cols),
        [
            shape(NB + SUB, HALF),
            shape(NB, NB),
            shape(loc_rows * NB, NB),
            shape(HALF * stride, HALF),
            shape(HALF * stride, HALF),
        ],
        10**8,
        own,
    )

    got = [send(packed, [((0, 0), (0, z))]) for z in planes if z > 0]
    packed = pick(col, [packed] + got)
    corner, packed = after((corner, packed))
    got = {z: send(corner, [((i, 1), (i, z)) for i in (0, 1)]) for z in planes if z != 1}
    for bit in row_bits:
        packed = spread(packed, "row", bit)
    got, top_a, top_b, packed = after((got, top_a, top_b, packed))
    packed_other = swap(packed, "row", 1)
    corner = pick(col, [got[z] if z != 1 else corner for z in planes])

    u_half, x_half, rest = call(
        first_kernel,
        [shape(NB, HALF), shape(HALF, HALF), shape(HALF, HALF)],
        5 * 10**9,
        pos, packed, packed_other,
        smem=1,
    )
    for bit in row_bits[:-1]:
        corner = spread(corner, "row", bit)
    corner, rest = after((corner, rest))
    last_got = swap(corner, "row", row_bits[-1])
    u0, x0 = call(middle_kernel, [shape(NB, NB)] * 2, 5 * 10**9, u_half, x_half, rest)
    corner, last_got, x0 = after((corner, last_got, x0))
    corner = jnp.where(row & row_bits[-1] != 0, last_got, corner)
    corner_other = swap(corner, "row", 1)

    for bit in col_bits[:-1]:
        left = spread(left, "col", bit)
    for first, second in zip(row_bits[:-2], row_bits[:1:-1]):
        top_a = spread(top_a, "row", first)
        top_b = spread(top_b, "row", second)
    got = (
        swap(left, "col", col_bits[-1]),
        swap(top_a, "row", row_bits[-2]),
        swap(top_b, "row", row_bits[1]),
    )
    got, left, top_a, top_b, x0 = after((got, left, top_a, top_b, x0))
    left = jnp.where(col & col_bits[-1] != 0, got[0], left)
    top_a = jnp.where(row & row_bits[-2] != 0, got[1], top_a)
    top_b = jnp.where(row & row_bits[1] != 0, got[2], top_b)
    right = swap(left, "col", 1)
    top_a = spread(top_a, "row", row_bits[-1])
    top_b = spread(top_b, "row", row_bits[0])
    u1, x1, w = call(
        second_kernel, [shape(NB, NB)] * 3, 10**10, pos, x0, corner, corner_other, smem=1
    )
    top_a, top_b, right, u1 = after((top_a, top_b, right, u1))
    other_a, other_b = swap(top_a, "row", 1), swap(top_b, "row", 1)
    out = call(
        functools.partial(last_kernel, loc_rows, loc_cols),
        shape(*own.shape),
        4 * 10**9,
        pos, own, top_a, top_b, other_a, other_b, u0, x0, u1, x1, w, left, right,
        smem=1,
        vmem=32,
    )
    return out.reshape(trailing_in.shape)


def solution(mesh):
    return jax.shard_map(
        functools.partial(on_device, mesh.shape["row"], mesh.shape["col"]),
        mesh=mesh,
        in_specs=(P(None, "row", None, None, "col", None),),
        out_specs=P(None, "row", None, None, "col", None),
        check_vma=False,
    )
```

```python
import functools

import jax
import jax.numpy as jnp
from jax import lax
from jax.experimental import pallas as pl
from jax.experimental.pallas import tpu as pltpu
from jax.sharding import PartitionSpec as P

NB = 256
HALF = 128
SUB = 8
HIGHEST = lax.Precision.HIGHEST
HIGH = lax.Precision.HIGH


def mm(a, b, precision=HIGHEST):
    return lax.dot_general(
        a, b, (((1,), (0,)), ((), ())), precision=precision, preferred_element_type=jnp.float32
    )


def mm_t(a, b, precision=HIGHEST):
    return lax.dot_general(
        a, b, (((1,), (1,)), ((), ())), precision=precision, preferred_element_type=jnp.float32
    )


def t_mm(a, b, precision=HIGHEST):
    return lax.dot_general(
        a, b, (((0,), (0,)), ((), ())), precision=precision, preferred_element_type=jnp.float32
    )


def spread(x):
    return jnp.broadcast_to(x, (SUB, HALF))


def factor_half(s):
    groups = HALF // SUB
    rows = [s[SUB * g : SUB * (g + 1), :] for g in range(groups)]
    lane = lax.broadcasted_iota(jnp.int32, (SUB, HALF), 1)
    sub = lax.broadcasted_iota(jnp.int32, (SUB, HALF), 0)
    eyes = [jnp.where(lane == sub + SUB * g, 1.0, 0.0).astype(jnp.float32) for g in range(groups)]
    out_u, out_x = [], []
    for g in range(groups):
        base = SUB * g
        own = rows[g]
        own_x = eyes[g]
        a = {}
        for i in range(SUB):
            for j in range(i, SUB):
                a[i, j] = spread(own[i : i + 1, base + j : base + j + 1])
        near = None
        if g + 1 < groups:
            near = [spread(rows[g + 1][:, base + j : base + j + 1]) for j in range(SUB)]
        u = [spread(own[i : i + 1, :]) for i in range(SUB)]
        x = [spread(own_x[i : i + 1, :]) for i in range(SUB)]
        r = [None] * SUB
        l = {}
        for k in range(SUB):
            r[k] = lax.rsqrt(a[k, k])
            for j in range(k + 1, SUB):
                l[k, j] = a[k, j] * r[k]
            for i in range(k + 1, SUB):
                for j in range(i, SUB):
                    a[i, j] = a[i, j] - l[k, i] * l[k, j]
            u[k] = u[k] * r[k]
            x[k] = x[k] * r[k]
            if near is not None:
                near[k] = near[k] * r[k]
            for i in range(k + 1, SUB):
                u[i] = u[i] - l[k, i] * u[k]
                x[i] = x[i] - l[k, i] * x[k]
                if near is not None:
                    near[i] = near[i] - l[k, i] * near[k]
        final_u, final_x = u[0], x[0]
        for i in range(1, SUB):
            final_u = jnp.where(sub == i, u[i], final_u)
            final_x = jnp.where(sub == i, x[i], final_x)
        out_u.append(jnp.where(lane >= sub + base, final_u, 0.0))
        out_x.append(final_x)
        if near is not None:
            nxt, nxt_x = rows[g + 1], eyes[g + 1]
            for k in range(SUB):
                nxt = nxt - near[k] * u[k]
                nxt_x = nxt_x - near[k] * x[k]
        if g + 2 < groups:
            v, vx = list(u), list(x)
            for i in reversed(range(SUB)):
                for j in range(i + 1, SUB):
                    v[i] = v[i] - l[i, j] * v[j]
                    vx[i] = vx[i] - l[i, j] * vx[j]
                v[i] = v[i] * r[i]
                vx[i] = vx[i] * r[i]
            for h in range(g + 2, groups):
                far, far_x = rows[h], eyes[h]
                for j in range(SUB):
                    c = spread(rows[h][:, base + j : base + j + 1])
                    far = far - c * v[j]
                    far_x = far_x - c * vx[j]
                rows[h], eyes[h] = far, far_x
        if near is not None:
            rows[g + 1], eyes[g + 1] = nxt, nxt_x
    return jnp.concatenate(out_u, axis=0), jnp.concatenate(out_x, axis=0)


def finish_blocks(u11, u12, x11, rest, u_ref, x_ref):
    zero = jnp.zeros((HALF, HALF), jnp.float32)
    u22, x22 = factor_half(rest)
    u_ref[:HALF, :HALF] = u11
    u_ref[:HALF, HALF:] = u12
    u_ref[HALF:, :HALF] = zero
    u_ref[HALF:, HALF:] = u22
    x_ref[:HALF, :HALF] = x11
    x_ref[:HALF, HALF:] = zero
    x_ref[HALF:, :HALF] = -mm(x22, t_mm(u12, x11))
    x_ref[HALF:, HALF:] = x22


def factor_blocks(s11, s12, s22, u_ref, x_ref):
    u11, x11 = factor_half(s11)
    u12 = mm(x11, s12)
    finish_blocks(u11, u12, x11, s22 - t_mm(u12, u12), u_ref, x_ref)


def tile_from(ref, start, stride):
    return jnp.concatenate(
        [ref[pl.ds(start, NB, stride=stride), :], ref[pl.ds(start + 1, NB, stride=stride), :]], axis=1
    )


def square_iotas():
    return (
        lax.broadcasted_iota(jnp.int32, (HALF, HALF), 0),
        lax.broadcasted_iota(jnp.int32, (HALF, HALF), 1),
    )


def pack_kernel(loc_rows, loc_cols, own, packed, corner, top_a, top_b, *left):
    stride = 2 * loc_cols
    for a in range(loc_rows):
        tile = tile_from(own, a * NB * stride, stride)
        left[a][...] = tile
        if a == 0:
            corner[...] = tile
            i, j = square_iotas()
            lower = tile[HALF:, HALF:]
            packed[:HALF, :] = jnp.where(i >= j, tile[:HALF, :HALF], lower)
            packed[HALF:NB, :] = tile[:HALF, HALF:]
            diagonal = jnp.sum(jnp.where(i == j, lower, 0.0), axis=0, keepdims=True)
            packed[NB:, :] = jnp.broadcast_to(diagonal, (packed.shape[0] - NB, HALF))
    half = HALF * stride
    top_a[...] = own[:half, :]
    top_b[...] = own[half : 2 * half, :]


def unpack(p):
    i, j = square_iotas()
    mixed = p[:HALF, :]
    turned = mixed.T
    b11 = jnp.where(i >= j, mixed, turned)
    diagonal = jnp.broadcast_to(p[NB : NB + 1, :], (HALF, HALF))
    b22 = jnp.where(i == j, diagonal, jnp.where(i < j, mixed, turned))
    return b11, p[HALF:NB, :], b22


def first_kernel(packed, u_ref, x_ref, rest_ref):
    b11, b12, b22 = unpack(packed[...])
    u11, x11 = factor_half(b11)
    u12 = mm(x11, b12)
    u_ref[:HALF, :] = u11
    u_ref[HALF:, :] = u12
    x_ref[...] = x11
    rest_ref[...] = b22 - t_mm(u12, u12)


def middle_kernel(ua, xa, rest, u_ref, x_ref):
    finish_blocks(ua[:HALF, :], ua[HALF:, :], xa[...], rest[...], u_ref, x_ref)


def second_kernel(pos, x0_ref, mine, other, u_ref, x_ref, w_ref):
    even = pos[0] % 2 == 0
    x0 = x0_ref[...]
    u01 = mm(x0, jnp.where(even, mine[...], other[...]))
    s = jnp.where(even, other[...], mine[...]) - t_mm(u01, u01)
    factor_blocks(s[:HALF, :HALF], s[:HALF, HALF:], s[HALF:, HALF:], u_ref, x_ref)
    w_ref[...] = -mm(x_ref[...], t_mm(u01, x0))


def store_row(a, loc_cols, pos, prow0, prow1, q0, q1, u0, u1, own, out):
    stride = 2 * loc_cols
    tile_row = pos[0] + a * pos[2]
    for b in range(loc_cols):
        tile_col = pos[1] + b * pos[3]

        def put(value, start=2 * b):
            out[pl.ds(start, NB, stride=stride), :] = value[:, :HALF]
            out[pl.ds(start + 1, NB, stride=stride), :] = value[:, HALF:]

        @pl.when(tile_row < tile_col)
        def _():
            put(jnp.zeros((NB, NB), jnp.float32))

        @pl.when((tile_row >= tile_col) & (tile_col >= 2))
        def _():
            put(
                tile_from(own, 2 * b, stride)
                - (mm(prow0, q0[b][...], HIGH) + mm(prow1, q1[b][...], HIGH))
            )

        if b == 0:

            @pl.when((tile_row > 0) & (tile_col == 0))
            def _():
                put(prow0)

            @pl.when((tile_row > 1) & (tile_col == 1))
            def _():
                put(prow1)

            if a == 0:

                @pl.when((tile_row == 0) & (tile_col == 0))
                def _():
                    put(u0[...].T)

                @pl.when((tile_row == 1) & (tile_col == 1))
                def _():
                    put(u1[...].T)


def panel_row(pos, left, right, x0, x1, w):
    even_col = pos[1] % 2 == 0
    l, r = left[...], right[...]
    b0, b1 = jnp.where(even_col, l, r), jnp.where(even_col, r, l)
    return mm_t(b0, x0[...], HIGH), mm_t(b0, w[...], HIGH) + mm_t(b1, x1[...], HIGH)


def columns_kernel(
    loc_cols, pos, own, left, right, mine_a, mine_b, other_a, other_b, u0, x0, u1, x1, w, out, *q
):
    stride = 2 * loc_cols
    even = pos[0] % 2 == 0

    def top_tile(a, b, start):
        halves = [
            jnp.concatenate(
                [ref[pl.ds(start + k, HALF, stride=stride), :] for k in (0, 1)], axis=1
            )
            for ref in (a, b)
        ]
        return jnp.concatenate(halves, axis=0)

    q0, q1 = q[:loc_cols], q[loc_cols:]
    for b in range(loc_cols):
        e, o = top_tile(mine_a, mine_b, 2 * b), top_tile(other_a, other_b, 2 * b)
        d0, d1 = jnp.where(even, e, o), jnp.where(even, o, e)
        q0[b][...] = mm(x0[...], d0, HIGH)
        q1[b][...] = mm(w[...], d0, HIGH) + mm(x1[...], d1, HIGH)
    prow0, prow1 = panel_row(pos, left, right, x0, x1, w)
    store_row(0, loc_cols, pos, prow0, prow1, q0, q1, u0, u1, own, out)


def later_kernel(a, loc_cols, pos, own, left, right, x0, x1, w, *rest):
    q, out = rest[: 2 * loc_cols], rest[-1]
    prow0, prow1 = panel_row(pos, left, right, x0, x1, w)
    store_row(
        a, loc_cols, pos, prow0, prow1, q[:loc_cols], q[loc_cols:], None, None, own, out
    )


VMEM = pl.BlockSpec(memory_space=pltpu.VMEM)
SMEM = pl.BlockSpec(memory_space=pltpu.SMEM)


def shape(*dims):
    return jax.ShapeDtypeStruct(dims, jnp.float32)


def call(kernel, out_shape, flops, *args, specs=None, out_specs=None, aliases=None, grid=(), vmem=16):
    return pl.pallas_call(
        kernel,
        grid=grid,
        out_shape=out_shape,
        in_specs=specs or [VMEM] * len(args),
        out_specs=out_specs or jax.tree.map(lambda _: VMEM, out_shape),
        input_output_aliases=aliases or {},
        compiler_params=pltpu.CompilerParams(vmem_limit_bytes=vmem * 2**20),
        cost_estimate=pl.CostEstimate(flops=flops, bytes_accessed=2**22, transcendentals=0),
    )(*args)


def on_device(n_row, n_col, trailing_in):
    row = lax.axis_index("row")
    col = lax.axis_index("col")
    loc_rows, _, _, loc_cols, _, _ = trailing_in.shape
    stride = 2 * loc_cols
    chips = n_row // 2
    chip = row // 2
    own = trailing_in.reshape(loc_rows * NB * stride, HALF)
    pos = jnp.stack([row, col, jnp.int32(n_row), jnp.int32(n_col)]).astype(jnp.int32)
    row_bits = [1 << k for k in range(1, (n_row - 1).bit_length())]
    col_bits = [1 << k for k in range(1, (n_col - 1).bit_length())][::-1]
    after = lax.optimization_barrier

    def swap(value, axis, bits):
        size = n_row if axis == "row" else n_col
        return lax.ppermute(value, axis, [(i, i ^ bits) for i in range(size)])

    def pick(index, values):
        out = values[0]
        for k, value in enumerate(values[1:], 1):
            out = jnp.where(index == k, value, out)
        return out

    def scatter(value):
        size = value.shape[0] // chips
        pieces = [value[k * size : (k + 1) * size] for k in range(chips)]
        return [pieces[0]] + [swap(pieces[k], "row", 2 * k) for k in range(1, chips)]

    def along(value):
        return [value] + [swap(value, "col", k) for k in range(1, n_col)]

    def gather(value):
        return [value] + [swap(value, "row", 2 * k) for k in range(1, chips)]

    def together(values):
        return jnp.concatenate([pick(chip ^ k, values) for k in range(chips)], axis=0)

    unit = SUB * chips
    packed_rows = -(-(NB + 1) // unit) * unit
    half = HALF * stride
    packed, corner, top_a, top_b, *left = call(
        functools.partial(pack_kernel, loc_rows, loc_cols),
        [shape(packed_rows, HALF), shape(NB, NB), shape(half, HALF), shape(half, HALF)]
        + [shape(NB, NB)] * loc_rows,
        10**8,
        own,
    )

    packed = jnp.where(row % 2 == 0, packed, swap(packed, "row", 1))
    got = scatter(packed)
    got_next = scatter(corner)
    piece = pick(chip, got)
    got = along(piece)
    got_next, got[0] = after((got_next, got[0]))
    next_piece = pick(chip, got_next)
    got_next = along(next_piece)
    piece = pick(col, got)
    packed = together(gather(piece))

    top_a, top_b, left, piece = after((top_a, top_b, left, piece))
    got_left = swap(left[0], "col", col_bits[-1]) if len(col_bits) == 1 else None
    got_a = swap(top_a, "row", row_bits[0])
    got_b = swap(top_b, "row", row_bits[-1])

    u_half, x_half, rest = call(
        first_kernel,
        [shape(NB, HALF), shape(HALF, HALF), shape(HALF, HALF)],
        5 * 10**9,
        packed,
    )
    got_next, rest = after((got_next, rest))
    next_piece = pick(col ^ 1, got_next)
    got_next = gather(next_piece)
    u0, x0 = call(middle_kernel, [shape(NB, NB)] * 2, 5 * 10**9, u_half, x_half, rest)
    got_next, got_left, got_a, got_b, x0 = after((got_next, got_left, got_a, got_b, x0))
    corner = together(got_next)
    corner_other = swap(corner, "row", 1)

    def spread(value, axis, bit, got=None):
        got = swap(value, axis, bit) if got is None else got
        return jnp.where((row if axis == "row" else col) & bit != 0, got, value)

    for first, second in zip(row_bits, row_bits[::-1]):
        top_a, top_b = spread(top_a, "row", first, got_a), spread(top_b, "row", second, got_b)
        got_a = got_b = None
    for bit in col_bits:
        left[0] = spread(left[0], "col", bit, got_left)
    right = [swap(left[0], "col", 1)]
    for a in range(1, loc_rows):
        left[a], x0 = after((left[a], x0))
        for bit in col_bits:
            left[a] = spread(left[a], "col", bit)

    u1, x1, w = call(
        second_kernel,
        [shape(NB, NB)] * 3,
        10**10,
        pos, x0, corner, corner_other,
        specs=[SMEM] + [VMEM] * 3,
    )
    top_a, top_b, left, right, u1 = after((top_a, top_b, left, right, u1))
    other_a, other_b = swap(top_a, "row", 1), swap(top_b, "row", 1)
    right += [swap(left[a], "col", 1) for a in range(1, loc_rows)]

    def block(a):
        return pl.BlockSpec((NB * stride, HALF), lambda i: (a, 0))

    out, *q = call(
        functools.partial(columns_kernel, loc_cols),
        [shape(*own.shape)] + [shape(NB, NB)] * (2 * loc_cols),
        3 * 10**9,
        pos, own, left[0], right[0], top_a, top_b, other_a, other_b, u0, x0, u1, x1, w,
        specs=[SMEM, block(0)] + [VMEM] * 11,
        out_specs=[block(0)] + [VMEM] * (2 * loc_cols),
        grid=(1,),
        vmem=24,
    )
    for a in range(1, loc_rows):
        out = call(
            functools.partial(later_kernel, a, loc_cols),
            shape(*own.shape),
            10**9,
            pos, own, left[a], right[a], x0, x1, w, *q, out,
            specs=[SMEM, block(a)] + [VMEM] * (5 + 2 * loc_cols) + [pl.BlockSpec(memory_space=pl.ANY)],
            out_specs=block(a),
            grid=(1,),
            aliases={7 + 2 * loc_cols: 0},
        )
    return out.reshape(trailing_in.shape)


def solution(mesh):
    return jax.shard_map(
        functools.partial(on_device, mesh.shape["row"], mesh.shape["col"]),
        mesh=mesh,
        in_specs=(P(None, "row", None, None, "col", None),),
        out_specs=P(None, "row", None, None, "col", None),
        check_vma=False,
    )
```

```python
import functools

import jax
import jax.numpy as jnp
from jax import lax
from jax.experimental import pallas as pl
from jax.experimental.pallas import tpu as pltpu
from jax.sharding import PartitionSpec as P

NB = 256
HALF = 128
SUB = 8
HIGHEST = lax.Precision.HIGHEST
HIGH = lax.Precision.HIGH


def mm(a, b, precision=HIGHEST):
    return lax.dot_general(
        a, b, (((1,), (0,)), ((), ())), precision=precision, preferred_element_type=jnp.float32
    )


def mm_t(a, b, precision=HIGHEST):
    return lax.dot_general(
        a, b, (((1,), (1,)), ((), ())), precision=precision, preferred_element_type=jnp.float32
    )


def t_mm(a, b, precision=HIGHEST):
    return lax.dot_general(
        a, b, (((0,), (0,)), ((), ())), precision=precision, preferred_element_type=jnp.float32
    )


def spread(x):
    return jnp.broadcast_to(x, (SUB, HALF))


def factor_half(s):
    groups = HALF // SUB
    rows = [s[SUB * g : SUB * (g + 1), :] for g in range(groups)]
    lane = lax.broadcasted_iota(jnp.int32, (SUB, HALF), 1)
    sub = lax.broadcasted_iota(jnp.int32, (SUB, HALF), 0)
    eyes = [jnp.where(lane == sub + SUB * g, 1.0, 0.0).astype(jnp.float32) for g in range(groups)]
    out_u, out_x = [], []
    for g in range(groups):
        base = SUB * g
        own = rows[g]
        own_x = eyes[g]
        a = {}
        for i in range(SUB):
            for j in range(i, SUB):
                a[i, j] = spread(own[i : i + 1, base + j : base + j + 1])
        near = None
        if g + 1 < groups:
            near = [spread(rows[g + 1][:, base + j : base + j + 1]) for j in range(SUB)]
        u = [spread(own[i : i + 1, :]) for i in range(SUB)]
        x = [spread(own_x[i : i + 1, :]) for i in range(SUB)]
        r = [None] * SUB
        l = {}
        for k in range(SUB):
            r[k] = lax.rsqrt(a[k, k])
            for j in range(k + 1, SUB):
                l[k, j] = a[k, j] * r[k]
            for i in range(k + 1, SUB):
                for j in range(i, SUB):
                    a[i, j] = a[i, j] - l[k, i] * l[k, j]
            u[k] = u[k] * r[k]
            x[k] = x[k] * r[k]
            if near is not None:
                near[k] = near[k] * r[k]
            for i in range(k + 1, SUB):
                u[i] = u[i] - l[k, i] * u[k]
                x[i] = x[i] - l[k, i] * x[k]
                if near is not None:
                    near[i] = near[i] - l[k, i] * near[k]
        final_u, final_x = u[0], x[0]
        for i in range(1, SUB):
            final_u = jnp.where(sub == i, u[i], final_u)
            final_x = jnp.where(sub == i, x[i], final_x)
        out_u.append(jnp.where(lane >= sub + base, final_u, 0.0))
        out_x.append(final_x)
        if near is not None:
            nxt, nxt_x = rows[g + 1], eyes[g + 1]
            for k in range(SUB):
                nxt = nxt - near[k] * u[k]
                nxt_x = nxt_x - near[k] * x[k]
        if g + 2 < groups:
            v, vx = list(u), list(x)
            for i in reversed(range(SUB)):
                for j in range(i + 1, SUB):
                    v[i] = v[i] - l[i, j] * v[j]
                    vx[i] = vx[i] - l[i, j] * vx[j]
                v[i] = v[i] * r[i]
                vx[i] = vx[i] * r[i]
            for h in range(g + 2, groups):
                far, far_x = rows[h], eyes[h]
                for j in range(SUB):
                    c = spread(rows[h][:, base + j : base + j + 1])
                    far = far - c * v[j]
                    far_x = far_x - c * vx[j]
                rows[h], eyes[h] = far, far_x
        if near is not None:
            rows[g + 1], eyes[g + 1] = nxt, nxt_x
    return jnp.concatenate(out_u, axis=0), jnp.concatenate(out_x, axis=0)


def finish_blocks(u11, u12, x11, rest, u_ref, x_ref):
    zero = jnp.zeros((HALF, HALF), jnp.float32)
    u22, x22 = factor_half(rest)
    u_ref[:HALF, :HALF] = u11
    u_ref[:HALF, HALF:] = u12
    u_ref[HALF:, :HALF] = zero
    u_ref[HALF:, HALF:] = u22
    x_ref[:HALF, :HALF] = x11
    x_ref[:HALF, HALF:] = zero
    x_ref[HALF:, :HALF] = -mm(x22, t_mm(u12, x11))
    x_ref[HALF:, HALF:] = x22


def factor_blocks(s11, s12, s22, u_ref, x_ref):
    u11, x11 = factor_half(s11)
    u12 = mm(x11, s12)
    finish_blocks(u11, u12, x11, s22 - t_mm(u12, u12), u_ref, x_ref)


def tile_from(ref, start, stride):
    return jnp.concatenate(
        [ref[pl.ds(start, NB, stride=stride), :], ref[pl.ds(start + 1, NB, stride=stride), :]], axis=1
    )


def pack_kernel(loc_rows, loc_cols, own, top_a, top_b, *left):
    stride = 2 * loc_cols
    for a in range(loc_rows):
        left[a][...] = tile_from(own, a * NB * stride, stride)
    half = HALF * stride
    top_a[...] = own[:half, :]
    top_b[...] = own[half : 2 * half, :]


def start_blocks(s, u_ref, x_ref, rest_ref):
    u11, x11 = factor_half(s[:HALF, :HALF])
    u12 = mm(x11, s[:HALF, HALF:])
    u_ref[:HALF, :] = u11
    u_ref[HALF:, :] = u12
    x_ref[...] = x11
    rest_ref[...] = s[HALF:, HALF:] - t_mm(u12, u12)


def first_kernel(pos, mine, other, u_ref, x_ref):
    s = jnp.where(pos[0] % 2 == 0, mine[...], other[...])
    factor_blocks(s[:HALF, :HALF], s[:HALF, HALF:], s[HALF:, HALF:], u_ref, x_ref)


def second_kernel(pos, x0, mine0, mine1, other0, other1, u01_ref, u_ref, x_ref, rest_ref):
    even = pos[0] % 2 == 0
    u01 = mm(x0[...], jnp.where(even, mine1[...], other1[...]))
    u01_ref[...] = u01
    start_blocks(jnp.where(even, other0[...], mine1[...]) - t_mm(u01, u01), u_ref, x_ref, rest_ref)


def third_kernel(x0, u01, ua, xa, rest, u_ref, x_ref, w_ref):
    finish_blocks(ua[:HALF, :], ua[HALF:, :], xa[...], rest[...], u_ref, x_ref)
    w_ref[...] = -mm(x_ref[...], t_mm(u01[...], x0[...]))


def rows_kernel(loc_rows, pos, x0, x1, w, *rest):
    left, right, out = rest[:loc_rows], rest[loc_rows : 2 * loc_rows], rest[2 * loc_rows :]
    even_col = pos[1] % 2 == 0
    for a in range(loc_rows):
        l, r = left[a][...], right[a][...]
        b0, b1 = jnp.where(even_col, l, r), jnp.where(even_col, r, l)
        out[2 * a][...] = mm_t(b0, x0[...], HIGH)
        out[2 * a + 1][...] = mm_t(b0, w[...], HIGH) + mm_t(b1, x1[...], HIGH)


def last_kernel(
    loc_rows, loc_cols, pos, own, mine_a, mine_b, other_a, other_b, u0, x0, u1, x1, w, *rest
):
    prows, out = rest[: 2 * loc_rows], rest[2 * loc_rows]
    stride = 2 * loc_cols
    even = pos[0] % 2 == 0

    def top_tile(a, b, start):
        halves = [
            jnp.concatenate(
                [ref[pl.ds(start + k, HALF, stride=stride), :] for k in (0, 1)], axis=1
            )
            for ref in (a, b)
        ]
        return jnp.concatenate(halves, axis=0)

    for b in range(loc_cols):
        tile_col = pos[1] + b * pos[3]
        e, o = top_tile(mine_a, mine_b, 2 * b), top_tile(other_a, other_b, 2 * b)
        d0, d1 = jnp.where(even, e, o), jnp.where(even, o, e)
        q0 = mm(x0[...], d0, HIGH)
        q1 = mm(w[...], d0, HIGH) + mm(x1[...], d1, HIGH)
        for a in range(loc_rows):
            tile_row = pos[0] + a * pos[2]
            start = a * NB * stride + 2 * b

            def put(value, start=start):
                out[pl.ds(start, NB, stride=stride), :] = value[:, :HALF]
                out[pl.ds(start + 1, NB, stride=stride), :] = value[:, HALF:]

            @pl.when(tile_row < tile_col)
            def _():
                put(jnp.zeros((NB, NB), jnp.float32))

            @pl.when((tile_row >= tile_col) & (tile_col >= 2))
            def _():
                put(
                    tile_from(own, start, stride)
                    - (mm(prows[2 * a][...], q0, HIGH) + mm(prows[2 * a + 1][...], q1, HIGH))
                )

            if b == 0:

                @pl.when((tile_row > 0) & (tile_col == 0))
                def _():
                    put(prows[2 * a][...])

                @pl.when((tile_row > 1) & (tile_col == 1))
                def _():
                    put(prows[2 * a + 1][...])

                if a == 0:

                    @pl.when((tile_row == 0) & (tile_col == 0))
                    def _():
                        put(u0[...].T)

                    @pl.when((tile_row == 1) & (tile_col == 1))
                    def _():
                        put(u1[...].T)


VMEM = pl.BlockSpec(memory_space=pltpu.VMEM)
SMEM = pl.BlockSpec(memory_space=pltpu.SMEM)


def shape(*dims):
    return jax.ShapeDtypeStruct(dims, jnp.float32)


def call(kernel, out_shape, flops, *args, smem=0, vmem=16):
    return pl.pallas_call(
        kernel,
        out_shape=out_shape,
        in_specs=[SMEM] * smem + [VMEM] * (len(args) - smem),
        out_specs=jax.tree.map(lambda _: VMEM, out_shape),
        compiler_params=pltpu.CompilerParams(vmem_limit_bytes=vmem * 2**20),
        cost_estimate=pl.CostEstimate(flops=flops, bytes_accessed=2**22, transcendentals=0),
    )(*args)


def on_device(n_row, n_col, trailing_in):
    row = lax.axis_index("row")
    col = lax.axis_index("col")
    loc_rows, _, _, loc_cols, _, _ = trailing_in.shape
    stride = 2 * loc_cols
    chips = n_row // 2
    chip = row // 2
    own = trailing_in.reshape(loc_rows * NB * stride, HALF)
    pos = jnp.stack([row, col, jnp.int32(n_row), jnp.int32(n_col)]).astype(jnp.int32)
    row_bits = [1 << k for k in range(1, (n_row - 1).bit_length())]
    col_bits = [1 << k for k in range(1, (n_col - 1).bit_length())][::-1]
    after = lax.optimization_barrier

    def swap(value, axis, bits):
        size = n_row if axis == "row" else n_col
        return lax.ppermute(value, axis, [(i, i ^ bits) for i in range(size)])

    def pick(index, values):
        out = values[0]
        for k, value in enumerate(values[1:], 1):
            out = jnp.where(index == k, value, out)
        return out

    def spread(value, axis, bit, got=None):
        got = swap(value, axis, bit) if got is None else got
        return jnp.where((row if axis == "row" else col) & bit != 0, got, value)

    half = HALF * stride
    top_a, top_b, *left = call(
        functools.partial(pack_kernel, loc_rows, loc_cols),
        [shape(half, HALF), shape(half, HALF)] + [shape(NB, NB)] * loc_rows,
        10**8,
        own,
    )

    size = NB // chips
    pieces = [left[0][k * size : (k + 1) * size] for k in range(chips)]
    piece = pick(chip, [pieces[0]] + [swap(pieces[k], "row", 2 * k) for k in range(1, chips)])
    along = [piece] + [swap(piece, "col", k) for k in range(1, n_col)]
    pair = jnp.concatenate([pick(col, along), pick(col ^ 1, along)], axis=0)
    got = [swap(pair, "row", 2 * k) for k in range(1, chips)]

    left[0], got[0] = after((left[0], got[0]))
    got_left = swap(left[0], "col", col_bits[-1]) if len(col_bits) == 1 else None
    got = [pair] + got
    lead = [
        jnp.concatenate(
            [pick(chip ^ k, got)[j * size : (j + 1) * size] for k in range(chips)], axis=0
        )
        for j in (0, 1)
    ]
    other = swap(jnp.where(row % 2 == 0, lead[0], lead[1]), "row", 1)
    top_a, top_b, lead[0] = after((top_a, top_b, lead[0]))
    got_a = swap(top_a, "row", row_bits[0])
    got_b = swap(top_b, "row", row_bits[-1])

    u0, x0 = call(first_kernel, [shape(NB, NB)] * 2, 10**10, pos, lead[0], other, smem=1)
    got_left, got_a, got_b, lead[1], x0 = after((got_left, got_a, got_b, lead[1], x0))
    other_next = swap(lead[1], "row", 1)

    for first, second in zip(row_bits, row_bits[::-1]):
        top_a, top_b = spread(top_a, "row", first, got_a), spread(top_b, "row", second, got_b)
        got_a = got_b = None
    for bit in col_bits:
        left[0] = spread(left[0], "col", bit, got_left)
    right = [swap(left[0], "col", 1)]
    for a in range(1, loc_rows):
        left[a], x0 = after((left[a], x0))
        for bit in col_bits:
            left[a] = spread(left[a], "col", bit)

    u01, u_half, x_half, rest = call(
        second_kernel,
        [shape(NB, NB), shape(NB, HALF), shape(HALF, HALF), shape(HALF, HALF)],
        5 * 10**9,
        pos, x0, lead[0], lead[1], other, other_next,
        smem=1,
    )
    left, rest = after((left, rest))
    right += [swap(left[a], "col", 1) for a in range(1, loc_rows)]
    u1, x1, w = call(
        third_kernel, [shape(NB, NB)] * 3, 5 * 10**9, x0, u01, u_half, x_half, rest
    )
    top_a, top_b, right, x1 = after((top_a, top_b, right, x1))
    other_a, other_b = swap(top_a, "row", 1), swap(top_b, "row", 1)
    prows = call(
        functools.partial(rows_kernel, loc_rows),
        [shape(NB, NB)] * (2 * loc_rows),
        2 * 10**9,
        pos, x0, x1, w, *left, *right,
        smem=1,
    )
    out = call(
        functools.partial(last_kernel, loc_rows, loc_cols),
        shape(*own.shape),
        3 * 10**9,
        pos, own, top_a, top_b, other_a, other_b, u0, x0, u1, x1, w, *prows,
        smem=1,
        vmem=24,
    )
    return out.reshape(trailing_in.shape)


def solution(mesh):
    return jax.shard_map(
        functools.partial(on_device, mesh.shape["row"], mesh.shape["col"]),
        mesh=mesh,
        in_specs=(P(None, "row", None, None, "col", None),),
        out_specs=P(None, "row", None, None, "col", None),
        check_vma=False,
    )
```

```python
import functools

import jax
import jax.numpy as jnp
from jax import lax
from jax.experimental import pallas as pl
from jax.experimental.pallas import tpu as pltpu
from jax.sharding import PartitionSpec as P

NB = 256
HALF = 128
SUB = 8
HIGHEST = lax.Precision.HIGHEST
HIGH = lax.Precision.HIGH


def mm(a, b, precision=HIGHEST):
    return lax.dot_general(
        a, b, (((1,), (0,)), ((), ())), precision=precision, preferred_element_type=jnp.float32
    )


def mm_t(a, b, precision=HIGHEST):
    return lax.dot_general(
        a, b, (((1,), (1,)), ((), ())), precision=precision, preferred_element_type=jnp.float32
    )


def t_mm(a, b, precision=HIGHEST):
    return lax.dot_general(
        a, b, (((0,), (0,)), ((), ())), precision=precision, preferred_element_type=jnp.float32
    )


def spread(x):
    return jnp.broadcast_to(x, (SUB, HALF))


def factor_half(s):
    groups = HALF // SUB
    rows = [s[SUB * g : SUB * (g + 1), :] for g in range(groups)]
    lane = lax.broadcasted_iota(jnp.int32, (SUB, HALF), 1)
    sub = lax.broadcasted_iota(jnp.int32, (SUB, HALF), 0)
    eyes = [jnp.where(lane == sub + SUB * g, 1.0, 0.0).astype(jnp.float32) for g in range(groups)]
    out_u, out_x = [], []
    for g in range(groups):
        base = SUB * g
        own = rows[g]
        own_x = eyes[g]
        a = {}
        for i in range(SUB):
            for j in range(i, SUB):
                a[i, j] = spread(own[i : i + 1, base + j : base + j + 1])
        near = None
        if g + 1 < groups:
            near = [spread(rows[g + 1][:, base + j : base + j + 1]) for j in range(SUB)]
        u = [spread(own[i : i + 1, :]) for i in range(SUB)]
        x = [spread(own_x[i : i + 1, :]) for i in range(SUB)]
        r = [None] * SUB
        l = {}
        for k in range(SUB):
            r[k] = lax.rsqrt(a[k, k])
            for j in range(k + 1, SUB):
                l[k, j] = a[k, j] * r[k]
            for i in range(k + 1, SUB):
                for j in range(i, SUB):
                    a[i, j] = a[i, j] - l[k, i] * l[k, j]
            u[k] = u[k] * r[k]
            x[k] = x[k] * r[k]
            if near is not None:
                near[k] = near[k] * r[k]
            for i in range(k + 1, SUB):
                u[i] = u[i] - l[k, i] * u[k]
                x[i] = x[i] - l[k, i] * x[k]
                if near is not None:
                    near[i] = near[i] - l[k, i] * near[k]
        final_u, final_x = u[0], x[0]
        for i in range(1, SUB):
            final_u = jnp.where(sub == i, u[i], final_u)
            final_x = jnp.where(sub == i, x[i], final_x)
        out_u.append(jnp.where(lane >= sub + base, final_u, 0.0))
        out_x.append(final_x)
        if near is not None:
            nxt, nxt_x = rows[g + 1], eyes[g + 1]
            for k in range(SUB):
                nxt = nxt - near[k] * u[k]
                nxt_x = nxt_x - near[k] * x[k]
        if g + 2 < groups:
            v, vx = list(u), list(x)
            for i in reversed(range(SUB)):
                for j in range(i + 1, SUB):
                    v[i] = v[i] - l[i, j] * v[j]
                    vx[i] = vx[i] - l[i, j] * vx[j]
                v[i] = v[i] * r[i]
                vx[i] = vx[i] * r[i]
            for h in range(g + 2, groups):
                far, far_x = rows[h], eyes[h]
                for j in range(SUB):
                    c = spread(rows[h][:, base + j : base + j + 1])
                    far = far - c * v[j]
                    far_x = far_x - c * vx[j]
                rows[h], eyes[h] = far, far_x
        if near is not None:
            rows[g + 1], eyes[g + 1] = nxt, nxt_x
    return jnp.concatenate(out_u, axis=0), jnp.concatenate(out_x, axis=0)


def finish_blocks(u11, u12, x11, rest, u_ref, x_ref):
    zero = jnp.zeros((HALF, HALF), jnp.float32)
    u22, x22 = factor_half(rest)
    u_ref[:HALF, :HALF] = u11
    u_ref[:HALF, HALF:] = u12
    u_ref[HALF:, :HALF] = zero
    u_ref[HALF:, HALF:] = u22
    x_ref[:HALF, :HALF] = x11
    x_ref[:HALF, HALF:] = zero
    x_ref[HALF:, :HALF] = -mm(x22, t_mm(u12, x11))
    x_ref[HALF:, HALF:] = x22


def factor_blocks(s11, s12, s22, u_ref, x_ref):
    u11, x11 = factor_half(s11)
    u12 = mm(x11, s12)
    finish_blocks(u11, u12, x11, s22 - t_mm(u12, u12), u_ref, x_ref)


def tile_from(ref, start, stride):
    return jnp.concatenate(
        [ref[pl.ds(start, NB, stride=stride), :], ref[pl.ds(start + 1, NB, stride=stride), :]], axis=1
    )


def pack_kernel(loc_rows, loc_cols, own, top, left):
    stride = 2 * loc_cols
    for a in range(loc_rows):
        left[a * NB : (a + 1) * NB, :] = tile_from(own, a * NB * stride, stride)
    top[...] = own[: NB * stride, :]


def start_blocks(s, u_ref, x_ref, rest_ref):
    u11, x11 = factor_half(s[:HALF, :HALF])
    u12 = mm(x11, s[:HALF, HALF:])
    u_ref[:HALF, :] = u11
    u_ref[HALF:, :] = u12
    x_ref[...] = x11
    rest_ref[...] = s[HALF:, HALF:] - t_mm(u12, u12)


def first_kernel(a00, u_ref, x_ref):
    s = a00[...]
    factor_blocks(s[:HALF, :HALF], s[:HALF, HALF:], s[HALF:, HALF:], u_ref, x_ref)


def second_kernel(x0, a01, a11, u01_ref, u_ref, x_ref, rest_ref):
    u01 = mm(x0[...], a01[...])
    u01_ref[...] = u01
    start_blocks(a11[...] - t_mm(u01, u01), u_ref, x_ref, rest_ref)


def third_kernel(x0, u01, ua, xa, rest, u_ref, x_ref, w_ref):
    finish_blocks(ua[:HALF, :], ua[HALF:, :], xa[...], rest[...], u_ref, x_ref)
    w_ref[...] = -mm(x_ref[...], t_mm(u01[...], x0[...]))


def rows_kernel(loc_rows, pos, x0, x1, w, left, right, *out):
    even_col = pos[1] % 2 == 0
    for a in range(loc_rows):
        l, r = left[a * NB : (a + 1) * NB, :], right[a * NB : (a + 1) * NB, :]
        b0, b1 = jnp.where(even_col, l, r), jnp.where(even_col, r, l)
        out[2 * a][...] = mm_t(b0, x0[...], HIGH)
        out[2 * a + 1][...] = mm_t(b0, w[...], HIGH) + mm_t(b1, x1[...], HIGH)


def last_kernel(loc_rows, loc_cols, pos, own, mine, other, u0, x0, u1, x1, w, *rest):
    prows, out = rest[: 2 * loc_rows], rest[2 * loc_rows]
    stride = 2 * loc_cols
    even = pos[0] % 2 == 0

    for b in range(loc_cols):
        tile_col = pos[1] + b * pos[3]
        e, o = tile_from(mine, 2 * b, stride), tile_from(other, 2 * b, stride)
        d0, d1 = jnp.where(even, e, o), jnp.where(even, o, e)
        q0 = mm(x0[...], d0, HIGH)
        q1 = mm(w[...], d0, HIGH) + mm(x1[...], d1, HIGH)
        for a in range(loc_rows):
            tile_row = pos[0] + a * pos[2]
            start = a * NB * stride + 2 * b

            def put(value, start=start):
                out[pl.ds(start, NB, stride=stride), :] = value[:, :HALF]
                out[pl.ds(start + 1, NB, stride=stride), :] = value[:, HALF:]

            @pl.when(tile_row < tile_col)
            def _():
                put(jnp.zeros((NB, NB), jnp.float32))

            @pl.when((tile_row >= tile_col) & (tile_col >= 2))
            def _():
                put(
                    tile_from(own, start, stride)
                    - (mm(prows[2 * a][...], q0, HIGH) + mm(prows[2 * a + 1][...], q1, HIGH))
                )

            if b == 0:

                @pl.when((tile_row > 0) & (tile_col == 0))
                def _():
                    put(prows[2 * a][...])

                @pl.when((tile_row > 1) & (tile_col == 1))
                def _():
                    put(prows[2 * a + 1][...])

                if a == 0:

                    @pl.when((tile_row == 0) & (tile_col == 0))
                    def _():
                        put(u0[...].T)

                    @pl.when((tile_row == 1) & (tile_col == 1))
                    def _():
                        put(u1[...].T)


VMEM = pl.BlockSpec(memory_space=pltpu.VMEM)
SMEM = pl.BlockSpec(memory_space=pltpu.SMEM)


def shape(*dims):
    return jax.ShapeDtypeStruct(dims, jnp.float32)


def call(kernel, out_shape, flops, *args, smem=0, vmem=16):
    return pl.pallas_call(
        kernel,
        out_shape=out_shape,
        in_specs=[SMEM] * smem + [VMEM] * (len(args) - smem),
        out_specs=jax.tree.map(lambda _: VMEM, out_shape),
        compiler_params=pltpu.CompilerParams(vmem_limit_bytes=vmem * 2**20),
        cost_estimate=pl.CostEstimate(flops=flops, bytes_accessed=2**22, transcendentals=0),
    )(*args)


def on_device(n_row, n_col, trailing_in):
    row = lax.axis_index("row")
    col = lax.axis_index("col")
    loc_rows, _, _, loc_cols, _, _ = trailing_in.shape
    stride = 2 * loc_cols
    own = trailing_in.reshape(loc_rows * NB * stride, HALF)
    pos = jnp.stack([row, col, jnp.int32(n_row), jnp.int32(n_col)]).astype(jnp.int32)
    planes = range(n_col)
    col_bits = [1 << k for k in range(1, (n_col - 1).bit_length())][::-1]
    after = lax.optimization_barrier

    def swap(value, axis, bits):
        size = n_row if axis == "row" else n_col
        return lax.ppermute(value, axis, [(i, i ^ bits) for i in range(size)])

    def exchange(value, axis):
        return lax.all_to_all(value, axis, 0, 0)

    def to_all(value, axis, size):
        return exchange(jnp.broadcast_to(value[None], (size, *value.shape)), axis)

    top, left = call(
        functools.partial(pack_kernel, loc_rows, loc_cols),
        [shape(NB * stride, HALF), shape(loc_rows * NB, NB)],
        10**8,
        own,
    )

    pieces = exchange(left[:NB].reshape(n_row, NB // n_row, NB), "row")
    pieces = to_all(pieces[:2], "col", n_col)
    left, pieces = after((left, pieces))
    a00 = to_all(pieces[0, 0], "row", n_row).reshape(NB, NB)
    pieces, a00 = after((pieces, a00))
    nexts = to_all(pieces[1], "row", n_row)

    bits = [1 << k for k in range(1, (n_row - 1).bit_length())]
    holders = ([0], [1])
    hops = []
    for first, second in zip(bits, bits[::-1]):
        pairs = []
        for mine, bit in zip(holders, (first, second)):
            new = [(h, h ^ bit) for h in mine]
            mine.extend(d for _, d in new)
            pairs += new
        hops.append(pairs)

    def hop(value, pairs):
        flat = [(s * n_col + z, d * n_col + z) for s, d in pairs for z in planes]
        return lax.ppermute(value, ("row", "col"), flat)

    def settle(value, got, pairs):
        is_target = functools.reduce(jnp.logical_or, [row == d for _, d in pairs])
        return jnp.where(is_target, got, value)

    got_left = swap(left, "col", col_bits[0]) if len(col_bits) == 1 else None
    top, a00 = after((top, a00))
    got_top = hop(top, hops[0])
    u0, x0 = call(first_kernel, [shape(NB, NB)] * 2, 10**10, a00)
    got_top, nexts, x0 = after((got_top, nexts, x0))
    a01, a11 = nexts[:, 0].reshape(NB, NB), nexts[:, 1].reshape(NB, NB)
    for k, pairs in enumerate(hops):
        top = settle(top, got_top if k == 0 else hop(top, pairs), pairs)
    u01, u_half, x_half, rest = call(
        second_kernel,
        [shape(NB, NB), shape(NB, HALF), shape(HALF, HALF), shape(HALF, HALF)],
        5 * 10**9,
        x0, a01, a11,
    )
    if got_left is not None:
        got_left, rest = after((got_left, rest))
    for bit in col_bits:
        got = swap(left, "col", bit) if got_left is None else got_left
        left = jnp.where(col & bit != 0, got, left)
    right = swap(left, "col", 1)
    u1, x1, w = call(
        third_kernel, [shape(NB, NB)] * 3, 5 * 10**9, x0, u01, u_half, x_half, rest
    )
    top, right, x1 = after((top, right, x1))
    other = swap(top, "row", 1)
    prows = call(
        functools.partial(rows_kernel, loc_rows),
        [shape(NB, NB)] * (2 * loc_rows),
        2 * 10**9,
        pos, x0, x1, w, left, right,
        smem=1,
    )
    out = call(
        functools.partial(last_kernel, loc_rows, loc_cols),
        shape(*own.shape),
        3 * 10**9,
        pos, own, top, other, u0, x0, u1, x1, w, *prows,
        smem=1,
        vmem=24,
    )
    return out.reshape(trailing_in.shape)


def solution(mesh):
    return jax.shard_map(
        functools.partial(on_device, mesh.shape["row"], mesh.shape["col"]),
        mesh=mesh,
        in_specs=(P(None, "row", None, None, "col", None),),
        out_specs=P(None, "row", None, None, "col", None),
        check_vma=False,
    )
```

```python
import functools

import jax
import jax.numpy as jnp
from jax import lax
from jax.experimental import pallas as pl
from jax.experimental.pallas import tpu as pltpu
from jax.sharding import PartitionSpec as P

NB = 256
HALF = 128
SUB = 8
HIGHEST = lax.Precision.HIGHEST
HIGH = lax.Precision.HIGH


def mm(a, b, precision=HIGHEST):
    return lax.dot_general(
        a, b, (((1,), (0,)), ((), ())), precision=precision, preferred_element_type=jnp.float32
    )


def mm_t(a, b, precision=HIGHEST):
    return lax.dot_general(
        a, b, (((1,), (1,)), ((), ())), precision=precision, preferred_element_type=jnp.float32
    )


def t_mm(a, b, precision=HIGHEST):
    return lax.dot_general(
        a, b, (((0,), (0,)), ((), ())), precision=precision, preferred_element_type=jnp.float32
    )


def spread(x):
    return jnp.broadcast_to(x, (SUB, HALF))


def factor_half(s):
    groups = HALF // SUB
    rows = [s[SUB * g : SUB * (g + 1), :] for g in range(groups)]
    lane = lax.broadcasted_iota(jnp.int32, (SUB, HALF), 1)
    sub = lax.broadcasted_iota(jnp.int32, (SUB, HALF), 0)
    eyes = [jnp.where(lane == sub + SUB * g, 1.0, 0.0).astype(jnp.float32) for g in range(groups)]
    out_u, out_x = [], []
    for g in range(groups):
        base = SUB * g
        own = rows[g]
        own_x = eyes[g]
        a = {}
        for i in range(SUB):
            for j in range(i, SUB):
                a[i, j] = spread(own[i : i + 1, base + j : base + j + 1])
        near = None
        if g + 1 < groups:
            near = [spread(rows[g + 1][:, base + j : base + j + 1]) for j in range(SUB)]
        u = [spread(own[i : i + 1, :]) for i in range(SUB)]
        x = [spread(own_x[i : i + 1, :]) for i in range(SUB)]
        r = [None] * SUB
        l = {}
        for k in range(SUB):
            r[k] = lax.rsqrt(a[k, k])
            for j in range(k + 1, SUB):
                l[k, j] = a[k, j] * r[k]
            for i in range(k + 1, SUB):
                for j in range(i, SUB):
                    a[i, j] = a[i, j] - l[k, i] * l[k, j]
            u[k] = u[k] * r[k]
            x[k] = x[k] * r[k]
            if near is not None:
                near[k] = near[k] * r[k]
            for i in range(k + 1, SUB):
                u[i] = u[i] - l[k, i] * u[k]
                x[i] = x[i] - l[k, i] * x[k]
                if near is not None:
                    near[i] = near[i] - l[k, i] * near[k]
        final_u, final_x = u[0], x[0]
        for i in range(1, SUB):
            final_u = jnp.where(sub == i, u[i], final_u)
            final_x = jnp.where(sub == i, x[i], final_x)
        out_u.append(jnp.where(lane >= sub + base, final_u, 0.0))
        out_x.append(final_x)
        if near is not None:
            nxt, nxt_x = rows[g + 1], eyes[g + 1]
            for k in range(SUB):
                nxt = nxt - near[k] * u[k]
                nxt_x = nxt_x - near[k] * x[k]
        if g + 2 < groups:
            v, vx = list(u), list(x)
            for i in reversed(range(SUB)):
                for j in range(i + 1, SUB):
                    v[i] = v[i] - l[i, j] * v[j]
                    vx[i] = vx[i] - l[i, j] * vx[j]
                v[i] = v[i] * r[i]
                vx[i] = vx[i] * r[i]
            for h in range(g + 2, groups):
                far, far_x = rows[h], eyes[h]
                for j in range(SUB):
                    c = spread(rows[h][:, base + j : base + j + 1])
                    far = far - c * v[j]
                    far_x = far_x - c * vx[j]
                rows[h], eyes[h] = far, far_x
        if near is not None:
            rows[g + 1], eyes[g + 1] = nxt, nxt_x
    return jnp.concatenate(out_u, axis=0), jnp.concatenate(out_x, axis=0)


def finish_blocks(u11, u12, x11, rest, u_ref, x_ref):
    zero = jnp.zeros((HALF, HALF), jnp.float32)
    u22, x22 = factor_half(rest)
    u_ref[:HALF, :HALF] = u11
    u_ref[:HALF, HALF:] = u12
    u_ref[HALF:, :HALF] = zero
    u_ref[HALF:, HALF:] = u22
    x_ref[:HALF, :HALF] = x11
    x_ref[:HALF, HALF:] = zero
    x_ref[HALF:, :HALF] = -mm(x22, t_mm(u12, x11))
    x_ref[HALF:, HALF:] = x22


def factor_blocks(s11, s12, s22, u_ref, x_ref):
    u11, x11 = factor_half(s11)
    u12 = mm(x11, s12)
    finish_blocks(u11, u12, x11, s22 - t_mm(u12, u12), u_ref, x_ref)


def tile_from(ref, start, stride):
    return jnp.concatenate(
        [ref[pl.ds(start, NB, stride=stride), :], ref[pl.ds(start + 1, NB, stride=stride), :]], axis=1
    )


def pack_kernel(loc_rows, loc_cols, own, top, *left):
    stride = 2 * loc_cols
    for a in range(loc_rows):
        left[a][...] = tile_from(own, a * NB * stride, stride)
    top[...] = own[: NB * stride, :]


def start_blocks(s, u_ref, x_ref, rest_ref):
    u11, x11 = factor_half(s[:HALF, :HALF])
    u12 = mm(x11, s[:HALF, HALF:])
    u_ref[:HALF, :] = u11
    u_ref[HALF:, :] = u12
    x_ref[...] = x11
    rest_ref[...] = s[HALF:, HALF:] - t_mm(u12, u12)


def first_kernel(pos, mine, other, u_ref, x_ref):
    s = jnp.where(pos[0] % 2 == 0, mine[...], other[...])
    factor_blocks(s[:HALF, :HALF], s[:HALF, HALF:], s[HALF:, HALF:], u_ref, x_ref)


def second_kernel(pos, x0, mine0, mine1, other0, other1, u01_ref, u_ref, x_ref, rest_ref):
    even = pos[0] % 2 == 0
    u01 = mm(x0[...], jnp.where(even, mine1[...], other1[...]))
    u01_ref[...] = u01
    start_blocks(jnp.where(even, other0[...], mine1[...]) - t_mm(u01, u01), u_ref, x_ref, rest_ref)


def third_kernel(x0, u01, ua, xa, rest, u_ref, x_ref, w_ref):
    finish_blocks(ua[:HALF, :], ua[HALF:, :], xa[...], rest[...], u_ref, x_ref)
    w_ref[...] = -mm(x_ref[...], t_mm(u01[...], x0[...]))


def rows_kernel(loc_rows, pos, x0, x1, w, *rest):
    left, right, out = rest[:loc_rows], rest[loc_rows : 2 * loc_rows], rest[2 * loc_rows :]
    even_col = pos[1] % 2 == 0
    for a in range(loc_rows):
        l, r = left[a][...], right[a][...]
        b0, b1 = jnp.where(even_col, l, r), jnp.where(even_col, r, l)
        out[2 * a][...] = mm_t(b0, x0[...], HIGH)
        out[2 * a + 1][...] = mm_t(b0, w[...], HIGH) + mm_t(b1, x1[...], HIGH)


def last_kernel(
    loc_rows, loc_cols, pos, own, mine, other, u0, x0, u1, x1, w, *rest
):
    prows, out = rest[: 2 * loc_rows], rest[2 * loc_rows]
    stride = 2 * loc_cols
    even = pos[0] % 2 == 0

    for b in range(loc_cols):
        tile_col = pos[1] + b * pos[3]
        e, o = tile_from(mine, 2 * b, stride), tile_from(other, 2 * b, stride)
        d0, d1 = jnp.where(even, e, o), jnp.where(even, o, e)
        q0 = mm(x0[...], d0, HIGH)
        q1 = mm(w[...], d0, HIGH) + mm(x1[...], d1, HIGH)
        for a in range(loc_rows):
            tile_row = pos[0] + a * pos[2]
            start = a * NB * stride + 2 * b

            def put(value, start=start):
                out[pl.ds(start, NB, stride=stride), :] = value[:, :HALF]
                out[pl.ds(start + 1, NB, stride=stride), :] = value[:, HALF:]

            @pl.when(tile_row < tile_col)
            def _():
                put(jnp.zeros((NB, NB), jnp.float32))

            @pl.when((tile_row >= tile_col) & (tile_col >= 2))
            def _():
                put(
                    tile_from(own, start, stride)
                    - (mm(prows[2 * a][...], q0, HIGH) + mm(prows[2 * a + 1][...], q1, HIGH))
                )

            if b == 0:

                @pl.when((tile_row > 0) & (tile_col == 0))
                def _():
                    put(prows[2 * a][...])

                @pl.when((tile_row > 1) & (tile_col == 1))
                def _():
                    put(prows[2 * a + 1][...])

                if a == 0:

                    @pl.when((tile_row == 0) & (tile_col == 0))
                    def _():
                        put(u0[...].T)

                    @pl.when((tile_row == 1) & (tile_col == 1))
                    def _():
                        put(u1[...].T)


VMEM = pl.BlockSpec(memory_space=pltpu.VMEM)
SMEM = pl.BlockSpec(memory_space=pltpu.SMEM)


def shape(*dims):
    return jax.ShapeDtypeStruct(dims, jnp.float32)


def call(kernel, out_shape, flops, *args, smem=0, vmem=16):
    return pl.pallas_call(
        kernel,
        out_shape=out_shape,
        in_specs=[SMEM] * smem + [VMEM] * (len(args) - smem),
        out_specs=jax.tree.map(lambda _: VMEM, out_shape),
        compiler_params=pltpu.CompilerParams(vmem_limit_bytes=vmem * 2**20),
        cost_estimate=pl.CostEstimate(flops=flops, bytes_accessed=2**22, transcendentals=0),
    )(*args)


def on_device(n_row, n_col, trailing_in):
    row = lax.axis_index("row")
    col = lax.axis_index("col")
    loc_rows, _, _, loc_cols, _, _ = trailing_in.shape
    stride = 2 * loc_cols
    chips = n_row // 2
    chip = row // 2
    own = trailing_in.reshape(loc_rows * NB * stride, HALF)
    pos = jnp.stack([row, col, jnp.int32(n_row), jnp.int32(n_col)]).astype(jnp.int32)
    planes = range(n_col)
    col_bits = [1 << k for k in range(1, (n_col - 1).bit_length())][::-1]
    after = lax.optimization_barrier

    def swap(value, axis, bits):
        size = n_row if axis == "row" else n_col
        return lax.ppermute(value, axis, [(i, i ^ bits) for i in range(size)])

    def pick(index, values):
        out = values[0]
        for k, value in enumerate(values[1:], 1):
            out = jnp.where(index == k, value, out)
        return out

    def spread(value, axis, bit, got=None):
        got = swap(value, axis, bit) if got is None else got
        return jnp.where((row if axis == "row" else col) & bit != 0, got, value)

    top, *left = call(
        functools.partial(pack_kernel, loc_rows, loc_cols),
        [shape(NB * stride, HALF)] + [shape(NB, NB)] * loc_rows,
        10**8,
        own,
    )

    size = NB // chips
    pieces = [left[0][k * size : (k + 1) * size] for k in range(chips)]
    piece = pick(chip, [pieces[0]] + [swap(pieces[k], "row", 2 * k) for k in range(1, chips)])
    along = [piece] + [swap(piece, "col", k) for k in range(1, n_col)]
    pair = jnp.concatenate([pick(col, along), pick(col ^ 1, along)], axis=0)
    got = [swap(pair, "row", 2 * k) for k in range(1, chips)]

    left[0], got[0] = after((left[0], got[0]))
    got_left = swap(left[0], "col", col_bits[-1]) if len(col_bits) == 1 else None
    got = [pair] + got
    lead = [
        jnp.concatenate(
            [pick(chip ^ k, got)[j * size : (j + 1) * size] for k in range(chips)], axis=0
        )
        for j in (0, 1)
    ]
    other = swap(jnp.where(row % 2 == 0, lead[0], lead[1]), "row", 1)
    bits = [1 << k for k in range(1, (n_row - 1).bit_length())]
    holders = ([0], [1])
    hops = []
    for first, second in zip(bits, bits[::-1]):
        pairs = []
        for mine, bit in zip(holders, (first, second)):
            new = [(h, h ^ bit) for h in mine]
            mine.extend(d for _, d in new)
            pairs += new
        hops.append(pairs)

    def hop(value, pairs):
        flat = [(s * n_col + z, d * n_col + z) for s, d in pairs for z in planes]
        return lax.ppermute(value, ("row", "col"), flat)

    def settle(value, got, pairs):
        is_target = functools.reduce(jnp.logical_or, [row == d for _, d in pairs])
        return jnp.where(is_target, got, value)

    top, lead[0] = after((top, lead[0]))
    got_top = hop(top, hops[0])

    u0, x0 = call(first_kernel, [shape(NB, NB)] * 2, 10**10, pos, lead[0], other, smem=1)
    got_left, got_top, lead[1], x0 = after((got_left, got_top, lead[1], x0))
    other_next = swap(lead[1], "row", 1)

    for pairs, following in zip(hops, hops[1:]):
        top = settle(top, got_top, pairs)
        got_top = hop(top, following)
    top = settle(top, got_top, hops[-1])
    for bit in col_bits:
        left[0] = spread(left[0], "col", bit, got_left)
    right = [swap(left[0], "col", 1)]
    got_last = []
    for a in range(1, loc_rows):
        left[a], x0 = after((left[a], x0))
        for bit in col_bits[:-1]:
            left[a] = spread(left[a], "col", bit)
        got_last.append(swap(left[a], "col", col_bits[-1]))

    u01, u_half, x_half, rest = call(
        second_kernel,
        [shape(NB, NB), shape(NB, HALF), shape(HALF, HALF), shape(HALF, HALF)],
        5 * 10**9,
        pos, x0, lead[0], lead[1], other, other_next,
        smem=1,
    )
    got_last, rest = after((got_last, rest))
    for a in range(1, loc_rows):
        left[a] = spread(left[a], "col", col_bits[-1], got_last[a - 1])
    right += [swap(left[a], "col", 1) for a in range(1, loc_rows)]
    u1, x1, w = call(
        third_kernel, [shape(NB, NB)] * 3, 5 * 10**9, x0, u01, u_half, x_half, rest
    )
    top, right, x1 = after((top, right, x1))
    other = swap(top, "row", 1)
    prows = call(
        functools.partial(rows_kernel, loc_rows),
        [shape(NB, NB)] * (2 * loc_rows),
        2 * 10**9,
        pos, x0, x1, w, *left, *right,
        smem=1,
    )
    out = call(
        functools.partial(last_kernel, loc_rows, loc_cols),
        shape(*own.shape),
        3 * 10**9,
        pos, own, top, other, u0, x0, u1, x1, w, *prows,
        smem=1,
        vmem=24,
    )
    return out.reshape(trailing_in.shape)


def solution(mesh):
    return jax.shard_map(
        functools.partial(on_device, mesh.shape["row"], mesh.shape["col"]),
        mesh=mesh,
        in_specs=(P(None, "row", None, None, "col", None),),
        out_specs=P(None, "row", None, None, "col", None),
        check_vma=False,
    )
```

```python
import functools

import jax
import jax.numpy as jnp
from jax import lax
from jax.experimental import pallas as pl
from jax.experimental.pallas import tpu as pltpu
from jax.sharding import PartitionSpec as P

NB = 256
HALF = 128
SUB = 8
HIGHEST = lax.Precision.HIGHEST
HIGH = lax.Precision.HIGH


def mm(a, b, precision=HIGHEST):
    return lax.dot_general(
        a, b, (((1,), (0,)), ((), ())), precision=precision, preferred_element_type=jnp.float32
    )


def mm_t(a, b, precision=HIGHEST):
    return lax.dot_general(
        a, b, (((1,), (1,)), ((), ())), precision=precision, preferred_element_type=jnp.float32
    )


def t_mm(a, b, precision=HIGHEST):
    return lax.dot_general(
        a, b, (((0,), (0,)), ((), ())), precision=precision, preferred_element_type=jnp.float32
    )


def spread(x):
    return jnp.broadcast_to(x, (SUB, HALF))


def factor_half(s):
    groups = HALF // SUB
    rows = [s[SUB * g : SUB * (g + 1), :] for g in range(groups)]
    lane = lax.broadcasted_iota(jnp.int32, (SUB, HALF), 1)
    sub = lax.broadcasted_iota(jnp.int32, (SUB, HALF), 0)
    eyes = [jnp.where(lane == sub + SUB * g, 1.0, 0.0).astype(jnp.float32) for g in range(groups)]
    out_u, out_x = [], []
    for g in range(groups):
        base = SUB * g
        own = rows[g]
        own_x = eyes[g]
        a = {}
        for j in range(SUB):
            column = spread(own[:, base + j : base + j + 1])
            for i in range(j + 1):
                a[i, j] = spread(column[i : i + 1, :])
        near = None
        if g + 1 < groups:
            near = [spread(rows[g + 1][:, base + j : base + j + 1]) for j in range(SUB)]
        u = [spread(own[i : i + 1, :]) for i in range(SUB)]
        x = [spread(own_x[i : i + 1, :]) for i in range(SUB)]
        r = [None] * SUB
        l = {}
        for k in range(SUB):
            r[k] = lax.rsqrt(a[k, k])
            for j in range(k + 1, SUB):
                l[k, j] = a[k, j] * r[k]
            for i in range(k + 1, SUB):
                for j in range(i, SUB):
                    a[i, j] = a[i, j] - l[k, i] * l[k, j]
            u[k] = u[k] * r[k]
            x[k] = x[k] * r[k]
            if near is not None:
                near[k] = near[k] * r[k]
            for i in range(k + 1, SUB):
                u[i] = u[i] - l[k, i] * u[k]
                x[i] = x[i] - l[k, i] * x[k]
                if near is not None:
                    near[i] = near[i] - l[k, i] * near[k]
        final_u, final_x = u[0], x[0]
        for i in range(1, SUB):
            final_u = jnp.where(sub == i, u[i], final_u)
            final_x = jnp.where(sub == i, x[i], final_x)
        out_u.append(jnp.where(lane >= sub + base, final_u, 0.0))
        out_x.append(final_x)
        if near is not None:
            nxt, nxt_x = rows[g + 1], eyes[g + 1]
            for k in range(SUB):
                nxt = nxt - near[k] * u[k]
                nxt_x = nxt_x - near[k] * x[k]
        if g + 2 < groups:
            v, vx = list(u), list(x)
            for i in reversed(range(SUB)):
                for j in range(i + 1, SUB):
                    v[i] = v[i] - l[i, j] * v[j]
                    vx[i] = vx[i] - l[i, j] * vx[j]
                v[i] = v[i] * r[i]
                vx[i] = vx[i] * r[i]
            for h in range(g + 2, groups):
                far, far_x = rows[h], eyes[h]
                for j in range(SUB):
                    c = spread(rows[h][:, base + j : base + j + 1])
                    far = far - c * v[j]
                    far_x = far_x - c * vx[j]
                rows[h], eyes[h] = far, far_x
        if near is not None:
            rows[g + 1], eyes[g + 1] = nxt, nxt_x
    return jnp.concatenate(out_u, axis=0), jnp.concatenate(out_x, axis=0)


def finish_blocks(u11, u12, x11, rest, u_ref, x_ref):
    zero = jnp.zeros((HALF, HALF), jnp.float32)
    u22, x22 = factor_half(rest)
    u_ref[:HALF, :HALF] = u11
    u_ref[:HALF, HALF:] = u12
    u_ref[HALF:, :HALF] = zero
    u_ref[HALF:, HALF:] = u22
    x_ref[:HALF, :HALF] = x11
    x_ref[:HALF, HALF:] = zero
    x_ref[HALF:, :HALF] = -mm(x22, t_mm(u12, x11))
    x_ref[HALF:, HALF:] = x22


def factor_blocks(s11, s12, s22, u_ref, x_ref):
    u11, x11 = factor_half(s11)
    u12 = mm(x11, s12)
    finish_blocks(u11, u12, x11, s22 - t_mm(u12, u12), u_ref, x_ref)


def tile_from(ref, start, stride):
    return jnp.concatenate(
        [ref[pl.ds(start, NB, stride=stride), :], ref[pl.ds(start + 1, NB, stride=stride), :]], axis=1
    )


def pack_kernel(loc_rows, loc_cols, own, top, left):
    stride = 2 * loc_cols
    for a in range(loc_rows):
        left[a * NB : (a + 1) * NB, :] = tile_from(own, a * NB * stride, stride)
    top[...] = own[: NB * stride, :]


def start_blocks(s, u_ref, x_ref, rest_ref):
    u11, x11 = factor_half(s[:HALF, :HALF])
    u12 = mm(x11, s[:HALF, HALF:])
    u_ref[:HALF, :] = u11
    u_ref[HALF:, :] = u12
    x_ref[...] = x11
    rest_ref[...] = s[HALF:, HALF:] - t_mm(u12, u12)


def first_kernel(pos, mine, other, u_ref, x_ref):
    s = jnp.where(pos[0] % 2 == 0, mine[...], other[...])
    factor_blocks(s[:HALF, :HALF], s[:HALF, HALF:], s[HALF:, HALF:], u_ref, x_ref)


def second_kernel(pos, x0, mine0, mine1, other0, other1, u01_ref, u_ref, x_ref, rest_ref):
    even = pos[0] % 2 == 0
    u01 = mm(x0[...], jnp.where(even, mine1[...], other1[...]))
    u01_ref[...] = u01
    start_blocks(jnp.where(even, other0[...], mine1[...]) - t_mm(u01, u01), u_ref, x_ref, rest_ref)


def third_kernel(x0, u01, ua, xa, rest, u_ref, x_ref, w_ref):
    finish_blocks(ua[:HALF, :], ua[HALF:, :], xa[...], rest[...], u_ref, x_ref)
    w_ref[...] = -mm(x_ref[...], t_mm(u01[...], x0[...]))


def rows_kernel(loc_rows, panels, x0, x1, w, *out):
    for a in range(loc_rows):
        rows = slice(a * NB, (a + 1) * NB)
        out[2 * a][...] = mm_t(panels[0, rows, :], x0[...], HIGH)
        out[2 * a + 1][...] = mm_t(panels[0, rows, :], w[...], HIGH) + mm_t(
            panels[1, rows, :], x1[...], HIGH
        )


def last_kernel(
    loc_rows, loc_cols, pos, own, mine, other, u0, x0, u1, x1, w, *rest
):
    prows, out = rest[: 2 * loc_rows], rest[2 * loc_rows]
    stride = 2 * loc_cols
    even = pos[0] % 2 == 0

    for b in range(loc_cols):
        tile_col = pos[1] + b * pos[3]
        e, o = tile_from(mine, 2 * b, stride), tile_from(other, 2 * b, stride)
        d0, d1 = jnp.where(even, e, o), jnp.where(even, o, e)
        q0 = mm(x0[...], d0, HIGH)
        q1 = mm(w[...], d0, HIGH) + mm(x1[...], d1, HIGH)
        for a in range(loc_rows):
            tile_row = pos[0] + a * pos[2]
            start = a * NB * stride + 2 * b

            def put(value, start=start):
                out[pl.ds(start, NB, stride=stride), :] = value[:, :HALF]
                out[pl.ds(start + 1, NB, stride=stride), :] = value[:, HALF:]

            @pl.when(tile_row < tile_col)
            def _():
                put(jnp.zeros((NB, NB), jnp.float32))

            @pl.when((tile_row >= tile_col) & (tile_col >= 2))
            def _():
                put(
                    tile_from(own, start, stride)
                    - (mm(prows[2 * a][...], q0, HIGH) + mm(prows[2 * a + 1][...], q1, HIGH))
                )

            if b == 0:

                @pl.when((tile_row > 0) & (tile_col == 0))
                def _():
                    put(prows[2 * a][...])

                @pl.when((tile_row > 1) & (tile_col == 1))
                def _():
                    put(prows[2 * a + 1][...])

                if a == 0:

                    @pl.when((tile_row == 0) & (tile_col == 0))
                    def _():
                        put(u0[...].T)

                    @pl.when((tile_row == 1) & (tile_col == 1))
                    def _():
                        put(u1[...].T)


VMEM = pl.BlockSpec(memory_space=pltpu.VMEM)
SMEM = pl.BlockSpec(memory_space=pltpu.SMEM)


def shape(*dims):
    return jax.ShapeDtypeStruct(dims, jnp.float32)


def call(kernel, out_shape, flops, *args, smem=0, vmem=16, specs=None, grid=()):
    return pl.pallas_call(
        kernel,
        grid=grid,
        out_shape=out_shape,
        in_specs=specs or [SMEM] * smem + [VMEM] * (len(args) - smem),
        out_specs=jax.tree.map(lambda _: VMEM, out_shape),
        compiler_params=pltpu.CompilerParams(vmem_limit_bytes=vmem * 2**20),
        cost_estimate=pl.CostEstimate(flops=flops, bytes_accessed=2**22, transcendentals=0),
    )(*args)


def on_device(n_row, n_col, trailing_in):
    row = lax.axis_index("row")
    col = lax.axis_index("col")
    loc_rows, _, _, loc_cols, _, _ = trailing_in.shape
    stride = 2 * loc_cols
    chips = n_row // 2
    chip = row // 2
    own = trailing_in.reshape(loc_rows * NB * stride, HALF)
    pos = jnp.stack([row, col, jnp.int32(n_row), jnp.int32(n_col)]).astype(jnp.int32)
    planes = range(n_col)
    after = lax.optimization_barrier

    def swap(value, axis, bits):
        size = n_row if axis == "row" else n_col
        return lax.ppermute(value, axis, [(i, i ^ bits) for i in range(size)])

    def pick(index, values):
        out = values[0]
        for k, value in enumerate(values[1:], 1):
            out = jnp.where(index == k, value, out)
        return out

    top, left = call(
        functools.partial(pack_kernel, loc_rows, loc_cols),
        [shape(NB * stride, HALF), shape(loc_rows * NB, NB)],
        10**8,
        own,
    )

    size = NB // chips
    pieces = [left[k * size : (k + 1) * size] for k in range(chips)]
    piece = pick(chip, [pieces[0]] + [swap(pieces[k], "row", 2 * k) for k in range(1, chips)])
    along = [piece] + [swap(piece, "col", k) for k in range(1, n_col)]
    pair = jnp.concatenate([pick(col, along), pick(col ^ 1, along)], axis=0)
    got = [swap(pair, "row", 2 * k) for k in range(1, chips)]

    left, pair = after((left, pair))
    panels = lax.all_gather(left, "col", axis=0)
    got = [pair] + got
    lead = [
        jnp.concatenate(
            [pick(chip ^ k, got)[j * size : (j + 1) * size] for k in range(chips)], axis=0
        )
        for j in (0, 1)
    ]
    other = swap(jnp.where(row % 2 == 0, lead[0], lead[1]), "row", 1)
    bits = [1 << k for k in range(1, (n_row - 1).bit_length())]
    holders = ([0], [1])
    hops = []
    for first, second in zip(bits, bits[::-1]):
        pairs = []
        for mine, bit in zip(holders, (first, second)):
            new = [(h, h ^ bit) for h in mine]
            mine.extend(d for _, d in new)
            pairs += new
        hops.append(pairs)

    def hop(value, pairs):
        flat = [(s * n_col + z, d * n_col + z) for s, d in pairs for z in planes]
        return lax.ppermute(value, ("row", "col"), flat)

    def settle(value, got, pairs):
        is_target = functools.reduce(jnp.logical_or, [row == d for _, d in pairs])
        return jnp.where(is_target, got, value)

    top, lead[0] = after((top, lead[0]))
    got_top = hop(top, hops[0])

    u0, x0 = call(first_kernel, [shape(NB, NB)] * 2, 10**10, pos, lead[0], other, smem=1)
    got_top, lead[1], x0 = after((got_top, lead[1], x0))
    other_next = swap(lead[1], "row", 1)

    for pairs, following in zip(hops, hops[1:]):
        top = settle(top, got_top, pairs)
        got_top = hop(top, following)
    top = settle(top, got_top, hops[-1])
    u01, u_half, x_half, rest = call(
        second_kernel,
        [shape(NB, NB), shape(NB, HALF), shape(HALF, HALF), shape(HALF, HALF)],
        5 * 10**9,
        pos, x0, lead[0], lead[1], other, other_next,
        smem=1,
    )
    u1, x1, w = call(
        third_kernel, [shape(NB, NB)] * 3, 5 * 10**9, x0, u01, u_half, x_half, rest
    )
    top, x1 = after((top, x1))
    other = swap(top, "row", 1)
    prows = call(
        functools.partial(rows_kernel, loc_rows),
        [shape(NB, NB)] * (2 * loc_rows),
        2 * 10**9,
        panels, x0, x1, w,
        specs=[pl.BlockSpec((2, loc_rows * NB, NB), lambda i: (0, 0, 0))] + [VMEM] * 3,
        grid=(1,),
    )
    out = call(
        functools.partial(last_kernel, loc_rows, loc_cols),
        shape(*own.shape),
        3 * 10**9,
        pos, own, top, other, u0, x0, u1, x1, w, *prows,
        smem=1,
        vmem=24,
    )
    return out.reshape(trailing_in.shape)


def solution(mesh):
    return jax.shard_map(
        functools.partial(on_device, mesh.shape["row"], mesh.shape["col"]),
        mesh=mesh,
        in_specs=(P(None, "row", None, None, "col", None),),
        out_specs=P(None, "row", None, None, "col", None),
        check_vma=False,
    )
```

```python
import functools

import jax
import jax.numpy as jnp
from jax import lax
from jax.experimental import pallas as pl
from jax.experimental.pallas import tpu as pltpu
from jax.sharding import PartitionSpec as P

NB = 256
HALF = 128
SUB = 8
HIGHEST = lax.Precision.HIGHEST
HIGH = lax.Precision.HIGH


def mm(a, b, precision=HIGHEST):
    return lax.dot_general(
        a, b, (((1,), (0,)), ((), ())), precision=precision, preferred_element_type=jnp.float32
    )


def mm_t(a, b, precision=HIGHEST):
    return lax.dot_general(
        a, b, (((1,), (1,)), ((), ())), precision=precision, preferred_element_type=jnp.float32
    )


def t_mm(a, b, precision=HIGHEST):
    return lax.dot_general(
        a, b, (((0,), (0,)), ((), ())), precision=precision, preferred_element_type=jnp.float32
    )


def spread(x):
    return jnp.broadcast_to(x, (SUB, HALF))


def factor_half(s):
    groups = HALF // SUB
    lane = lax.broadcasted_iota(jnp.int32, (SUB, HALF), 1)
    sub = lax.broadcasted_iota(jnp.int32, (SUB, HALF), 0)
    rows = [s[SUB * g : SUB * (g + 1), :] for g in range(groups)]
    own_diagonal = [jnp.where(lane == sub + SUB * g, rows[g], 0.0) for g in range(groups)]
    diagonal = spread(jnp.sum(sum(own_diagonal), axis=0, keepdims=True))
    scale = lax.rsqrt(diagonal)
    unscale = diagonal * scale
    eyes = []
    for g in range(groups):
        down = spread(lax.rsqrt(jnp.sum(own_diagonal[g], axis=1, keepdims=True)))
        rows[g] = (rows[g] * scale) * down
        eyes.append(jnp.where(lane == sub + SUB * g, 1.0, 0.0).astype(jnp.float32))
    out_u, out_x = [], []
    for g in range(groups):
        base = SUB * g
        own = rows[g]
        own_x = eyes[g]
        a = {}
        for j in range(SUB):
            column = spread(own[:, base + j : base + j + 1])
            for i in range(j + 1):
                a[i, j] = spread(column[i : i + 1, :])
        near = None
        if g + 1 < groups:
            near = [spread(rows[g + 1][:, base + j : base + j + 1]) for j in range(SUB)]
        u = [spread(own[i : i + 1, :]) for i in range(SUB)]
        x = [spread(own_x[i : i + 1, :]) for i in range(SUB)]
        r = [None] * SUB
        l = {}
        for k in range(0, SUB, 2):
            p, q, t = a[k, k], a[k, k + 1], a[k + 1, k + 1]
            r[k] = lax.rsqrt(p)
            root = lax.rsqrt(p * t - q * q)
            both = r[k] * root
            r[k + 1] = (p * r[k]) * root
            l[k, k + 1] = q * r[k]
            for j in range(k + 2, SUB):
                l[k, j] = a[k, j] * r[k]
                l[k + 1, j] = (p * a[k + 1, j] - q * a[k, j]) * both
            for i in range(k + 2, SUB):
                for j in range(i, SUB):
                    a[i, j] = (a[i, j] - l[k, i] * l[k, j]) - l[k + 1, i] * l[k + 1, j]
            for m in (k, k + 1):
                u[m] = u[m] * r[m]
                x[m] = x[m] * r[m]
                if near is not None:
                    near[m] = near[m] * r[m]
                for i in range(m + 1, SUB):
                    u[i] = u[i] - l[m, i] * u[m]
                    x[i] = x[i] - l[m, i] * x[m]
                    if near is not None:
                        near[i] = near[i] - l[m, i] * near[m]
        final_u, final_x = u[0], x[0]
        for i in range(1, SUB):
            final_u = jnp.where(sub == i, u[i], final_u)
            final_x = jnp.where(sub == i, x[i], final_x)
        out_u.append(jnp.where(lane >= sub + base, final_u * unscale, 0.0))
        out_x.append(final_x * scale)
        if near is not None:
            nxt, nxt_x = rows[g + 1], eyes[g + 1]
            for k in range(SUB):
                nxt = nxt - near[k] * u[k]
                nxt_x = nxt_x - near[k] * x[k]
        if g + 2 < groups:
            v, vx = list(u), list(x)
            for i in reversed(range(SUB)):
                for j in range(i + 1, SUB):
                    v[i] = v[i] - l[i, j] * v[j]
                    vx[i] = vx[i] - l[i, j] * vx[j]
                v[i] = v[i] * r[i]
                vx[i] = vx[i] * r[i]
            for h in range(g + 2, groups):
                far, far_x = rows[h], eyes[h]
                for j in range(SUB):
                    c = spread(rows[h][:, base + j : base + j + 1])
                    far = far - c * v[j]
                    far_x = far_x - c * vx[j]
                rows[h], eyes[h] = far, far_x
        if near is not None:
            rows[g + 1], eyes[g + 1] = nxt, nxt_x
    return jnp.concatenate(out_u, axis=0), jnp.concatenate(out_x, axis=0)


def finish_blocks(u11, u12, x11, rest, u_ref, x_ref):
    zero = jnp.zeros((HALF, HALF), jnp.float32)
    u22, x22 = factor_half(rest)
    u_ref[:HALF, :HALF] = u11
    u_ref[:HALF, HALF:] = u12
    u_ref[HALF:, :HALF] = zero
    u_ref[HALF:, HALF:] = u22
    x_ref[:HALF, :HALF] = x11
    x_ref[:HALF, HALF:] = zero
    x_ref[HALF:, :HALF] = -mm(x22, t_mm(u12, x11))
    x_ref[HALF:, HALF:] = x22


def factor_blocks(s11, s12, s22, u_ref, x_ref):
    u11, x11 = factor_half(s11)
    u12 = mm(x11, s12)
    finish_blocks(u11, u12, x11, s22 - t_mm(u12, u12), u_ref, x_ref)


def tile_from(ref, start, stride):
    return jnp.concatenate(
        [ref[pl.ds(start, NB, stride=stride), :], ref[pl.ds(start + 1, NB, stride=stride), :]], axis=1
    )


def pack_kernel(loc_rows, loc_cols, own, top_a, top_b, *left):
    stride = 2 * loc_cols
    for a in range(loc_rows):
        left[a][...] = tile_from(own, a * NB * stride, stride)
    half = HALF * stride
    top_a[...] = own[:half, :]
    top_b[...] = own[half : 2 * half, :]


def start_blocks(s, u_ref, x_ref, rest_ref):
    u11, x11 = factor_half(s[:HALF, :HALF])
    u12 = mm(x11, s[:HALF, HALF:])
    u_ref[:HALF, :] = u11
    u_ref[HALF:, :] = u12
    x_ref[...] = x11
    rest_ref[...] = s[HALF:, HALF:] - t_mm(u12, u12)


def first_kernel(pos, mine, other, u_ref, x_ref):
    s = jnp.where(pos[0] % 2 == 0, mine[...], other[...])
    factor_blocks(s[:HALF, :HALF], s[:HALF, HALF:], s[HALF:, HALF:], u_ref, x_ref)


def second_kernel(pos, x0, mine0, mine1, other0, other1, u01_ref, u_ref, x_ref, rest_ref):
    even = pos[0] % 2 == 0
    u01 = mm(x0[...], jnp.where(even, mine1[...], other1[...]))
    u01_ref[...] = u01
    start_blocks(jnp.where(even, other0[...], mine1[...]) - t_mm(u01, u01), u_ref, x_ref, rest_ref)


def third_kernel(x0, u01, ua, xa, rest, u_ref, x_ref, w_ref):
    finish_blocks(ua[:HALF, :], ua[HALF:, :], xa[...], rest[...], u_ref, x_ref)
    w_ref[...] = -mm(x_ref[...], t_mm(u01[...], x0[...]))


def rows_kernel(loc_rows, pos, x0, x1, w, *rest):
    left, right, out = rest[:loc_rows], rest[loc_rows : 2 * loc_rows], rest[2 * loc_rows :]
    even_col = pos[1] % 2 == 0
    for a in range(loc_rows):
        l, r = left[a][...], right[a][...]
        b0, b1 = jnp.where(even_col, l, r), jnp.where(even_col, r, l)
        out[2 * a][...] = mm_t(b0, x0[...], HIGH)
        out[2 * a + 1][...] = mm_t(b0, w[...], HIGH) + mm_t(b1, x1[...], HIGH)


def last_kernel(
    loc_rows, loc_cols, pos, own, mine_a, mine_b, other_a, other_b, u0, x0, u1, x1, w, *rest
):
    prows, out = rest[: 2 * loc_rows], rest[2 * loc_rows]
    stride = 2 * loc_cols
    even = pos[0] % 2 == 0

    def top_tile(a, b, start):
        halves = [
            jnp.concatenate(
                [ref[pl.ds(start + k, HALF, stride=stride), :] for k in (0, 1)], axis=1
            )
            for ref in (a, b)
        ]
        return jnp.concatenate(halves, axis=0)

    for b in range(loc_cols):
        tile_col = pos[1] + b * pos[3]
        e, o = top_tile(mine_a, mine_b, 2 * b), top_tile(other_a, other_b, 2 * b)
        d0, d1 = jnp.where(even, e, o), jnp.where(even, o, e)
        q0 = mm(x0[...], d0, HIGH)
        q1 = mm(w[...], d0, HIGH) + mm(x1[...], d1, HIGH)
        for a in range(loc_rows):
            tile_row = pos[0] + a * pos[2]
            start = a * NB * stride + 2 * b

            def put(value, start=start):
                out[pl.ds(start, NB, stride=stride), :] = value[:, :HALF]
                out[pl.ds(start + 1, NB, stride=stride), :] = value[:, HALF:]

            @pl.when(tile_row < tile_col)
            def _():
                put(jnp.zeros((NB, NB), jnp.float32))

            @pl.when((tile_row >= tile_col) & (tile_col >= 2))
            def _():
                put(
                    tile_from(own, start, stride)
                    - (mm(prows[2 * a][...], q0, HIGH) + mm(prows[2 * a + 1][...], q1, HIGH))
                )

            if b == 0:

                @pl.when((tile_row > 0) & (tile_col == 0))
                def _():
                    put(prows[2 * a][...])

                @pl.when((tile_row > 1) & (tile_col == 1))
                def _():
                    put(prows[2 * a + 1][...])

                if a == 0:

                    @pl.when((tile_row == 0) & (tile_col == 0))
                    def _():
                        put(u0[...].T)

                    @pl.when((tile_row == 1) & (tile_col == 1))
                    def _():
                        put(u1[...].T)


VMEM = pl.BlockSpec(memory_space=pltpu.VMEM)
SMEM = pl.BlockSpec(memory_space=pltpu.SMEM)


def shape(*dims):
    return jax.ShapeDtypeStruct(dims, jnp.float32)


def call(kernel, out_shape, flops, *args, smem=0, vmem=16):
    return pl.pallas_call(
        kernel,
        out_shape=out_shape,
        in_specs=[SMEM] * smem + [VMEM] * (len(args) - smem),
        out_specs=jax.tree.map(lambda _: VMEM, out_shape),
        compiler_params=pltpu.CompilerParams(vmem_limit_bytes=vmem * 2**20),
        cost_estimate=pl.CostEstimate(flops=flops, bytes_accessed=2**22, transcendentals=0),
    )(*args)


def on_device(n_row, n_col, trailing_in):
    row = lax.axis_index("row")
    col = lax.axis_index("col")
    loc_rows, _, _, loc_cols, _, _ = trailing_in.shape
    stride = 2 * loc_cols
    chips = n_row // 2
    chip = row // 2
    own = trailing_in.reshape(loc_rows * NB * stride, HALF)
    pos = jnp.stack([row, col, jnp.int32(n_row), jnp.int32(n_col)]).astype(jnp.int32)
    row_bits = [1 << k for k in range(1, (n_row - 1).bit_length())]
    col_bits = [1 << k for k in range(1, (n_col - 1).bit_length())][::-1]
    after = lax.optimization_barrier

    def swap(value, axis, bits):
        size = n_row if axis == "row" else n_col
        return lax.ppermute(value, axis, [(i, i ^ bits) for i in range(size)])

    def pick(index, values):
        out = values[0]
        for k, value in enumerate(values[1:], 1):
            out = jnp.where(index == k, value, out)
        return out

    def spread(value, axis, bit, got=None):
        got = swap(value, axis, bit) if got is None else got
        return jnp.where((row if axis == "row" else col) & bit != 0, got, value)

    half = HALF * stride
    top_a, top_b, *left = call(
        functools.partial(pack_kernel, loc_rows, loc_cols),
        [shape(half, HALF), shape(half, HALF)] + [shape(NB, NB)] * loc_rows,
        10**8,
        own,
    )

    size = NB // chips
    pieces = [left[0][k * size : (k + 1) * size] for k in range(chips)]
    piece = pick(chip, [pieces[0]] + [swap(pieces[k], "row", 2 * k) for k in range(1, chips)])
    along = [piece] + [swap(piece, "col", k) for k in range(1, n_col)]
    pair = jnp.concatenate([pick(col, along), pick(col ^ 1, along)], axis=0)
    got = [swap(pair, "row", 2 * k) for k in range(1, chips)]

    left[0], got[0] = after((left[0], got[0]))
    got_left = swap(left[0], "col", col_bits[-1]) if len(col_bits) == 1 else None
    got = [pair] + got
    lead = [
        jnp.concatenate(
            [pick(chip ^ k, got)[j * size : (j + 1) * size] for k in range(chips)], axis=0
        )
        for j in (0, 1)
    ]
    other = swap(jnp.where(row % 2 == 0, lead[0], lead[1]), "row", 1)
    top_a, top_b, lead[0] = after((top_a, top_b, lead[0]))
    got_a = swap(top_a, "row", row_bits[0])
    got_b = swap(top_b, "row", row_bits[-1])

    u0, x0 = call(first_kernel, [shape(NB, NB)] * 2, 10**10, pos, lead[0], other, smem=1)
    got_left, got_a, got_b, lead[1], x0 = after((got_left, got_a, got_b, lead[1], x0))
    other_next = swap(lead[1], "row", 1)

    for first, second in zip(row_bits, row_bits[::-1]):
        top_a, top_b = spread(top_a, "row", first, got_a), spread(top_b, "row", second, got_b)
        got_a = got_b = None
    for bit in col_bits:
        left[0] = spread(left[0], "col", bit, got_left)
    right = [swap(left[0], "col", 1)]
    for a in range(1, loc_rows):
        left[a], x0 = after((left[a], x0))
        for bit in col_bits:
            left[a] = spread(left[a], "col", bit)

    u01, u_half, x_half, rest = call(
        second_kernel,
        [shape(NB, NB), shape(NB, HALF), shape(HALF, HALF), shape(HALF, HALF)],
        5 * 10**9,
        pos, x0, lead[0], lead[1], other, other_next,
        smem=1,
    )
    left, rest = after((left, rest))
    right += [swap(left[a], "col", 1) for a in range(1, loc_rows)]
    u1, x1, w = call(
        third_kernel, [shape(NB, NB)] * 3, 5 * 10**9, x0, u01, u_half, x_half, rest
    )
    top_a, top_b, right, x1 = after((top_a, top_b, right, x1))
    other_a, other_b = swap(top_a, "row", 1), swap(top_b, "row", 1)
    prows = call(
        functools.partial(rows_kernel, loc_rows),
        [shape(NB, NB)] * (2 * loc_rows),
        2 * 10**9,
        pos, x0, x1, w, *left, *right,
        smem=1,
    )
    out = call(
        functools.partial(last_kernel, loc_rows, loc_cols),
        shape(*own.shape),
        3 * 10**9,
        pos, own, top_a, top_b, other_a, other_b, u0, x0, u1, x1, w, *prows,
        smem=1,
        vmem=24,
    )
    return out.reshape(trailing_in.shape)


def solution(mesh):
    return jax.shard_map(
        functools.partial(on_device, mesh.shape["row"], mesh.shape["col"]),
        mesh=mesh,
        in_specs=(P(None, "row", None, None, "col", None),),
        out_specs=P(None, "row", None, None, "col", None),
        check_vma=False,
    )
```

```python
import functools

import jax
import jax.numpy as jnp
from jax import lax
from jax.experimental import pallas as pl
from jax.experimental.pallas import tpu as pltpu
from jax.sharding import PartitionSpec as P

NB = 256
HALF = 128
SUB = 8
HIGHEST = lax.Precision.HIGHEST
HIGH = lax.Precision.HIGH


def mm(a, b, precision=HIGHEST):
    return lax.dot_general(
        a, b, (((1,), (0,)), ((), ())), precision=precision, preferred_element_type=jnp.float32
    )


def mm_t(a, b, precision=HIGHEST):
    return lax.dot_general(
        a, b, (((1,), (1,)), ((), ())), precision=precision, preferred_element_type=jnp.float32
    )


def t_mm(a, b, precision=HIGHEST):
    return lax.dot_general(
        a, b, (((0,), (0,)), ((), ())), precision=precision, preferred_element_type=jnp.float32
    )


def spread(x):
    return jnp.broadcast_to(x, (SUB, HALF))


def factor_half(s):
    groups = HALF // SUB
    lane = lax.broadcasted_iota(jnp.int32, (SUB, HALF), 1)
    sub = lax.broadcasted_iota(jnp.int32, (SUB, HALF), 0)
    rows = [s[SUB * g : SUB * (g + 1), :] for g in range(groups)]
    own_diagonal = [jnp.where(lane == sub + SUB * g, rows[g], 0.0) for g in range(groups)]
    diagonal = spread(jnp.sum(sum(own_diagonal), axis=0, keepdims=True))
    scale = lax.rsqrt(diagonal)
    unscale = diagonal * scale
    eyes = []
    for g in range(groups):
        down = spread(lax.rsqrt(jnp.sum(own_diagonal[g], axis=1, keepdims=True)))
        rows[g] = (rows[g] * scale) * down
        eyes.append(jnp.where(lane == sub + SUB * g, 1.0, 0.0).astype(jnp.float32))
    out_u, out_x = [], []
    for g in range(groups):
        base = SUB * g
        own = rows[g]
        own_x = eyes[g]
        a = {}
        for j in range(SUB):
            column = spread(own[:, base + j : base + j + 1])
            for i in range(j + 1):
                a[i, j] = spread(column[i : i + 1, :])
        near = None
        if g + 1 < groups:
            near = [spread(rows[g + 1][:, base + j : base + j + 1]) for j in range(SUB)]
        u = [spread(own[i : i + 1, :]) for i in range(SUB)]
        x = [spread(own_x[i : i + 1, :]) for i in range(SUB)]
        r = [None] * SUB
        l = {}
        for k in range(0, SUB, 2):
            p, q, t = a[k, k], a[k, k + 1], a[k + 1, k + 1]
            r[k] = lax.rsqrt(p)
            root = lax.rsqrt(p * t - q * q)
            both = r[k] * root
            r[k + 1] = (p * r[k]) * root
            l[k, k + 1] = q * r[k]
            for j in range(k + 2, SUB):
                l[k, j] = a[k, j] * r[k]
                l[k + 1, j] = (p * a[k + 1, j] - q * a[k, j]) * both
            for i in range(k + 2, SUB):
                for j in range(i, SUB):
                    a[i, j] = (a[i, j] - l[k, i] * l[k, j]) - l[k + 1, i] * l[k + 1, j]
            for m in (k, k + 1):
                u[m] = u[m] * r[m]
                x[m] = x[m] * r[m]
                if near is not None:
                    near[m] = near[m] * r[m]
                for i in range(m + 1, SUB):
                    u[i] = u[i] - l[m, i] * u[m]
                    x[i] = x[i] - l[m, i] * x[m]
                    if near is not None:
                        near[i] = near[i] - l[m, i] * near[m]
        final_u, final_x = u[0], x[0]
        for i in range(1, SUB):
            final_u = jnp.where(sub == i, u[i], final_u)
            final_x = jnp.where(sub == i, x[i], final_x)
        out_u.append(jnp.where(lane >= sub + base, final_u * unscale, 0.0))
        out_x.append(final_x * scale)
        if near is not None:
            nxt, nxt_x = rows[g + 1], eyes[g + 1]
            for k in range(SUB):
                nxt = nxt - near[k] * u[k]
                nxt_x = nxt_x - near[k] * x[k]
        if g + 2 < groups:
            v, vx = list(u), list(x)
            for i in reversed(range(SUB)):
                for j in range(i + 1, SUB):
                    v[i] = v[i] - l[i, j] * v[j]
                    vx[i] = vx[i] - l[i, j] * vx[j]
                v[i] = v[i] * r[i]
                vx[i] = vx[i] * r[i]
            for h in range(g + 2, groups):
                far, far_x = rows[h], eyes[h]
                for j in range(SUB):
                    c = spread(rows[h][:, base + j : base + j + 1])
                    far = far - c * v[j]
                    far_x = far_x - c * vx[j]
                rows[h], eyes[h] = far, far_x
        if near is not None:
            rows[g + 1], eyes[g + 1] = nxt, nxt_x
    return jnp.concatenate(out_u, axis=0), jnp.concatenate(out_x, axis=0)


def finish_blocks(u11, u12, x11, rest, u_ref, x_ref):
    zero = jnp.zeros((HALF, HALF), jnp.float32)
    u22, x22 = factor_half(rest)
    u_ref[:HALF, :HALF] = u11
    u_ref[:HALF, HALF:] = u12
    u_ref[HALF:, :HALF] = zero
    u_ref[HALF:, HALF:] = u22
    x_ref[:HALF, :HALF] = x11
    x_ref[:HALF, HALF:] = zero
    x_ref[HALF:, :HALF] = -mm(x22, t_mm(u12, x11))
    x_ref[HALF:, HALF:] = x22


def factor_blocks(s11, s12, s22, u_ref, x_ref):
    u11, x11 = factor_half(s11)
    u12 = mm(x11, s12)
    finish_blocks(u11, u12, x11, s22 - t_mm(u12, u12), u_ref, x_ref)


def tile_from(ref, start, stride):
    return jnp.concatenate(
        [ref[pl.ds(start, NB, stride=stride), :], ref[pl.ds(start + 1, NB, stride=stride), :]], axis=1
    )


def pack_kernel(loc_rows, loc_cols, own, top_a, top_b, *left):
    stride = 2 * loc_cols
    for a in range(loc_rows):
        left[a][...] = tile_from(own, a * NB * stride, stride)
    half = HALF * stride
    top_a[...] = own[:half, :]
    top_b[...] = own[half : 2 * half, :]


def first_kernel(pos, mine, other, u_ref, x_ref):
    s = jnp.where(pos[0] % 2 == 0, mine[...], other[...])
    factor_blocks(s[:HALF, :HALF], s[:HALF, HALF:], s[HALF:, HALF:], u_ref, x_ref)


def second_kernel(pos, x0, mine0, mine1, other0, other1, u_ref, x_ref, w_ref):
    even = pos[0] % 2 == 0
    u01 = mm(x0[...], jnp.where(even, mine1[...], other1[...]))
    s = jnp.where(even, other0[...], mine1[...]) - t_mm(u01, u01)
    factor_blocks(s[:HALF, :HALF], s[:HALF, HALF:], s[HALF:, HALF:], u_ref, x_ref)
    w_ref[...] = -mm(x_ref[...], t_mm(u01, x0[...]))


def last_kernel(
    loc_rows, loc_cols, pos, own, mine_a, mine_b, other_a, other_b, u0, x0, u1, x1, w, *rest
):
    left, right = rest[:loc_rows], rest[loc_rows : 2 * loc_rows]
    out, prows = rest[2 * loc_rows :]
    stride = 2 * loc_cols
    even = pos[0] % 2 == 0
    even_col = pos[1] % 2 == 0
    for a in range(loc_rows):
        l, r = left[a][...], right[a][...]
        b0, b1 = jnp.where(even_col, l, r), jnp.where(even_col, r, l)
        prows[2 * a] = mm_t(b0, x0[...], HIGH)
        prows[2 * a + 1] = mm_t(b0, w[...], HIGH) + mm_t(b1, x1[...], HIGH)

    def top_tile(a, b, start):
        halves = [
            jnp.concatenate(
                [ref[pl.ds(start + k, HALF, stride=stride), :] for k in (0, 1)], axis=1
            )
            for ref in (a, b)
        ]
        return jnp.concatenate(halves, axis=0)

    for b in range(loc_cols):
        tile_col = pos[1] + b * pos[3]
        e, o = top_tile(mine_a, mine_b, 2 * b), top_tile(other_a, other_b, 2 * b)
        d0, d1 = jnp.where(even, e, o), jnp.where(even, o, e)
        q0 = mm(x0[...], d0, HIGH)
        q1 = mm(w[...], d0, HIGH) + mm(x1[...], d1, HIGH)
        for a in range(loc_rows):
            tile_row = pos[0] + a * pos[2]
            start = a * NB * stride + 2 * b

            def put(value, start=start):
                out[pl.ds(start, NB, stride=stride), :] = value[:, :HALF]
                out[pl.ds(start + 1, NB, stride=stride), :] = value[:, HALF:]

            @pl.when(tile_row < tile_col)
            def _():
                put(jnp.zeros((NB, NB), jnp.float32))

            @pl.when((tile_row >= tile_col) & (tile_col >= 2))
            def _():
                put(
                    tile_from(own, start, stride)
                    - (mm(prows[2 * a], q0, HIGH) + mm(prows[2 * a + 1], q1, HIGH))
                )

            if b == 0:

                @pl.when((tile_row > 0) & (tile_col == 0))
                def _():
                    put(prows[2 * a])

                @pl.when((tile_row > 1) & (tile_col == 1))
                def _():
                    put(prows[2 * a + 1])

                if a == 0:

                    @pl.when((tile_row == 0) & (tile_col == 0))
                    def _():
                        put(u0[...].T)

                    @pl.when((tile_row == 1) & (tile_col == 1))
                    def _():
                        put(u1[...].T)


VMEM = pl.BlockSpec(memory_space=pltpu.VMEM)
SMEM = pl.BlockSpec(memory_space=pltpu.SMEM)


def shape(*dims):
    return jax.ShapeDtypeStruct(dims, jnp.float32)


def call(kernel, out_shape, flops, *args, smem=0, vmem=16, scratch=()):
    return pl.pallas_call(
        kernel,
        out_shape=out_shape,
        in_specs=[SMEM] * smem + [VMEM] * (len(args) - smem),
        out_specs=jax.tree.map(lambda _: VMEM, out_shape),
        scratch_shapes=list(scratch),
        compiler_params=pltpu.CompilerParams(vmem_limit_bytes=vmem * 2**20),
        cost_estimate=pl.CostEstimate(flops=flops, bytes_accessed=2**22, transcendentals=0),
    )(*args)


def on_device(n_row, n_col, trailing_in):
    row = lax.axis_index("row")
    col = lax.axis_index("col")
    loc_rows, _, _, loc_cols, _, _ = trailing_in.shape
    stride = 2 * loc_cols
    chips = n_row // 2
    chip = row // 2
    own = trailing_in.reshape(loc_rows * NB * stride, HALF)
    pos = jnp.stack([row, col, jnp.int32(n_row), jnp.int32(n_col)]).astype(jnp.int32)
    row_bits = [1 << k for k in range(1, (n_row - 1).bit_length())]
    col_bits = [1 << k for k in range(1, (n_col - 1).bit_length())][::-1]
    after = lax.optimization_barrier

    def swap(value, axis, bits):
        size = n_row if axis == "row" else n_col
        return lax.ppermute(value, axis, [(i, i ^ bits) for i in range(size)])

    def pick(index, values):
        out = values[0]
        for k, value in enumerate(values[1:], 1):
            out = jnp.where(index == k, value, out)
        return out

    def settle(value, axis, bit, got):
        return jnp.where((row if axis == "row" else col) & bit != 0, got, value)

    half = HALF * stride
    top_a, top_b, *left = call(
        functools.partial(pack_kernel, loc_rows, loc_cols),
        [shape(half, HALF), shape(half, HALF)] + [shape(NB, NB)] * loc_rows,
        10**8,
        own,
    )

    size = NB // chips
    pieces = [left[0][k * size : (k + 1) * size] for k in range(chips)]
    piece = pick(chip, [pieces[0]] + [swap(pieces[k], "row", 2 * k) for k in range(1, chips)])
    along = [piece] + [swap(piece, "col", k) for k in range(1, n_col)]
    top_a, top_b, along[1] = after((top_a, top_b, along[1]))
    got_a, got_b = swap(top_a, "row", row_bits[0]), swap(top_b, "row", row_bits[-1])
    pair = jnp.concatenate([pick(col, along), pick(col ^ 1, along)], axis=0)
    got = [pair] + [swap(pair, "row", 2 * k) for k in range(1, chips)]
    left[0], got[1] = after((left[0], got[1]))
    got_left = [swap(left[0], "col", col_bits[0])]
    got_a, got_b, got = after((got_a, got_b, got))
    lead = [
        jnp.concatenate(
            [pick(chip ^ k, got)[j * size : (j + 1) * size] for k in range(chips)], axis=0
        )
        for j in (0, 1)
    ]
    lead_other = swap(jnp.where(row % 2 == 0, lead[0], lead[1]), "row", 1)

    left, lead[0] = after((left, lead[0]))
    top_a = settle(top_a, "row", row_bits[0], got_a)
    top_b = settle(top_b, "row", row_bits[-1], got_b)
    for first, second in zip(row_bits[1:-1], row_bits[-2:0:-1]):
        top_a = settle(top_a, "row", first, swap(top_a, "row", first))
        top_b = settle(top_b, "row", second, swap(top_b, "row", second))
    got_a, got_b = swap(top_a, "row", row_bits[-1]), swap(top_b, "row", row_bits[0])
    got_left += [swap(left[a], "col", col_bits[0]) for a in range(1, loc_rows)]
    u0, x0 = call(first_kernel, [shape(NB, NB)] * 2, 10**10, pos, lead[0], lead_other, smem=1)

    got_a, got_b, got_left, lead[1], x0 = after((got_a, got_b, got_left, lead[1], x0))
    lead_next = swap(lead[1], "row", 1)
    right = []
    for a in range(loc_rows):
        left[a] = settle(left[a], "col", col_bits[0], got_left[a])
        for bit in col_bits[1:]:
            left[a] = settle(left[a], "col", bit, swap(left[a], "col", bit))
        right.append(swap(left[a], "col", 1))
    top_a = settle(top_a, "row", row_bits[-1], got_a)
    top_b = settle(top_b, "row", row_bits[0], got_b)
    other_a, other_b = swap(top_a, "row", 1), swap(top_b, "row", 1)
    u1, x1, w = call(
        second_kernel,
        [shape(NB, NB)] * 3,
        10**10,
        pos, x0, lead[0], lead[1], lead_other, lead_next,
        smem=1,
    )
    right, other_a, other_b, x1 = after((right, other_a, other_b, x1))
    out = call(
        functools.partial(last_kernel, loc_rows, loc_cols),
        shape(*own.shape),
        10**7,
        pos, own, top_a, top_b, other_a, other_b, u0, x0, u1, x1, w, *left, *right,
        smem=1,
        vmem=24,
        scratch=[pltpu.VMEM((2 * loc_rows, NB, NB), jnp.float32)],
    )
    return out.reshape(trailing_in.shape)


def solution(mesh):
    return jax.shard_map(
        functools.partial(on_device, mesh.shape["row"], mesh.shape["col"]),
        mesh=mesh,
        in_specs=(P(None, "row", None, None, "col", None),),
        out_specs=P(None, "row", None, None, "col", None),
        check_vma=False,
    )
```

```python
import functools

import jax
import jax.numpy as jnp
from jax import lax
from jax.experimental import pallas as pl
from jax.experimental.pallas import tpu as pltpu
from jax.sharding import PartitionSpec as P

NB = 256
HALF = 128
SUB = 8
HIGHEST = lax.Precision.HIGHEST
HIGH = lax.Precision.HIGH


def mm(a, b, precision=HIGHEST):
    return lax.dot_general(
        a, b, (((1,), (0,)), ((), ())), precision=precision, preferred_element_type=jnp.float32
    )


def mm_t(a, b, precision=HIGHEST):
    return lax.dot_general(
        a, b, (((1,), (1,)), ((), ())), precision=precision, preferred_element_type=jnp.float32
    )


def t_mm(a, b, precision=HIGHEST):
    return lax.dot_general(
        a, b, (((0,), (0,)), ((), ())), precision=precision, preferred_element_type=jnp.float32
    )


def spread(x):
    return jnp.broadcast_to(x, (SUB, HALF))


def factor_half(s):
    groups = HALF // SUB
    lane = lax.broadcasted_iota(jnp.int32, (SUB, HALF), 1)
    sub = lax.broadcasted_iota(jnp.int32, (SUB, HALF), 0)
    rows = [s[SUB * g : SUB * (g + 1), :] for g in range(groups)]
    own_diagonal = [jnp.where(lane == sub + SUB * g, rows[g], 0.0) for g in range(groups)]
    diagonal = spread(jnp.sum(sum(own_diagonal), axis=0, keepdims=True))
    scale = lax.rsqrt(diagonal)
    unscale = diagonal * scale
    eyes = []
    for g in range(groups):
        down = spread(lax.rsqrt(jnp.sum(own_diagonal[g], axis=1, keepdims=True)))
        rows[g] = (rows[g] * scale) * down
        eyes.append(jnp.where(lane == sub + SUB * g, 1.0, 0.0).astype(jnp.float32))
    out_u, out_x = [], []
    for g in range(groups):
        base = SUB * g
        own = rows[g]
        own_x = eyes[g]
        a = {}
        for j in range(SUB):
            column = spread(own[:, base + j : base + j + 1])
            for i in range(j + 1):
                a[i, j] = spread(column[i : i + 1, :])
        near = None
        if g + 1 < groups:
            near = [spread(rows[g + 1][:, base + j : base + j + 1]) for j in range(SUB)]
        u = [spread(own[i : i + 1, :]) for i in range(SUB)]
        x = [spread(own_x[i : i + 1, :]) for i in range(SUB)]
        r = [None] * SUB
        l = {}
        for k in range(0, SUB, 2):
            p, q, t = a[k, k], a[k, k + 1], a[k + 1, k + 1]
            r[k] = lax.rsqrt(p)
            root = lax.rsqrt(p * t - q * q)
            both = r[k] * root
            r[k + 1] = (p * r[k]) * root
            l[k, k + 1] = q * r[k]
            for j in range(k + 2, SUB):
                l[k, j] = a[k, j] * r[k]
                l[k + 1, j] = (p * a[k + 1, j] - q * a[k, j]) * both
            for i in range(k + 2, SUB):
                for j in range(i, SUB):
                    a[i, j] = (a[i, j] - l[k, i] * l[k, j]) - l[k + 1, i] * l[k + 1, j]
            for m in (k, k + 1):
                u[m] = u[m] * r[m]
                x[m] = x[m] * r[m]
                if near is not None:
                    near[m] = near[m] * r[m]
                for i in range(m + 1, SUB):
                    u[i] = u[i] - l[m, i] * u[m]
                    x[i] = x[i] - l[m, i] * x[m]
                    if near is not None:
                        near[i] = near[i] - l[m, i] * near[m]
        final_u, final_x = u[0], x[0]
        for i in range(1, SUB):
            final_u = jnp.where(sub == i, u[i], final_u)
            final_x = jnp.where(sub == i, x[i], final_x)
        out_u.append(jnp.where(lane >= sub + base, final_u * unscale, 0.0))
        out_x.append(final_x * scale)
        if near is not None:
            nxt, nxt_x = rows[g + 1], eyes[g + 1]
            for k in range(SUB):
                nxt = nxt - near[k] * u[k]
                nxt_x = nxt_x - near[k] * x[k]
        if g + 2 < groups:
            v, vx = list(u), list(x)
            for i in reversed(range(SUB)):
                for j in range(i + 1, SUB):
                    v[i] = v[i] - l[i, j] * v[j]
                    vx[i] = vx[i] - l[i, j] * vx[j]
                v[i] = v[i] * r[i]
                vx[i] = vx[i] * r[i]
            for h in range(g + 2, groups):
                far, far_x = rows[h], eyes[h]
                for j in range(SUB):
                    c = spread(rows[h][:, base + j : base + j + 1])
                    far = far - c * v[j]
                    far_x = far_x - c * vx[j]
                rows[h], eyes[h] = far, far_x
        if near is not None:
            rows[g + 1], eyes[g + 1] = nxt, nxt_x
    return jnp.concatenate(out_u, axis=0), jnp.concatenate(out_x, axis=0)


def finish_blocks(u11, u12, x11, rest, u_ref, x_ref):
    zero = jnp.zeros((HALF, HALF), jnp.float32)
    u22, x22 = factor_half(rest)
    u_ref[:HALF, :HALF] = u11
    u_ref[:HALF, HALF:] = u12
    u_ref[HALF:, :HALF] = zero
    u_ref[HALF:, HALF:] = u22
    x_ref[:HALF, :HALF] = x11
    x_ref[:HALF, HALF:] = zero
    x_ref[HALF:, :HALF] = -mm(x22, t_mm(u12, x11))
    x_ref[HALF:, HALF:] = x22


def factor_blocks(s11, s12, s22, u_ref, x_ref):
    u11, x11 = factor_half(s11)
    u12 = mm(x11, s12)
    finish_blocks(u11, u12, x11, s22 - t_mm(u12, u12), u_ref, x_ref)


def tile_from(ref, start, stride):
    return jnp.concatenate(
        [ref[pl.ds(start, NB, stride=stride), :], ref[pl.ds(start + 1, NB, stride=stride), :]], axis=1
    )


def pack_kernel(loc_rows, loc_cols, own, top_a, top_b, *left):
    stride = 2 * loc_cols
    for a in range(loc_rows):
        left[a][...] = tile_from(own, a * NB * stride, stride)
    half = HALF * stride
    top_a[...] = own[:half, :]
    top_b[...] = own[half : 2 * half, :]


def start_blocks(s, u_ref, x_ref, rest_ref):
    u11, x11 = factor_half(s[:HALF, :HALF])
    u12 = mm(x11, s[:HALF, HALF:])
    u_ref[:HALF, :] = u11
    u_ref[HALF:, :] = u12
    x_ref[...] = x11
    rest_ref[...] = s[HALF:, HALF:] - t_mm(u12, u12)


def first_kernel(pos, mine, other, u_ref, x_ref):
    s = jnp.where(pos[0] % 2 == 0, mine[...], other[...])
    factor_blocks(s[:HALF, :HALF], s[:HALF, HALF:], s[HALF:, HALF:], u_ref, x_ref)


def second_kernel(pos, x0, mine0, mine1, other0, other1, u01_ref, u_ref, x_ref, rest_ref):
    even = pos[0] % 2 == 0
    u01 = mm(x0[...], jnp.where(even, mine1[...], other1[...]))
    u01_ref[...] = u01
    start_blocks(jnp.where(even, other0[...], mine1[...]) - t_mm(u01, u01), u_ref, x_ref, rest_ref)


def third_kernel(x0, u01, ua, xa, rest, u_ref, x_ref, w_ref):
    finish_blocks(ua[:HALF, :], ua[HALF:, :], xa[...], rest[...], u_ref, x_ref)
    w_ref[...] = -mm(x_ref[...], t_mm(u01[...], x0[...]))


def last_kernel(
    loc_rows, loc_cols, pos, own, mine_a, mine_b, other_a, other_b, u0, x0, u1, x1, w, *rest
):
    left, right = rest[:loc_rows], rest[loc_rows : 2 * loc_rows]
    out, prows = rest[2 * loc_rows :]
    stride = 2 * loc_cols
    even = pos[0] % 2 == 0
    even_col = pos[1] % 2 == 0
    for a in range(loc_rows):
        l, r = left[a][...], right[a][...]
        b0, b1 = jnp.where(even_col, l, r), jnp.where(even_col, r, l)
        prows[2 * a] = mm_t(b0, x0[...], HIGH)
        prows[2 * a + 1] = mm_t(b0, w[...], HIGH) + mm_t(b1, x1[...], HIGH)

    def top_tile(a, b, start):
        halves = [
            jnp.concatenate(
                [ref[pl.ds(start + k, HALF, stride=stride), :] for k in (0, 1)], axis=1
            )
            for ref in (a, b)
        ]
        return jnp.concatenate(halves, axis=0)

    for b in range(loc_cols):
        tile_col = pos[1] + b * pos[3]
        e, o = top_tile(mine_a, mine_b, 2 * b), top_tile(other_a, other_b, 2 * b)
        d0, d1 = jnp.where(even, e, o), jnp.where(even, o, e)
        q0 = mm(x0[...], d0, HIGH)
        q1 = mm(w[...], d0, HIGH) + mm(x1[...], d1, HIGH)
        for a in range(loc_rows):
            tile_row = pos[0] + a * pos[2]
            start = a * NB * stride + 2 * b

            def put(value, start=start):
                out[pl.ds(start, NB, stride=stride), :] = value[:, :HALF]
                out[pl.ds(start + 1, NB, stride=stride), :] = value[:, HALF:]

            @pl.when(tile_row < tile_col)
            def _():
                put(jnp.zeros((NB, NB), jnp.float32))

            @pl.when((tile_row >= tile_col) & (tile_col >= 2))
            def _():
                put(
                    tile_from(own, start, stride)
                    - (mm(prows[2 * a], q0, HIGH) + mm(prows[2 * a + 1], q1, HIGH))
                )

            if b == 0:

                @pl.when((tile_row > 0) & (tile_col == 0))
                def _():
                    put(prows[2 * a])

                @pl.when((tile_row > 1) & (tile_col == 1))
                def _():
                    put(prows[2 * a + 1])

                if a == 0:

                    @pl.when((tile_row == 0) & (tile_col == 0))
                    def _():
                        put(u0[...].T)

                    @pl.when((tile_row == 1) & (tile_col == 1))
                    def _():
                        put(u1[...].T)


VMEM = pl.BlockSpec(memory_space=pltpu.VMEM)
SMEM = pl.BlockSpec(memory_space=pltpu.SMEM)


def shape(*dims):
    return jax.ShapeDtypeStruct(dims, jnp.float32)


def call(kernel, out_shape, flops, *args, smem=0, vmem=16, scratch=()):
    return pl.pallas_call(
        kernel,
        out_shape=out_shape,
        in_specs=[SMEM] * smem + [VMEM] * (len(args) - smem),
        out_specs=jax.tree.map(lambda _: VMEM, out_shape),
        scratch_shapes=list(scratch),
        compiler_params=pltpu.CompilerParams(vmem_limit_bytes=vmem * 2**20),
        cost_estimate=pl.CostEstimate(flops=flops, bytes_accessed=2**22, transcendentals=0),
    )(*args)


def on_device(n_row, n_col, trailing_in):
    row = lax.axis_index("row")
    col = lax.axis_index("col")
    loc_rows, _, _, loc_cols, _, _ = trailing_in.shape
    stride = 2 * loc_cols
    chips = n_row // 2
    chip = row // 2
    own = trailing_in.reshape(loc_rows * NB * stride, HALF)
    pos = jnp.stack([row, col, jnp.int32(n_row), jnp.int32(n_col)]).astype(jnp.int32)
    row_bits = [1 << k for k in range(1, (n_row - 1).bit_length())]
    col_bits = [1 << k for k in range(1, (n_col - 1).bit_length())][::-1]
    after = lax.optimization_barrier

    def swap(value, axis, bits):
        size = n_row if axis == "row" else n_col
        return lax.ppermute(value, axis, [(i, i ^ bits) for i in range(size)])

    def pick(index, values):
        out = values[0]
        for k, value in enumerate(values[1:], 1):
            out = jnp.where(index == k, value, out)
        return out

    def settle(value, axis, bit, got):
        return jnp.where((row if axis == "row" else col) & bit != 0, got, value)

    half = HALF * stride
    top_a, top_b, *left = call(
        functools.partial(pack_kernel, loc_rows, loc_cols),
        [shape(half, HALF), shape(half, HALF)] + [shape(NB, NB)] * loc_rows,
        10**8,
        own,
    )

    size = NB // chips
    pieces = [left[0][k * size : (k + 1) * size] for k in range(chips)]
    got = [swap(pieces[k], "row", 2 * k) for k in range(1, chips)]
    top_a, top_b, got = after((top_a, top_b, got))
    got_a, got_b = swap(top_a, "row", row_bits[0]), swap(top_b, "row", row_bits[-1])
    piece = pick(chip, [pieces[0]] + got)
    along = [piece] + [swap(piece, "col", k) for k in range(1, n_col)]
    got_a, got_b, along = after((got_a, got_b, along))
    pair = jnp.concatenate([pick(col, along), pick(col ^ 1, along)], axis=0)
    got = [pair] + [swap(pair, "row", 2 * k) for k in range(1, chips)]
    left[0], got[1] = after((left[0], got[1]))
    got_left = [swap(left[0], "col", col_bits[0])]
    lead = [
        jnp.concatenate(
            [pick(chip ^ k, got)[j * size : (j + 1) * size] for k in range(chips)], axis=0
        )
        for j in (0, 1)
    ]
    lead_other = swap(jnp.where(row % 2 == 0, lead[0], lead[1]), "row", 1)

    top_a, top_b, got_a, got_b, lead[0] = after((top_a, top_b, got_a, got_b, lead[0]))
    top_a = settle(top_a, "row", row_bits[0], got_a)
    top_b = settle(top_b, "row", row_bits[-1], got_b)
    for first, second in zip(row_bits[1:-1], row_bits[-2:0:-1]):
        top_a = settle(top_a, "row", first, swap(top_a, "row", first))
        top_b = settle(top_b, "row", second, swap(top_b, "row", second))
    got_a, got_b = swap(top_a, "row", row_bits[-1]), swap(top_b, "row", row_bits[0])
    u0, x0 = call(first_kernel, [shape(NB, NB)] * 2, 10**10, pos, lead[0], lead_other, smem=1)

    got_left, lead[1], x0 = after((got_left, lead[1], x0))
    lead_next = swap(lead[1], "row", 1)
    left, x0 = after((left, x0))
    got_left += [swap(left[a], "col", col_bits[0]) for a in range(1, loc_rows)]

    def columns(a):
        value = settle(left[a], "col", col_bits[0], got_left[a])
        for bit in col_bits[1:]:
            value = settle(value, "col", bit, swap(value, "col", bit))
        return value, swap(value, "col", 1)

    both = [columns(0)]
    u01, u_half, x_half, rest = call(
        second_kernel,
        [shape(NB, NB), shape(NB, HALF), shape(HALF, HALF), shape(HALF, HALF)],
        5 * 10**9,
        pos, x0, lead[0], lead[1], lead_other, lead_next,
        smem=1,
    )
    got_a, got_b, got_left[1:], rest = after((got_a, got_b, got_left[1:], rest))
    top_a = settle(top_a, "row", row_bits[-1], got_a)
    top_b = settle(top_b, "row", row_bits[0], got_b)
    other_a, other_b = swap(top_a, "row", 1), swap(top_b, "row", 1)
    both += [columns(a) for a in range(1, loc_rows)]
    left, right = [b[0] for b in both], [b[1] for b in both]
    u1, x1, w = call(
        third_kernel, [shape(NB, NB)] * 3, 5 * 10**9, x0, u01, u_half, x_half, rest
    )
    right, other_a, other_b, x1 = after((right, other_a, other_b, x1))
    out = call(
        functools.partial(last_kernel, loc_rows, loc_cols),
        shape(*own.shape),
        10**7,
        pos, own, top_a, top_b, other_a, other_b, u0, x0, u1, x1, w, *left, *right,
        smem=1,
        vmem=24,
        scratch=[pltpu.VMEM((2 * loc_rows, NB, NB), jnp.float32)],
    )
    return out.reshape(trailing_in.shape)


def solution(mesh):
    return jax.shard_map(
        functools.partial(on_device, mesh.shape["row"], mesh.shape["col"]),
        mesh=mesh,
        in_specs=(P(None, "row", None, None, "col", None),),
        out_specs=P(None, "row", None, None, "col", None),
        check_vma=False,
    )
```

```python
import functools

import jax
import jax.numpy as jnp
from jax import lax
from jax.experimental import pallas as pl
from jax.experimental.pallas import tpu as pltpu
from jax.sharding import PartitionSpec as P

NB = 256
HALF = 128
SUB = 8
HIGHEST = lax.Precision.HIGHEST
HIGH = lax.Precision.HIGH


def mm(a, b, precision=HIGHEST):
    return lax.dot_general(
        a, b, (((1,), (0,)), ((), ())), precision=precision, preferred_element_type=jnp.float32
    )


def mm_t(a, b, precision=HIGHEST):
    return lax.dot_general(
        a, b, (((1,), (1,)), ((), ())), precision=precision, preferred_element_type=jnp.float32
    )


def t_mm(a, b, precision=HIGHEST):
    return lax.dot_general(
        a, b, (((0,), (0,)), ((), ())), precision=precision, preferred_element_type=jnp.float32
    )


def spread(x):
    return jnp.broadcast_to(x, (SUB, HALF))


def factor_half(s):
    groups = HALF // SUB
    lane = lax.broadcasted_iota(jnp.int32, (SUB, HALF), 1)
    sub = lax.broadcasted_iota(jnp.int32, (SUB, HALF), 0)
    rows = [s[SUB * g : SUB * (g + 1), :] for g in range(groups)]
    own_diagonal = [jnp.where(lane == sub + SUB * g, rows[g], 0.0) for g in range(groups)]
    diagonal = spread(jnp.sum(sum(own_diagonal), axis=0, keepdims=True))
    scale = lax.rsqrt(diagonal)
    unscale = diagonal * scale
    eyes = []
    for g in range(groups):
        down = spread(lax.rsqrt(jnp.sum(own_diagonal[g], axis=1, keepdims=True)))
        rows[g] = (rows[g] * scale) * down
        eyes.append(jnp.where(lane == sub + SUB * g, 1.0, 0.0).astype(jnp.float32))
    out_u, out_x = [], []
    for g in range(groups):
        base = SUB * g
        own = rows[g]
        own_x = eyes[g]
        a = {}
        for j in range(SUB):
            column = spread(own[:, base + j : base + j + 1])
            for i in range(j + 1):
                a[i, j] = spread(column[i : i + 1, :])
        near = None
        if g + 1 < groups:
            near = [spread(rows[g + 1][:, base + j : base + j + 1]) for j in range(SUB)]
        u = [spread(own[i : i + 1, :]) for i in range(SUB)]
        x = [spread(own_x[i : i + 1, :]) for i in range(SUB)]
        r = [None] * SUB
        l = {}
        for k in range(0, SUB, 2):
            p, q, t = a[k, k], a[k, k + 1], a[k + 1, k + 1]
            r[k] = lax.rsqrt(p)
            root = lax.rsqrt(p * t - q * q)
            both = r[k] * root
            r[k + 1] = (p * r[k]) * root
            l[k, k + 1] = q * r[k]
            for j in range(k + 2, SUB):
                l[k, j] = a[k, j] * r[k]
                l[k + 1, j] = (p * a[k + 1, j] - q * a[k, j]) * both
            for i in range(k + 2, SUB):
                for j in range(i, SUB):
                    a[i, j] = (a[i, j] - l[k, i] * l[k, j]) - l[k + 1, i] * l[k + 1, j]
            for m in (k, k + 1):
                u[m] = u[m] * r[m]
                x[m] = x[m] * r[m]
                if near is not None:
                    near[m] = near[m] * r[m]
                for i in range(m + 1, SUB):
                    u[i] = u[i] - l[m, i] * u[m]
                    x[i] = x[i] - l[m, i] * x[m]
                    if near is not None:
                        near[i] = near[i] - l[m, i] * near[m]
        final_u, final_x = u[0], x[0]
        for i in range(1, SUB):
            final_u = jnp.where(sub == i, u[i], final_u)
            final_x = jnp.where(sub == i, x[i], final_x)
        out_u.append(jnp.where(lane >= sub + base, final_u * unscale, 0.0))
        out_x.append(final_x * scale)
        if near is not None:
            nxt, nxt_x = rows[g + 1], eyes[g + 1]
            for k in range(SUB):
                nxt = nxt - near[k] * u[k]
                nxt_x = nxt_x - near[k] * x[k]
        if g + 2 < groups:
            v, vx = list(u), list(x)
            for i in reversed(range(SUB)):
                for j in range(i + 1, SUB):
                    v[i] = v[i] - l[i, j] * v[j]
                    vx[i] = vx[i] - l[i, j] * vx[j]
                v[i] = v[i] * r[i]
                vx[i] = vx[i] * r[i]
            for h in range(g + 2, groups):
                far, far_x = rows[h], eyes[h]
                for j in range(SUB):
                    c = spread(rows[h][:, base + j : base + j + 1])
                    far = far - c * v[j]
                    far_x = far_x - c * vx[j]
                rows[h], eyes[h] = far, far_x
        if near is not None:
            rows[g + 1], eyes[g + 1] = nxt, nxt_x
    return jnp.concatenate(out_u, axis=0), jnp.concatenate(out_x, axis=0)


def finish_blocks(u11, u12, x11, rest, u_ref, x_ref):
    zero = jnp.zeros((HALF, HALF), jnp.float32)
    u22, x22 = factor_half(rest)
    u_ref[:HALF, :HALF] = u11
    u_ref[:HALF, HALF:] = u12
    u_ref[HALF:, :HALF] = zero
    u_ref[HALF:, HALF:] = u22
    x_ref[:HALF, :HALF] = x11
    x_ref[:HALF, HALF:] = zero
    x_ref[HALF:, :HALF] = -mm(x22, t_mm(u12, x11))
    x_ref[HALF:, HALF:] = x22


def factor_blocks(s11, s12, s22, u_ref, x_ref):
    u11, x11 = factor_half(s11)
    u12 = mm(x11, s12)
    finish_blocks(u11, u12, x11, s22 - t_mm(u12, u12), u_ref, x_ref)


def tile_from(ref, start, stride):
    return jnp.concatenate(
        [ref[pl.ds(start, NB, stride=stride), :], ref[pl.ds(start + 1, NB, stride=stride), :]], axis=1
    )


def pack_kernel(loc_rows, loc_cols, own, top_a, top_b, *left):
    stride = 2 * loc_cols
    for a in range(loc_rows):
        left[a][...] = tile_from(own, a * NB * stride, stride)
    half = HALF * stride
    top_a[...] = own[:half, :]
    top_b[...] = own[half : 2 * half, :]


def first_kernel(pos, mine, other, u_ref, x_ref):
    s = jnp.where(pos[0] % 2 == 0, mine[...], other[...])
    factor_blocks(s[:HALF, :HALF], s[:HALF, HALF:], s[HALF:, HALF:], u_ref, x_ref)


def second_kernel(pos, x0, mine0, mine1, other0, other1, u_ref, x_ref, w_ref):
    even = pos[0] % 2 == 0
    u01 = mm(x0[...], jnp.where(even, mine1[...], other1[...]))
    s = jnp.where(even, other0[...], mine1[...]) - t_mm(u01, u01)
    factor_blocks(s[:HALF, :HALF], s[:HALF, HALF:], s[HALF:, HALF:], u_ref, x_ref)
    w_ref[...] = -mm(x_ref[...], t_mm(u01, x0[...]))


def last_kernel(
    loc_rows, loc_cols, pos, own, mine_a, mine_b, other_a, other_b, u0, x0, u1, x1, w, *rest
):
    left, right = rest[:loc_rows], rest[loc_rows : 2 * loc_rows]
    out, prows = rest[2 * loc_rows :]
    stride = 2 * loc_cols
    even = pos[0] % 2 == 0
    even_col = pos[1] % 2 == 0
    for a in range(loc_rows):
        l, r = left[a][...], right[a][...]
        b0, b1 = jnp.where(even_col, l, r), jnp.where(even_col, r, l)
        prows[2 * a] = mm_t(b0, x0[...], HIGH)
        prows[2 * a + 1] = mm_t(b0, w[...], HIGH) + mm_t(b1, x1[...], HIGH)

    def top_tile(a, b, start):
        halves = [
            jnp.concatenate(
                [ref[pl.ds(start + k, HALF, stride=stride), :] for k in (0, 1)], axis=1
            )
            for ref in (a, b)
        ]
        return jnp.concatenate(halves, axis=0)

    for b in range(loc_cols):
        tile_col = pos[1] + b * pos[3]
        e, o = top_tile(mine_a, mine_b, 2 * b), top_tile(other_a, other_b, 2 * b)
        d0, d1 = jnp.where(even, e, o), jnp.where(even, o, e)
        q0 = mm(x0[...], d0, HIGH)
        q1 = mm(w[...], d0, HIGH) + mm(x1[...], d1, HIGH)
        for a in range(loc_rows):
            tile_row = pos[0] + a * pos[2]
            start = a * NB * stride + 2 * b

            def put(value, start=start):
                out[pl.ds(start, NB, stride=stride), :] = value[:, :HALF]
                out[pl.ds(start + 1, NB, stride=stride), :] = value[:, HALF:]

            @pl.when(tile_row < tile_col)
            def _():
                put(jnp.zeros((NB, NB), jnp.float32))

            @pl.when((tile_row >= tile_col) & (tile_col >= 2))
            def _():
                put(
                    tile_from(own, start, stride)
                    - (mm(prows[2 * a], q0, HIGH) + mm(prows[2 * a + 1], q1, HIGH))
                )

            if b == 0:

                @pl.when((tile_row > 0) & (tile_col == 0))
                def _():
                    put(prows[2 * a])

                @pl.when((tile_row > 1) & (tile_col == 1))
                def _():
                    put(prows[2 * a + 1])

                if a == 0:

                    @pl.when((tile_row == 0) & (tile_col == 0))
                    def _():
                        put(u0[...].T)

                    @pl.when((tile_row == 1) & (tile_col == 1))
                    def _():
                        put(u1[...].T)


VMEM = pl.BlockSpec(memory_space=pltpu.VMEM)
SMEM = pl.BlockSpec(memory_space=pltpu.SMEM)


def shape(*dims):
    return jax.ShapeDtypeStruct(dims, jnp.float32)


def call(kernel, out_shape, flops, *args, smem=0, vmem=16, scratch=()):
    return pl.pallas_call(
        kernel,
        out_shape=out_shape,
        in_specs=[SMEM] * smem + [VMEM] * (len(args) - smem),
        out_specs=jax.tree.map(lambda _: VMEM, out_shape),
        scratch_shapes=list(scratch),
        compiler_params=pltpu.CompilerParams(vmem_limit_bytes=vmem * 2**20),
        cost_estimate=pl.CostEstimate(flops=flops, bytes_accessed=2**22, transcendentals=0),
    )(*args)


def on_device(n_row, n_col, trailing_in):
    row = lax.axis_index("row")
    col = lax.axis_index("col")
    loc_rows, _, _, loc_cols, _, _ = trailing_in.shape
    stride = 2 * loc_cols
    chips = n_row // 2
    chip = row // 2
    own = trailing_in.reshape(loc_rows * NB * stride, HALF)
    pos = jnp.stack([row, col, jnp.int32(n_row), jnp.int32(n_col)]).astype(jnp.int32)
    row_bits = [1 << k for k in range(1, (n_row - 1).bit_length())]
    col_bits = [1 << k for k in range(1, (n_col - 1).bit_length())][::-1]
    after = lax.optimization_barrier

    def swap(value, axis, bits):
        size = n_row if axis == "row" else n_col
        return lax.ppermute(value, axis, [(i, i ^ bits) for i in range(size)])

    def pick(index, values):
        out = values[0]
        for k, value in enumerate(values[1:], 1):
            out = jnp.where(index == k, value, out)
        return out

    def settle(value, axis, bit, got):
        return jnp.where((row if axis == "row" else col) & bit != 0, got, value)

    half = HALF * stride
    top_a, top_b, *left = call(
        functools.partial(pack_kernel, loc_rows, loc_cols),
        [shape(half, HALF), shape(half, HALF)] + [shape(NB, NB)] * loc_rows,
        10**8,
        own,
    )

    size = NB // chips
    pieces = [left[0][k * size : (k + 1) * size] for k in range(chips)]
    got_a, got_b = swap(top_a, "row", row_bits[0]), swap(top_b, "row", row_bits[-1])
    got_left = [swap(left[0], "col", col_bits[0])]
    piece = pick(chip, [pieces[0]] + [swap(pieces[k], "row", 2 * k) for k in range(1, chips)])
    along = [piece] + [swap(piece, "col", k) for k in range(1, n_col)]
    got_a, got_b, got_left, along = after((got_a, got_b, got_left, along))
    pair = jnp.concatenate([pick(col, along), pick(col ^ 1, along)], axis=0)
    got = [pair] + [swap(pair, "row", 2 * k) for k in range(1, chips)]
    lead = [
        jnp.concatenate(
            [pick(chip ^ k, got)[j * size : (j + 1) * size] for k in range(chips)], axis=0
        )
        for j in (0, 1)
    ]
    lead_other = swap(jnp.where(row % 2 == 0, lead[0], lead[1]), "row", 1)

    def columns(a):
        value = settle(left[a], "col", col_bits[0], got_left[a])
        for bit in col_bits[1:]:
            value = settle(value, "col", bit, swap(value, "col", bit))
        return value, swap(value, "col", 1)

    top_a, top_b, left[1:], lead[0] = after((top_a, top_b, left[1:], lead[0]))
    top_a = settle(top_a, "row", row_bits[0], got_a)
    top_b = settle(top_b, "row", row_bits[-1], got_b)
    for first, second in zip(row_bits[1:-1], row_bits[-2:0:-1]):
        top_a = settle(top_a, "row", first, swap(top_a, "row", first))
        top_b = settle(top_b, "row", second, swap(top_b, "row", second))
    got_a, got_b = swap(top_a, "row", row_bits[-1]), swap(top_b, "row", row_bits[0])
    got_left += [swap(left[a], "col", col_bits[0]) for a in range(1, loc_rows)]
    both = [columns(0)]
    lead_other, both[0] = after((lead_other, both[0]))
    u0, x0 = call(first_kernel, [shape(NB, NB)] * 2, 10**10, pos, lead[0], lead_other, smem=1)

    got_a, got_b, got_left, lead[1], x0 = after((got_a, got_b, got_left, lead[1], x0))
    lead_next = swap(lead[1], "row", 1)
    both += [columns(a) for a in range(1, loc_rows)]
    left, right = [b[0] for b in both], [b[1] for b in both]
    top_a = settle(top_a, "row", row_bits[-1], got_a)
    top_b = settle(top_b, "row", row_bits[0], got_b)
    other_a, other_b = swap(top_a, "row", 1), swap(top_b, "row", 1)
    u1, x1, w = call(
        second_kernel,
        [shape(NB, NB)] * 3,
        10**10,
        pos, x0, lead[0], lead[1], lead_other, lead_next,
        smem=1,
    )
    right, other_a, other_b, x1 = after((right, other_a, other_b, x1))
    out = call(
        functools.partial(last_kernel, loc_rows, loc_cols),
        shape(*own.shape),
        10**7,
        pos, own, top_a, top_b, other_a, other_b, u0, x0, u1, x1, w, *left, *right,
        smem=1,
        vmem=24,
        scratch=[pltpu.VMEM((2 * loc_rows, NB, NB), jnp.float32)],
    )
    return out.reshape(trailing_in.shape)


def solution(mesh):
    return jax.shard_map(
        functools.partial(on_device, mesh.shape["row"], mesh.shape["col"]),
        mesh=mesh,
        in_specs=(P(None, "row", None, None, "col", None),),
        out_specs=P(None, "row", None, None, "col", None),
        check_vma=False,
    )
```

```python
import functools

import jax
import jax.numpy as jnp
from jax import lax
from jax.experimental import pallas as pl
from jax.experimental.pallas import tpu as pltpu
from jax.sharding import PartitionSpec as P

NB = 256
HALF = 128
SUB = 8
HIGHEST = lax.Precision.HIGHEST
HIGH = lax.Precision.HIGH


def mm(a, b, precision=HIGHEST):
    return lax.dot_general(
        a, b, (((1,), (0,)), ((), ())), precision=precision, preferred_element_type=jnp.float32
    )


def mm_t(a, b, precision=HIGHEST):
    return lax.dot_general(
        a, b, (((1,), (1,)), ((), ())), precision=precision, preferred_element_type=jnp.float32
    )


def t_mm(a, b, precision=HIGHEST):
    return lax.dot_general(
        a, b, (((0,), (0,)), ((), ())), precision=precision, preferred_element_type=jnp.float32
    )


def spread(x):
    return jnp.broadcast_to(x, (SUB, HALF))


def factor_half(s):
    groups = HALF // SUB
    lane = lax.broadcasted_iota(jnp.int32, (SUB, HALF), 1)
    sub = lax.broadcasted_iota(jnp.int32, (SUB, HALF), 0)
    rows = [s[SUB * g : SUB * (g + 1), :] for g in range(groups)]
    own_diagonal = [jnp.where(lane == sub + SUB * g, rows[g], 0.0) for g in range(groups)]
    diagonal = spread(jnp.sum(sum(own_diagonal), axis=0, keepdims=True))
    scale = lax.rsqrt(diagonal)
    unscale = diagonal * scale
    eyes = []
    for g in range(groups):
        down = spread(lax.rsqrt(jnp.sum(own_diagonal[g], axis=1, keepdims=True)))
        rows[g] = (rows[g] * scale) * down
        eyes.append(jnp.where(lane == sub + SUB * g, 1.0, 0.0).astype(jnp.float32))
    out_u, out_x = [], []
    for g in range(groups):
        base = SUB * g
        own = rows[g]
        own_x = eyes[g]
        a = {}
        for j in range(SUB):
            column = spread(own[:, base + j : base + j + 1])
            for i in range(j + 1):
                a[i, j] = spread(column[i : i + 1, :])
        near = None
        if g + 1 < groups:
            near = [spread(rows[g + 1][:, base + j : base + j + 1]) for j in range(SUB)]
        u = [spread(own[i : i + 1, :]) for i in range(SUB)]
        x = [spread(own_x[i : i + 1, :]) for i in range(SUB)]
        r = [None] * SUB
        l = {}
        for k in range(0, SUB, 2):
            p, q, t = a[k, k], a[k, k + 1], a[k + 1, k + 1]
            r[k] = lax.rsqrt(p)
            root = lax.rsqrt(p * t - q * q)
            both = r[k] * root
            r[k + 1] = (p * r[k]) * root
            l[k, k + 1] = q * r[k]
            for j in range(k + 2, SUB):
                l[k, j] = a[k, j] * r[k]
                l[k + 1, j] = (p * a[k + 1, j] - q * a[k, j]) * both
            for i in range(k + 2, SUB):
                for j in range(i, SUB):
                    a[i, j] = (a[i, j] - l[k, i] * l[k, j]) - l[k + 1, i] * l[k + 1, j]
            for m in (k, k + 1):
                u[m] = u[m] * r[m]
                x[m] = x[m] * r[m]
                if near is not None:
                    near[m] = near[m] * r[m]
                for i in range(m + 1, SUB):
                    u[i] = u[i] - l[m, i] * u[m]
                    x[i] = x[i] - l[m, i] * x[m]
                    if near is not None:
                        near[i] = near[i] - l[m, i] * near[m]
        final_u, final_x = u[0], x[0]
        for i in range(1, SUB):
            final_u = jnp.where(sub == i, u[i], final_u)
            final_x = jnp.where(sub == i, x[i], final_x)
        out_u.append(jnp.where(lane >= sub + base, final_u * unscale, 0.0))
        out_x.append(final_x * scale)
        if near is not None:
            nxt, nxt_x = rows[g + 1], eyes[g + 1]
            for k in range(SUB):
                nxt = nxt - near[k] * u[k]
                nxt_x = nxt_x - near[k] * x[k]
        if g + 2 < groups:
            v, vx = list(u), list(x)
            for i in reversed(range(SUB)):
                for j in range(i + 1, SUB):
                    v[i] = v[i] - l[i, j] * v[j]
                    vx[i] = vx[i] - l[i, j] * vx[j]
                v[i] = v[i] * r[i]
                vx[i] = vx[i] * r[i]
            for h in range(g + 2, groups):
                far, far_x = rows[h], eyes[h]
                for j in range(SUB):
                    c = spread(rows[h][:, base + j : base + j + 1])
                    far = far - c * v[j]
                    far_x = far_x - c * vx[j]
                rows[h], eyes[h] = far, far_x
        if near is not None:
            rows[g + 1], eyes[g + 1] = nxt, nxt_x
    return jnp.concatenate(out_u, axis=0), jnp.concatenate(out_x, axis=0)


def finish_blocks(u11, u12, x11, rest, u_ref, x_ref):
    zero = jnp.zeros((HALF, HALF), jnp.float32)
    u22, x22 = factor_half(rest)
    u_ref[:HALF, :HALF] = u11
    u_ref[:HALF, HALF:] = u12
    u_ref[HALF:, :HALF] = zero
    u_ref[HALF:, HALF:] = u22
    x_ref[:HALF, :HALF] = x11
    x_ref[:HALF, HALF:] = zero
    x_ref[HALF:, :HALF] = -mm(x22, t_mm(u12, x11))
    x_ref[HALF:, HALF:] = x22


def factor_blocks(s11, s12, s22, u_ref, x_ref):
    u11, x11 = factor_half(s11)
    u12 = mm(x11, s12)
    finish_blocks(u11, u12, x11, s22 - t_mm(u12, u12), u_ref, x_ref)


def tile_from(ref, start, stride):
    return jnp.concatenate(
        [ref[pl.ds(start, NB, stride=stride), :], ref[pl.ds(start + 1, NB, stride=stride), :]], axis=1
    )


def corner_kernel(loc_cols, own, corner, held, sem):
    stride = 2 * loc_cols
    copy = pltpu.make_async_copy(own.at[pl.ds(0, NB * stride), :], held, sem)
    copy.start()
    copy.wait()
    corner[...] = tile_from(held, 0, stride)


def pack_kernel(loc_rows, loc_cols, own, top_a, top_b, *left):
    stride = 2 * loc_cols
    for a in range(1, loc_rows):
        left[a - 1][...] = tile_from(own, a * NB * stride, stride)
    half = HALF * stride
    top_a[...] = own[:half, :]
    top_b[...] = own[half : 2 * half, :]


def first_kernel(pos, mine, other, u_ref, x_ref):
    s = jnp.where(pos[0] % 2 == 0, mine[...], other[...])
    factor_blocks(s[:HALF, :HALF], s[:HALF, HALF:], s[HALF:, HALF:], u_ref, x_ref)


def second_kernel(pos, x0, mine0, mine1, other0, other1, u_ref, x_ref, w_ref):
    even = pos[0] % 2 == 0
    u01 = mm(x0[...], jnp.where(even, mine1[...], other1[...]))
    s = jnp.where(even, other0[...], mine1[...]) - t_mm(u01, u01)
    factor_blocks(s[:HALF, :HALF], s[:HALF, HALF:], s[HALF:, HALF:], u_ref, x_ref)
    w_ref[...] = -mm(x_ref[...], t_mm(u01, x0[...]))


def last_kernel(
    loc_rows, loc_cols, pos, own, mine_a, mine_b, other_a, other_b, u0, x0, u1, x1, w, *rest
):
    left, right = rest[:loc_rows], rest[loc_rows : 2 * loc_rows]
    out, prows = rest[2 * loc_rows :]
    stride = 2 * loc_cols
    even = pos[0] % 2 == 0
    even_col = pos[1] % 2 == 0
    for a in range(loc_rows):
        l, r = left[a][...], right[a][...]
        b0, b1 = jnp.where(even_col, l, r), jnp.where(even_col, r, l)
        prows[2 * a] = mm_t(b0, x0[...], HIGH)
        prows[2 * a + 1] = mm_t(b0, w[...], HIGH) + mm_t(b1, x1[...], HIGH)

    def top_tile(a, b, start):
        halves = [
            jnp.concatenate(
                [ref[pl.ds(start + k, HALF, stride=stride), :] for k in (0, 1)], axis=1
            )
            for ref in (a, b)
        ]
        return jnp.concatenate(halves, axis=0)

    for b in range(loc_cols):
        tile_col = pos[1] + b * pos[3]
        e, o = top_tile(mine_a, mine_b, 2 * b), top_tile(other_a, other_b, 2 * b)
        d0, d1 = jnp.where(even, e, o), jnp.where(even, o, e)
        q0 = mm(x0[...], d0, HIGH)
        q1 = mm(w[...], d0, HIGH) + mm(x1[...], d1, HIGH)
        for a in range(loc_rows):
            tile_row = pos[0] + a * pos[2]
            start = a * NB * stride + 2 * b

            def put(value, start=start):
                out[pl.ds(start, NB, stride=stride), :] = value[:, :HALF]
                out[pl.ds(start + 1, NB, stride=stride), :] = value[:, HALF:]

            @pl.when(tile_row < tile_col)
            def _():
                put(jnp.zeros((NB, NB), jnp.float32))

            @pl.when((tile_row >= tile_col) & (tile_col >= 2))
            def _():
                put(
                    tile_from(own, start, stride)
                    - (mm(prows[2 * a], q0, HIGH) + mm(prows[2 * a + 1], q1, HIGH))
                )

            if b == 0:

                @pl.when((tile_row > 0) & (tile_col == 0))
                def _():
                    put(prows[2 * a])

                @pl.when((tile_row > 1) & (tile_col == 1))
                def _():
                    put(prows[2 * a + 1])

                if a == 0:

                    @pl.when((tile_row == 0) & (tile_col == 0))
                    def _():
                        put(u0[...].T)

                    @pl.when((tile_row == 1) & (tile_col == 1))
                    def _():
                        put(u1[...].T)


VMEM = pl.BlockSpec(memory_space=pltpu.VMEM)
SMEM = pl.BlockSpec(memory_space=pltpu.SMEM)


def shape(*dims):
    return jax.ShapeDtypeStruct(dims, jnp.float32)


def call(kernel, out_shape, flops, *args, smem=0, vmem=16, scratch=()):
    return pl.pallas_call(
        kernel,
        out_shape=out_shape,
        in_specs=[SMEM] * smem + [VMEM] * (len(args) - smem),
        out_specs=jax.tree.map(lambda _: VMEM, out_shape),
        scratch_shapes=list(scratch),
        compiler_params=pltpu.CompilerParams(vmem_limit_bytes=vmem * 2**20),
        cost_estimate=pl.CostEstimate(flops=flops, bytes_accessed=2**22, transcendentals=0),
    )(*args)


def on_device(n_row, n_col, trailing_in):
    row = lax.axis_index("row")
    col = lax.axis_index("col")
    loc_rows, _, _, loc_cols, _, _ = trailing_in.shape
    stride = 2 * loc_cols
    chips = n_row // 2
    chip = row // 2
    own = trailing_in.reshape(loc_rows * NB * stride, HALF)
    pos = jnp.stack([row, col, jnp.int32(n_row), jnp.int32(n_col)]).astype(jnp.int32)
    row_bits = [1 << k for k in range(1, (n_row - 1).bit_length())]
    col_bits = [1 << k for k in range(1, (n_col - 1).bit_length())][::-1]
    after = lax.optimization_barrier

    def swap(value, axis, bits):
        size = n_row if axis == "row" else n_col
        return lax.ppermute(value, axis, [(i, i ^ bits) for i in range(size)])

    def pick(index, values):
        out = values[0]
        for k, value in enumerate(values[1:], 1):
            out = jnp.where(index == k, value, out)
        return out

    def settle(value, axis, bit, got):
        return jnp.where((row if axis == "row" else col) & bit != 0, got, value)

    half = HALF * stride
    corner = pl.pallas_call(
        functools.partial(corner_kernel, loc_cols),
        out_shape=shape(NB, NB),
        in_specs=[pl.BlockSpec(memory_space=pl.ANY)],
        out_specs=VMEM,
        scratch_shapes=[pltpu.VMEM((NB * stride, HALF), jnp.float32), pltpu.SemaphoreType.DMA],
        compiler_params=pltpu.CompilerParams(vmem_limit_bytes=62 * 2**20),
    )(own)
    top_a, top_b, *left = call(
        functools.partial(pack_kernel, loc_rows, loc_cols),
        [shape(half, HALF), shape(half, HALF)] + [shape(NB, NB)] * (loc_rows - 1),
        10**8,
        own,
    )
    left = [corner] + left

    size = NB // chips
    pieces = [left[0][k * size : (k + 1) * size] for k in range(chips)]
    got = [swap(pieces[k], "row", 2 * k) for k in range(1, chips)]
    top_a, top_b, got = after((top_a, top_b, got))
    got_a, got_b = swap(top_a, "row", row_bits[0]), swap(top_b, "row", row_bits[-1])
    piece = pick(chip, [pieces[0]] + got)
    along = [piece] + [swap(piece, "col", k) for k in range(1, n_col)]
    got_a, got_b, along = after((got_a, got_b, along))
    pair = jnp.concatenate([pick(col, along), pick(col ^ 1, along)], axis=0)
    left[0], pair = after((left[0], pair))
    got_left = [swap(left[0], "col", col_bits[0])]
    got = [pair] + [swap(pair, "row", 2 * k) for k in range(1, chips)]
    lead = [
        jnp.concatenate(
            [pick(chip ^ k, got)[j * size : (j + 1) * size] for k in range(chips)], axis=0
        )
        for j in (0, 1)
    ]
    lead_other = swap(jnp.where(row % 2 == 0, lead[0], lead[1]), "row", 1)

    def columns(a):
        value = settle(left[a], "col", col_bits[0], got_left[a])
        for bit in col_bits[1:]:
            value = settle(value, "col", bit, swap(value, "col", bit))
        return value, swap(value, "col", 1)

    top_a, top_b, left[1:], lead[0] = after((top_a, top_b, left[1:], lead[0]))
    top_a = settle(top_a, "row", row_bits[0], got_a)
    top_b = settle(top_b, "row", row_bits[-1], got_b)
    for first, second in zip(row_bits[1:-1], row_bits[-2:0:-1]):
        top_a = settle(top_a, "row", first, swap(top_a, "row", first))
        top_b = settle(top_b, "row", second, swap(top_b, "row", second))
    got_a, got_b = swap(top_a, "row", row_bits[-1]), swap(top_b, "row", row_bits[0])
    got_left += [swap(left[a], "col", col_bits[0]) for a in range(1, loc_rows)]
    lead_other, got_left[0] = after((lead_other, got_left[0]))
    u0, x0 = call(first_kernel, [shape(NB, NB)] * 2, 10**10, pos, lead[0], lead_other, smem=1)

    got_a, got_b, got_left, lead[1], x0 = after((got_a, got_b, got_left, lead[1], x0))
    lead_next = swap(lead[1], "row", 1)
    both = [columns(a) for a in range(loc_rows)]
    left, right = [b[0] for b in both], [b[1] for b in both]
    top_a = settle(top_a, "row", row_bits[-1], got_a)
    top_b = settle(top_b, "row", row_bits[0], got_b)
    other_a, other_b = swap(top_a, "row", 1), swap(top_b, "row", 1)
    u1, x1, w = call(
        second_kernel,
        [shape(NB, NB)] * 3,
        10**10,
        pos, x0, lead[0], lead[1], lead_other, lead_next,
        smem=1,
    )
    right, other_a, other_b, x1 = after((right, other_a, other_b, x1))
    out = call(
        functools.partial(last_kernel, loc_rows, loc_cols),
        shape(*own.shape),
        10**7,
        pos, own, top_a, top_b, other_a, other_b, u0, x0, u1, x1, w, *left, *right,
        smem=1,
        vmem=24,
        scratch=[pltpu.VMEM((2 * loc_rows, NB, NB), jnp.float32)],
    )
    return out.reshape(trailing_in.shape)


def solution(mesh):
    return jax.shard_map(
        functools.partial(on_device, mesh.shape["row"], mesh.shape["col"]),
        mesh=mesh,
        in_specs=(P(None, "row", None, None, "col", None),),
        out_specs=P(None, "row", None, None, "col", None),
        check_vma=False,
    )
```

```python
import functools

import jax
import jax.numpy as jnp
from jax import lax
from jax.experimental import pallas as pl
from jax.experimental.pallas import tpu as pltpu
from jax.sharding import PartitionSpec as P

NB = 256
HALF = 128
SUB = 8
HIGHEST = lax.Precision.HIGHEST
HIGH = lax.Precision.HIGH


def mm(a, b, precision=HIGHEST):
    return lax.dot_general(
        a, b, (((1,), (0,)), ((), ())), precision=precision, preferred_element_type=jnp.float32
    )


def mm_t(a, b, precision=HIGHEST):
    return lax.dot_general(
        a, b, (((1,), (1,)), ((), ())), precision=precision, preferred_element_type=jnp.float32
    )


def t_mm(a, b, precision=HIGHEST):
    return lax.dot_general(
        a, b, (((0,), (0,)), ((), ())), precision=precision, preferred_element_type=jnp.float32
    )


def spread(x):
    return jnp.broadcast_to(x, (SUB, HALF))


def factor_half(s):
    groups = HALF // SUB
    lane = lax.broadcasted_iota(jnp.int32, (SUB, HALF), 1)
    sub = lax.broadcasted_iota(jnp.int32, (SUB, HALF), 0)
    rows = [s[SUB * g : SUB * (g + 1), :] for g in range(groups)]
    own_diagonal = [jnp.where(lane == sub + SUB * g, rows[g], 0.0) for g in range(groups)]
    diagonal = spread(jnp.sum(sum(own_diagonal), axis=0, keepdims=True))
    scale = lax.rsqrt(diagonal)
    unscale = diagonal * scale
    eyes = []
    for g in range(groups):
        down = spread(lax.rsqrt(jnp.sum(own_diagonal[g], axis=1, keepdims=True)))
        rows[g] = (rows[g] * scale) * down
        eyes.append(jnp.where(lane == sub + SUB * g, 1.0, 0.0).astype(jnp.float32))
    out_u, out_x = [], []
    for g in range(groups):
        base = SUB * g
        own = rows[g]
        own_x = eyes[g]
        a = {}
        for j in range(SUB):
            column = spread(own[:, base + j : base + j + 1])
            for i in range(j + 1):
                a[i, j] = spread(column[i : i + 1, :])
        near = None
        if g + 1 < groups:
            near = [spread(rows[g + 1][:, base + j : base + j + 1]) for j in range(SUB)]
        u = [spread(own[i : i + 1, :]) for i in range(SUB)]
        x = [spread(own_x[i : i + 1, :]) for i in range(SUB)]
        r = [None] * SUB
        l = {}
        for k in range(0, SUB, 2):
            p, q, t = a[k, k], a[k, k + 1], a[k + 1, k + 1]
            r[k] = lax.rsqrt(p)
            root = lax.rsqrt(p * t - q * q)
            both = r[k] * root
            r[k + 1] = (p * r[k]) * root
            l[k, k + 1] = q * r[k]
            for j in range(k + 2, SUB):
                l[k, j] = a[k, j] * r[k]
                l[k + 1, j] = (p * a[k + 1, j] - q * a[k, j]) * both
            for i in range(k + 2, SUB):
                for j in range(i, SUB):
                    a[i, j] = (a[i, j] - l[k, i] * l[k, j]) - l[k + 1, i] * l[k + 1, j]
            for m in (k, k + 1):
                u[m] = u[m] * r[m]
                x[m] = x[m] * r[m]
                if near is not None:
                    near[m] = near[m] * r[m]
                for i in range(m + 1, SUB):
                    u[i] = u[i] - l[m, i] * u[m]
                    x[i] = x[i] - l[m, i] * x[m]
                    if near is not None:
                        near[i] = near[i] - l[m, i] * near[m]
        final_u, final_x = u[0], x[0]
        for i in range(1, SUB):
            final_u = jnp.where(sub == i, u[i], final_u)
            final_x = jnp.where(sub == i, x[i], final_x)
        out_u.append(jnp.where(lane >= sub + base, final_u * unscale, 0.0))
        out_x.append(final_x * scale)
        if near is not None:
            nxt, nxt_x = rows[g + 1], eyes[g + 1]
            for k in range(SUB):
                nxt = nxt - near[k] * u[k]
                nxt_x = nxt_x - near[k] * x[k]
        if g + 2 < groups:
            v, vx = list(u), list(x)
            for i in reversed(range(SUB)):
                for j in range(i + 1, SUB):
                    v[i] = v[i] - l[i, j] * v[j]
                    vx[i] = vx[i] - l[i, j] * vx[j]
                v[i] = v[i] * r[i]
                vx[i] = vx[i] * r[i]
            for h in range(g + 2, groups):
                far, far_x = rows[h], eyes[h]
                for j in range(SUB):
                    c = spread(rows[h][:, base + j : base + j + 1])
                    far = far - c * v[j]
                    far_x = far_x - c * vx[j]
                rows[h], eyes[h] = far, far_x
        if near is not None:
            rows[g + 1], eyes[g + 1] = nxt, nxt_x
    return jnp.concatenate(out_u, axis=0), jnp.concatenate(out_x, axis=0)


def finish_blocks(u11, u12, x11, rest, u_ref, x_ref):
    zero = jnp.zeros((HALF, HALF), jnp.float32)
    u22, x22 = factor_half(rest)
    u_ref[:HALF, :HALF] = u11
    u_ref[:HALF, HALF:] = u12
    u_ref[HALF:, :HALF] = zero
    u_ref[HALF:, HALF:] = u22
    x_ref[:HALF, :HALF] = x11
    x_ref[:HALF, HALF:] = zero
    x_ref[HALF:, :HALF] = -mm(x22, t_mm(u12, x11))
    x_ref[HALF:, HALF:] = x22


def factor_blocks(s11, s12, s22, u_ref, x_ref):
    u11, x11 = factor_half(s11)
    u12 = mm(x11, s12)
    finish_blocks(u11, u12, x11, s22 - t_mm(u12, u12), u_ref, x_ref)


def tile_from(ref, start, stride):
    return jnp.concatenate(
        [ref[pl.ds(start, NB, stride=stride), :], ref[pl.ds(start + 1, NB, stride=stride), :]], axis=1
    )


def pack_kernel(loc_rows, loc_cols, own, top_a, top_b, *left):
    stride = 2 * loc_cols
    for a in range(loc_rows):
        left[a][...] = tile_from(own, a * NB * stride, stride)
    half = HALF * stride
    top_a[...] = own[:half, :]
    top_b[...] = own[half : 2 * half, :]


def first_kernel(pos, mine, other, u_ref, x_ref):
    s = jnp.where(pos[0] % 2 == 0, mine[...], other[...])
    factor_blocks(s[:HALF, :HALF], s[:HALF, HALF:], s[HALF:, HALF:], u_ref, x_ref)


def second_kernel(pos, x0, mine0, mine1, other0, other1, u_ref, x_ref, w_ref):
    even = pos[0] % 2 == 0
    u01 = mm(x0[...], jnp.where(even, mine1[...], other1[...]))
    s = jnp.where(even, other0[...], mine1[...]) - t_mm(u01, u01)
    factor_blocks(s[:HALF, :HALF], s[:HALF, HALF:], s[HALF:, HALF:], u_ref, x_ref)
    w_ref[...] = -mm(x_ref[...], t_mm(u01, x0[...]))


def last_kernel(
    loc_rows, loc_cols, pos, own, mine_a, mine_b, other_a, other_b, u0, x0, u1, x1, w, *rest
):
    left, right = rest[:loc_rows], rest[loc_rows : 2 * loc_rows]
    out, prows = rest[2 * loc_rows :]
    stride = 2 * loc_cols
    even = pos[0] % 2 == 0
    even_col = pos[1] % 2 == 0
    for a in range(loc_rows):
        l, r = left[a][...], right[a][...]
        b0, b1 = jnp.where(even_col, l, r), jnp.where(even_col, r, l)
        prows[2 * a] = mm_t(b0, x0[...], HIGH)
        prows[2 * a + 1] = mm_t(b0, w[...], HIGH) + mm_t(b1, x1[...], HIGH)

    def top_tile(a, b, start):
        halves = [
            jnp.concatenate(
                [ref[pl.ds(start + k, HALF, stride=stride), :] for k in (0, 1)], axis=1
            )
            for ref in (a, b)
        ]
        return jnp.concatenate(halves, axis=0)

    for b in range(loc_cols):
        tile_col = pos[1] + b * pos[3]
        e, o = top_tile(mine_a, mine_b, 2 * b), top_tile(other_a, other_b, 2 * b)
        d0, d1 = jnp.where(even, e, o), jnp.where(even, o, e)
        q0 = mm(x0[...], d0, HIGH)
        q1 = mm(w[...], d0, HIGH) + mm(x1[...], d1, HIGH)
        for a in range(loc_rows):
            tile_row = pos[0] + a * pos[2]
            start = a * NB * stride + 2 * b

            def put(value, start=start):
                out[pl.ds(start, NB, stride=stride), :] = value[:, :HALF]
                out[pl.ds(start + 1, NB, stride=stride), :] = value[:, HALF:]

            @pl.when(tile_row < tile_col)
            def _():
                put(jnp.zeros((NB, NB), jnp.float32))

            @pl.when((tile_row >= tile_col) & (tile_col >= 2))
            def _():
                put(
                    tile_from(own, start, stride)
                    - (mm(prows[2 * a], q0, HIGH) + mm(prows[2 * a + 1], q1, HIGH))
                )

            if b == 0:

                @pl.when((tile_row > 0) & (tile_col == 0))
                def _():
                    put(prows[2 * a])

                @pl.when((tile_row > 1) & (tile_col == 1))
                def _():
                    put(prows[2 * a + 1])

                if a == 0:

                    @pl.when((tile_row == 0) & (tile_col == 0))
                    def _():
                        put(u0[...].T)

                    @pl.when((tile_row == 1) & (tile_col == 1))
                    def _():
                        put(u1[...].T)


VMEM = pl.BlockSpec(memory_space=pltpu.VMEM)
SMEM = pl.BlockSpec(memory_space=pltpu.SMEM)


def shape(*dims):
    return jax.ShapeDtypeStruct(dims, jnp.float32)


def call(kernel, out_shape, flops, *args, smem=0, vmem=16, scratch=()):
    return pl.pallas_call(
        kernel,
        out_shape=out_shape,
        in_specs=[SMEM] * smem + [VMEM] * (len(args) - smem),
        out_specs=jax.tree.map(lambda _: VMEM, out_shape),
        scratch_shapes=list(scratch),
        compiler_params=pltpu.CompilerParams(vmem_limit_bytes=vmem * 2**20),
        cost_estimate=pl.CostEstimate(flops=flops, bytes_accessed=2**22, transcendentals=0),
    )(*args)


def on_device(n_row, n_col, trailing_in):
    row = lax.axis_index("row")
    col = lax.axis_index("col")
    loc_rows, _, _, loc_cols, _, _ = trailing_in.shape
    stride = 2 * loc_cols
    chips = n_row // 2
    chip = row // 2
    own = trailing_in.reshape(loc_rows * NB * stride, HALF)
    pos = jnp.stack([row, col, jnp.int32(n_row), jnp.int32(n_col)]).astype(jnp.int32)
    row_bits = [1 << k for k in range(1, (n_row - 1).bit_length())]
    col_bits = [1 << k for k in range(1, (n_col - 1).bit_length())][::-1]
    after = lax.optimization_barrier

    def swap(value, axis, bits):
        size = n_row if axis == "row" else n_col
        return lax.ppermute(value, axis, [(i, i ^ bits) for i in range(size)])

    def pick(index, values):
        out = values[0]
        for k, value in enumerate(values[1:], 1):
            out = jnp.where(index == k, value, out)
        return out

    def settle(value, axis, bit, got):
        return jnp.where((row if axis == "row" else col) & bit != 0, got, value)

    half = HALF * stride
    top_a, top_b, *left = call(
        functools.partial(pack_kernel, loc_rows, loc_cols),
        [shape(half, HALF), shape(half, HALF)] + [shape(NB, NB)] * loc_rows,
        10**8,
        own,
    )

    size = NB // chips
    pieces = [left[0][k * size : (k + 1) * size] for k in range(chips)]
    got = [swap(pieces[k], "row", 2 * k) for k in range(1, chips)]
    top_a, top_b, got = after((top_a, top_b, got))
    got_a, got_b = swap(top_a, "row", row_bits[0]), swap(top_b, "row", row_bits[-1])
    piece = pick(chip, [pieces[0]] + got)
    along = [piece] + [swap(piece, "col", k) for k in range(1, n_col)]
    got_a, got_b, along = after((got_a, got_b, along))
    pair = jnp.concatenate([pick(col, along), pick(col ^ 1, along)], axis=0)
    left, pair = after((left, pair))
    got_left = [swap(value, "col", col_bits[0]) for value in left]
    got = [pair] + [swap(pair, "row", 2 * k) for k in range(1, chips)]
    lead = [
        jnp.concatenate(
            [pick(chip ^ k, got)[j * size : (j + 1) * size] for k in range(chips)], axis=0
        )
        for j in (0, 1)
    ]
    lead_other = swap(jnp.where(row % 2 == 0, lead[0], lead[1]), "row", 1)

    def columns(a):
        value = settle(left[a], "col", col_bits[0], got_left[a])
        for bit in col_bits[1:]:
            value = settle(value, "col", bit, swap(value, "col", bit))
        return value, swap(value, "col", 1)

    top_a, top_b, lead[0] = after((top_a, top_b, lead[0]))
    top_a = settle(top_a, "row", row_bits[0], got_a)
    top_b = settle(top_b, "row", row_bits[-1], got_b)
    for first, second in zip(row_bits[1:-1], row_bits[-2:0:-1]):
        top_a = settle(top_a, "row", first, swap(top_a, "row", first))
        top_b = settle(top_b, "row", second, swap(top_b, "row", second))
    got_a, got_b = swap(top_a, "row", row_bits[-1]), swap(top_b, "row", row_bits[0])
    u0, x0 = call(first_kernel, [shape(NB, NB)] * 2, 10**10, pos, lead[0], lead_other, smem=1)

    got_a, got_b, got_left, lead[1], x0 = after((got_a, got_b, got_left, lead[1], x0))
    lead_next = swap(lead[1], "row", 1)
    both = [columns(a) for a in range(loc_rows)]
    left, right = [b[0] for b in both], [b[1] for b in both]
    top_a = settle(top_a, "row", row_bits[-1], got_a)
    top_b = settle(top_b, "row", row_bits[0], got_b)
    other_a, other_b = swap(top_a, "row", 1), swap(top_b, "row", 1)
    u1, x1, w = call(
        second_kernel,
        [shape(NB, NB)] * 3,
        10**10,
        pos, x0, lead[0], lead[1], lead_other, lead_next,
        smem=1,
    )
    right, other_a, other_b, x1 = after((right, other_a, other_b, x1))
    out = call(
        functools.partial(last_kernel, loc_rows, loc_cols),
        shape(*own.shape),
        10**7,
        pos, own, top_a, top_b, other_a, other_b, u0, x0, u1, x1, w, *left, *right,
        smem=1,
        vmem=24,
        scratch=[pltpu.VMEM((2 * loc_rows, NB, NB), jnp.float32)],
    )
    return out.reshape(trailing_in.shape)


def solution(mesh):
    return jax.shard_map(
        functools.partial(on_device, mesh.shape["row"], mesh.shape["col"]),
        mesh=mesh,
        in_specs=(P(None, "row", None, None, "col", None),),
        out_specs=P(None, "row", None, None, "col", None),
        check_vma=False,
    )
```

```python
import functools

import jax
import jax.numpy as jnp
from jax import lax
from jax.experimental import pallas as pl
from jax.experimental.pallas import tpu as pltpu
from jax.sharding import PartitionSpec as P

NB = 256
HALF = 128
SUB = 8
HIGHEST = lax.Precision.HIGHEST
HIGH = lax.Precision.HIGH


def mm(a, b, precision=HIGHEST):
    return lax.dot_general(
        a, b, (((1,), (0,)), ((), ())), precision=precision, preferred_element_type=jnp.float32
    )


def mm_t(a, b, precision=HIGHEST):
    return lax.dot_general(
        a, b, (((1,), (1,)), ((), ())), precision=precision, preferred_element_type=jnp.float32
    )


def t_mm(a, b, precision=HIGHEST):
    return lax.dot_general(
        a, b, (((0,), (0,)), ((), ())), precision=precision, preferred_element_type=jnp.float32
    )


def spread(x):
    return jnp.broadcast_to(x, (SUB, HALF))


def factor_half(s):
    groups = HALF // SUB
    lane = lax.broadcasted_iota(jnp.int32, (SUB, HALF), 1)
    sub = lax.broadcasted_iota(jnp.int32, (SUB, HALF), 0)
    rows = [s[SUB * g : SUB * (g + 1), :] for g in range(groups)]
    own_diagonal = [jnp.where(lane == sub + SUB * g, rows[g], 0.0) for g in range(groups)]
    diagonal = spread(jnp.sum(sum(own_diagonal), axis=0, keepdims=True))
    scale = lax.rsqrt(diagonal)
    unscale = diagonal * scale
    eyes = []
    for g in range(groups):
        down = spread(lax.rsqrt(jnp.sum(own_diagonal[g], axis=1, keepdims=True)))
        rows[g] = (rows[g] * scale) * down
        eyes.append(jnp.where(lane == sub + SUB * g, 1.0, 0.0).astype(jnp.float32))
    out_u, out_x = [], []
    for g in range(groups):
        base = SUB * g
        own = rows[g]
        own_x = eyes[g]
        a = {}
        for j in range(SUB):
            column = spread(own[:, base + j : base + j + 1])
            for i in range(j + 1):
                a[i, j] = spread(column[i : i + 1, :])
        near = None
        if g + 1 < groups:
            near = [spread(rows[g + 1][:, base + j : base + j + 1]) for j in range(SUB)]
        u = [spread(own[i : i + 1, :]) for i in range(SUB)]
        x = [spread(own_x[i : i + 1, :]) for i in range(SUB)]
        r = [None] * SUB
        l = {}
        for k in range(0, SUB, 2):
            p, q, t = a[k, k], a[k, k + 1], a[k + 1, k + 1]
            r[k] = lax.rsqrt(p)
            root = lax.rsqrt(p * t - q * q)
            both = r[k] * root
            r[k + 1] = (p * r[k]) * root
            l[k, k + 1] = q * r[k]
            for j in range(k + 2, SUB):
                l[k, j] = a[k, j] * r[k]
                l[k + 1, j] = (p * a[k + 1, j] - q * a[k, j]) * both
            for i in range(k + 2, SUB):
                for j in range(i, SUB):
                    a[i, j] = (a[i, j] - l[k, i] * l[k, j]) - l[k + 1, i] * l[k + 1, j]
            for m in (k, k + 1):
                u[m] = u[m] * r[m]
                x[m] = x[m] * r[m]
                if near is not None:
                    near[m] = near[m] * r[m]
                for i in range(m + 1, SUB):
                    u[i] = u[i] - l[m, i] * u[m]
                    x[i] = x[i] - l[m, i] * x[m]
                    if near is not None:
                        near[i] = near[i] - l[m, i] * near[m]
        final_u, final_x = u[0], x[0]
        for i in range(1, SUB):
            final_u = jnp.where(sub == i, u[i], final_u)
            final_x = jnp.where(sub == i, x[i], final_x)
        out_u.append(jnp.where(lane >= sub + base, final_u * unscale, 0.0))
        out_x.append(final_x * scale)
        if near is not None:
            nxt, nxt_x = rows[g + 1], eyes[g + 1]
            for k in range(SUB):
                nxt = nxt - near[k] * u[k]
                nxt_x = nxt_x - near[k] * x[k]
        if g + 2 < groups:
            v, vx = list(u), list(x)
            for i in reversed(range(SUB)):
                for j in range(i + 1, SUB):
                    v[i] = v[i] - l[i, j] * v[j]
                    vx[i] = vx[i] - l[i, j] * vx[j]
                v[i] = v[i] * r[i]
                vx[i] = vx[i] * r[i]
            for h in range(g + 2, groups):
                far, far_x = rows[h], eyes[h]
                for j in range(SUB):
                    c = spread(rows[h][:, base + j : base + j + 1])
                    far = far - c * v[j]
                    far_x = far_x - c * vx[j]
                rows[h], eyes[h] = far, far_x
        if near is not None:
            rows[g + 1], eyes[g + 1] = nxt, nxt_x
    return jnp.concatenate(out_u, axis=0), jnp.concatenate(out_x, axis=0)


def finish_blocks(u11, u12, x11, rest, u_ref, x_ref):
    zero = jnp.zeros((HALF, HALF), jnp.float32)
    u22, x22 = factor_half(rest)
    u_ref[:HALF, :HALF] = u11
    u_ref[:HALF, HALF:] = u12
    u_ref[HALF:, :HALF] = zero
    u_ref[HALF:, HALF:] = u22
    x_ref[:HALF, :HALF] = x11
    x_ref[:HALF, HALF:] = zero
    x_ref[HALF:, :HALF] = -mm(x22, t_mm(u12, x11))
    x_ref[HALF:, HALF:] = x22


def factor_blocks(s11, s12, s22, u_ref, x_ref):
    u11, x11 = factor_half(s11)
    u12 = mm(x11, s12)
    finish_blocks(u11, u12, x11, s22 - t_mm(u12, u12), u_ref, x_ref)


def tile_from(ref, start, stride):
    return jnp.concatenate(
        [ref[pl.ds(start, NB, stride=stride), :], ref[pl.ds(start + 1, NB, stride=stride), :]], axis=1
    )


def pack_kernel(loc_rows, loc_cols, own, top_a, top_b, left_a, left_b):
    stride = 2 * loc_cols
    tiles = [tile_from(own, a * NB * stride, stride) for a in range(loc_rows)]
    first = left_a.shape[0]
    both = jnp.concatenate(tiles, axis=0)
    left_a[...] = both[:first, :]
    left_b[...] = both[first:, :]
    half = HALF * stride
    top_a[...] = own[:half, :]
    top_b[...] = own[half : 2 * half, :]


def first_kernel(pos, mine, other, u_ref, x_ref):
    s = jnp.where(pos[0] % 2 == 0, mine[...], other[...])
    factor_blocks(s[:HALF, :HALF], s[:HALF, HALF:], s[HALF:, HALF:], u_ref, x_ref)


def second_kernel(pos, x0, mine0, mine1, other0, other1, u_ref, x_ref, w_ref):
    even = pos[0] % 2 == 0
    u01 = mm(x0[...], jnp.where(even, mine1[...], other1[...]))
    s = jnp.where(even, other0[...], mine1[...]) - t_mm(u01, u01)
    factor_blocks(s[:HALF, :HALF], s[:HALF, HALF:], s[HALF:, HALF:], u_ref, x_ref)
    w_ref[...] = -mm(x_ref[...], t_mm(u01, x0[...]))


def columns_kernel(loc_cols, pos, mine_a, mine_b, other_a, other_b, x0, x1, w, *q):
    stride = 2 * loc_cols
    even = pos[0] % 2 == 0

    def top_tile(a, b, start):
        halves = [
            jnp.concatenate(
                [ref[pl.ds(start + k, HALF, stride=stride), :] for k in (0, 1)], axis=1
            )
            for ref in (a, b)
        ]
        return jnp.concatenate(halves, axis=0)

    for b in range(loc_cols):
        e, o = top_tile(mine_a, mine_b, 2 * b), top_tile(other_a, other_b, 2 * b)
        d0, d1 = jnp.where(even, e, o), jnp.where(even, o, e)
        q[b][...] = mm(x0[...], d0, HIGH)
        q[loc_cols + b][...] = mm(w[...], d0, HIGH) + mm(x1[...], d1, HIGH)


def last_kernel(loc_rows, loc_cols, pos, own, u0, x0, u1, x1, w, *rest):
    left = jnp.concatenate([rest[0][...], rest[1][...]], axis=0)
    right = jnp.concatenate([rest[2][...], rest[3][...]], axis=0)
    q, out = rest[4:-1], rest[-1]
    stride = 2 * loc_cols
    even_col = pos[1] % 2 == 0
    for a in range(loc_rows):
        tile_row = pos[0] + a * pos[2]
        l, r = left[a * NB : (a + 1) * NB, :], right[a * NB : (a + 1) * NB, :]
        b0, b1 = jnp.where(even_col, l, r), jnp.where(even_col, r, l)
        prow0 = mm_t(b0, x0[...], HIGH)
        prow1 = mm_t(b0, w[...], HIGH) + mm_t(b1, x1[...], HIGH)
        for b in range(loc_cols):
            tile_col = pos[1] + b * pos[3]
            start = a * NB * stride + 2 * b

            def put(value, start=start):
                out[pl.ds(start, NB, stride=stride), :] = value[:, :HALF]
                out[pl.ds(start + 1, NB, stride=stride), :] = value[:, HALF:]

            @pl.when(tile_row < tile_col)
            def _():
                put(jnp.zeros((NB, NB), jnp.float32))

            @pl.when((tile_row >= tile_col) & (tile_col >= 2))
            def _():
                put(
                    tile_from(own, start, stride)
                    - (mm(prow0, q[b][...], HIGH) + mm(prow1, q[loc_cols + b][...], HIGH))
                )

            if b == 0:

                @pl.when((tile_row > 0) & (tile_col == 0))
                def _():
                    put(prow0)

                @pl.when((tile_row > 1) & (tile_col == 1))
                def _():
                    put(prow1)

                if a == 0:

                    @pl.when((tile_row == 0) & (tile_col == 0))
                    def _():
                        put(u0[...].T)

                    @pl.when((tile_row == 1) & (tile_col == 1))
                    def _():
                        put(u1[...].T)


VMEM = pl.BlockSpec(memory_space=pltpu.VMEM)
SMEM = pl.BlockSpec(memory_space=pltpu.SMEM)


def shape(*dims):
    return jax.ShapeDtypeStruct(dims, jnp.float32)


def call(kernel, out_shape, flops, *args, smem=0, vmem=16, scratch=()):
    return pl.pallas_call(
        kernel,
        out_shape=out_shape,
        in_specs=[SMEM] * smem + [VMEM] * (len(args) - smem),
        out_specs=jax.tree.map(lambda _: VMEM, out_shape),
        scratch_shapes=list(scratch),
        compiler_params=pltpu.CompilerParams(vmem_limit_bytes=vmem * 2**20),
        cost_estimate=pl.CostEstimate(flops=flops, bytes_accessed=2**22, transcendentals=0),
    )(*args)


def on_device(n_row, n_col, trailing_in):
    row = lax.axis_index("row")
    col = lax.axis_index("col")
    loc_rows, _, _, loc_cols, _, _ = trailing_in.shape
    stride = 2 * loc_cols
    chips = n_row // 2
    chip = row // 2
    own = trailing_in.reshape(loc_rows * NB * stride, HALF)
    pos = jnp.stack([row, col, jnp.int32(n_row), jnp.int32(n_col)]).astype(jnp.int32)
    row_bits = [1 << k for k in range(1, (n_row - 1).bit_length())]
    col_bits = [1 << k for k in range(1, (n_col - 1).bit_length())][::-1]
    after = lax.optimization_barrier

    def swap(value, axis, bits):
        size = n_row if axis == "row" else n_col
        return lax.ppermute(value, axis, [(i, i ^ bits) for i in range(size)])

    def pick(index, values):
        out = values[0]
        for k, value in enumerate(values[1:], 1):
            out = jnp.where(index == k, value, out)
        return out

    def settle(value, axis, bit, got):
        return jnp.where((row if axis == "row" else col) & bit != 0, got, value)

    half = HALF * stride
    first_part = loc_rows * NB * 3 // 4
    top_a, top_b, *left = call(
        functools.partial(pack_kernel, loc_rows, loc_cols),
        [
            shape(half, HALF),
            shape(half, HALF),
            shape(first_part, NB),
            shape(loc_rows * NB - first_part, NB),
        ],
        10**8,
        own,
    )

    size = NB // chips
    pieces = [left[0][k * size : (k + 1) * size] for k in range(chips)]
    got = [swap(pieces[k], "row", 2 * k) for k in range(1, chips)]
    top_a, top_b, got = after((top_a, top_b, got))
    got_a, got_b = swap(top_a, "row", row_bits[0]), swap(top_b, "row", row_bits[-1])
    piece = pick(chip, [pieces[0]] + got)
    along = [piece] + [swap(piece, "col", k) for k in range(1, n_col)]
    got_a, got_b, along = after((got_a, got_b, along))
    pair = jnp.concatenate([pick(col, along), pick(col ^ 1, along)], axis=0)
    left[0], pair = after((left[0], pair))
    got_left = [swap(left[0], "col", col_bits[0])]
    got = [pair] + [swap(pair, "row", 2 * k) for k in range(1, chips)]
    lead = [
        jnp.concatenate(
            [pick(chip ^ k, got)[j * size : (j + 1) * size] for k in range(chips)], axis=0
        )
        for j in (0, 1)
    ]
    lead_other = swap(jnp.where(row % 2 == 0, lead[0], lead[1]), "row", 1)

    def columns(a):
        value = settle(left[a], "col", col_bits[0], got_left[a])
        for bit in col_bits[1:]:
            value = settle(value, "col", bit, swap(value, "col", bit))
        return value, swap(value, "col", 1)

    top_a, top_b, lead[0] = after((top_a, top_b, lead[0]))
    top_a = settle(top_a, "row", row_bits[0], got_a)
    top_b = settle(top_b, "row", row_bits[-1], got_b)
    for first, second in zip(row_bits[1:-1], row_bits[-2:0:-1]):
        top_a = settle(top_a, "row", first, swap(top_a, "row", first))
        top_b = settle(top_b, "row", second, swap(top_b, "row", second))
    got_a, got_b = swap(top_a, "row", row_bits[-1]), swap(top_b, "row", row_bits[0])
    u0, x0 = call(first_kernel, [shape(NB, NB)] * 2, 10**10, pos, lead[0], lead_other, smem=1)

    got_a, got_b, got_left, lead[1], x0 = after((got_a, got_b, got_left, lead[1], x0))
    lead_next = swap(lead[1], "row", 1)
    left[1], x0 = after((left[1], x0))
    got_left.append(swap(left[1], "col", col_bits[0]))
    both = [columns(0)]
    top_a = settle(top_a, "row", row_bits[-1], got_a)
    top_b = settle(top_b, "row", row_bits[0], got_b)
    other_a, other_b = swap(top_a, "row", 1), swap(top_b, "row", 1)
    u1, x1, w = call(
        second_kernel,
        [shape(NB, NB)] * 3,
        10**10,
        pos, x0, lead[0], lead[1], lead_other, lead_next,
        smem=1,
    )
    other_a, other_b, both[0], got_left[1], x1 = after(
        (other_a, other_b, both[0], got_left[1], x1)
    )
    both.append(columns(1))
    q = list(
        call(
            functools.partial(columns_kernel, loc_cols),
            [shape(NB, NB)] * (2 * loc_cols),
            10**9,
            pos, top_a, top_b, other_a, other_b, x0, x1, w,
            smem=1,
        )
    )
    both[1], q[0] = after((both[1], q[0]))
    out = call(
        functools.partial(last_kernel, loc_rows, loc_cols),
        shape(*own.shape),
        10**7,
        pos, own, u0, x0, u1, x1, w, both[0][0], both[1][0], both[0][1], both[1][1], *q,
        smem=1,
        vmem=24,
    )
    return out.reshape(trailing_in.shape)


def solution(mesh):
    return jax.shard_map(
        functools.partial(on_device, mesh.shape["row"], mesh.shape["col"]),
        mesh=mesh,
        in_specs=(P(None, "row", None, None, "col", None),),
        out_specs=P(None, "row", None, None, "col", None),
        check_vma=False,
    )
```

```python
import functools

import jax
import jax.numpy as jnp
from jax import lax
from jax.experimental import pallas as pl
from jax.experimental.pallas import tpu as pltpu
from jax.sharding import PartitionSpec as P

NB = 256
HALF = 128
SUB = 8
HIGHEST = lax.Precision.HIGHEST
HIGH = lax.Precision.HIGH


def mm(a, b, precision=HIGHEST):
    return lax.dot_general(
        a, b, (((1,), (0,)), ((), ())), precision=precision, preferred_element_type=jnp.float32
    )


def mm_t(a, b, precision=HIGHEST):
    return lax.dot_general(
        a, b, (((1,), (1,)), ((), ())), precision=precision, preferred_element_type=jnp.float32
    )


def t_mm(a, b, precision=HIGHEST):
    return lax.dot_general(
        a, b, (((0,), (0,)), ((), ())), precision=precision, preferred_element_type=jnp.float32
    )


def spread(x):
    return jnp.broadcast_to(x, (SUB, HALF))


def factor_half(s):
    groups = HALF // SUB
    lane = lax.broadcasted_iota(jnp.int32, (SUB, HALF), 1)
    sub = lax.broadcasted_iota(jnp.int32, (SUB, HALF), 0)
    rows = [s[SUB * g : SUB * (g + 1), :] for g in range(groups)]
    own_diagonal = [jnp.where(lane == sub + SUB * g, rows[g], 0.0) for g in range(groups)]
    diagonal = spread(jnp.sum(sum(own_diagonal), axis=0, keepdims=True))
    scale = lax.rsqrt(diagonal)
    unscale = diagonal * scale
    eyes = []
    for g in range(groups):
        down = spread(lax.rsqrt(jnp.sum(own_diagonal[g], axis=1, keepdims=True)))
        rows[g] = (rows[g] * scale) * down
        eyes.append(jnp.where(lane == sub + SUB * g, 1.0, 0.0).astype(jnp.float32))
    out_u, out_x = [], []
    for g in range(groups):
        base = SUB * g
        own = rows[g]
        own_x = eyes[g]
        a = {}
        for j in range(SUB):
            column = spread(own[:, base + j : base + j + 1])
            for i in range(j + 1):
                a[i, j] = spread(column[i : i + 1, :])
        near = None
        if g + 1 < groups:
            near = [spread(rows[g + 1][:, base + j : base + j + 1]) for j in range(SUB)]
        u = [spread(own[i : i + 1, :]) for i in range(SUB)]
        x = [spread(own_x[i : i + 1, :]) for i in range(SUB)]
        r = [None] * SUB
        l = {}
        for k in range(0, SUB, 2):
            p, q, t = a[k, k], a[k, k + 1], a[k + 1, k + 1]
            r[k] = lax.rsqrt(p)
            root = lax.rsqrt(p * t - q * q)
            both = r[k] * root
            r[k + 1] = (p * r[k]) * root
            l[k, k + 1] = q * r[k]
            for j in range(k + 2, SUB):
                l[k, j] = a[k, j] * r[k]
                l[k + 1, j] = (p * a[k + 1, j] - q * a[k, j]) * both
            for i in range(k + 2, SUB):
                for j in range(i, SUB):
                    a[i, j] = (a[i, j] - l[k, i] * l[k, j]) - l[k + 1, i] * l[k + 1, j]
            for m in (k, k + 1):
                u[m] = u[m] * r[m]
                x[m] = x[m] * r[m]
                if near is not None:
                    near[m] = near[m] * r[m]
                for i in range(m + 1, SUB):
                    u[i] = u[i] - l[m, i] * u[m]
                    x[i] = x[i] - l[m, i] * x[m]
                    if near is not None:
                        near[i] = near[i] - l[m, i] * near[m]
        final_u, final_x = u[0], x[0]
        for i in range(1, SUB):
            final_u = jnp.where(sub == i, u[i], final_u)
            final_x = jnp.where(sub == i, x[i], final_x)
        out_u.append(jnp.where(lane >= sub + base, final_u * unscale, 0.0))
        out_x.append(final_x * scale)
        if near is not None:
            nxt, nxt_x = rows[g + 1], eyes[g + 1]
            for k in range(SUB):
                nxt = nxt - near[k] * u[k]
                nxt_x = nxt_x - near[k] * x[k]
        if g + 2 < groups:
            v, vx = list(u), list(x)
            for i in reversed(range(SUB)):
                for j in range(i + 1, SUB):
                    v[i] = v[i] - l[i, j] * v[j]
                    vx[i] = vx[i] - l[i, j] * vx[j]
                v[i] = v[i] * r[i]
                vx[i] = vx[i] * r[i]
            for h in range(g + 2, groups):
                far, far_x = rows[h], eyes[h]
                for j in range(SUB):
                    c = spread(rows[h][:, base + j : base + j + 1])
                    far = far - c * v[j]
                    far_x = far_x - c * vx[j]
                rows[h], eyes[h] = far, far_x
        if near is not None:
            rows[g + 1], eyes[g + 1] = nxt, nxt_x
    return jnp.concatenate(out_u, axis=0), jnp.concatenate(out_x, axis=0)


def finish_blocks(u11, u12, x11, rest, u_ref, x_ref):
    zero = jnp.zeros((HALF, HALF), jnp.float32)
    u22, x22 = factor_half(rest)
    u_ref[:HALF, :HALF] = u11
    u_ref[:HALF, HALF:] = u12
    u_ref[HALF:, :HALF] = zero
    u_ref[HALF:, HALF:] = u22
    x_ref[:HALF, :HALF] = x11
    x_ref[:HALF, HALF:] = zero
    x_ref[HALF:, :HALF] = -mm(x22, t_mm(u12, x11))
    x_ref[HALF:, HALF:] = x22


def factor_blocks(s11, s12, s22, u_ref, x_ref):
    u11, x11 = factor_half(s11)
    u12 = mm(x11, s12)
    finish_blocks(u11, u12, x11, s22 - t_mm(u12, u12), u_ref, x_ref)


def tile_from(ref, start, stride):
    return jnp.concatenate(
        [ref[pl.ds(start, NB, stride=stride), :], ref[pl.ds(start + 1, NB, stride=stride), :]], axis=1
    )


def pack_kernel(loc_rows, loc_cols, own, top_a, top_b, *left):
    stride = 2 * loc_cols
    for a in range(loc_rows):
        left[a][...] = tile_from(own, a * NB * stride, stride)
    half = HALF * stride
    top_a[...] = own[:half, :]
    top_b[...] = own[half : 2 * half, :]


def first_kernel(pos, mine, other, u_ref, x_ref):
    s = jnp.where(pos[0] % 2 == 0, mine[...], other[...])
    factor_blocks(s[:HALF, :HALF], s[:HALF, HALF:], s[HALF:, HALF:], u_ref, x_ref)


def second_kernel(pos, x0, mine0, mine1, other0, other1, u_ref, x_ref, w_ref):
    even = pos[0] % 2 == 0
    u01 = mm(x0[...], jnp.where(even, mine1[...], other1[...]))
    s = jnp.where(even, other0[...], mine1[...]) - t_mm(u01, u01)
    factor_blocks(s[:HALF, :HALF], s[:HALF, HALF:], s[HALF:, HALF:], u_ref, x_ref)
    w_ref[...] = -mm(x_ref[...], t_mm(u01, x0[...]))


def store_row(a, loc_cols, pos, prow0, prow1, q0, q1, u0, u1, own, out):
    stride = 2 * loc_cols
    tile_row = pos[0] + a * pos[2]
    for b in range(loc_cols):
        tile_col = pos[1] + b * pos[3]

        def put(value, start=2 * b):
            out[pl.ds(start, NB, stride=stride), :] = value[:, :HALF]
            out[pl.ds(start + 1, NB, stride=stride), :] = value[:, HALF:]

        @pl.when(tile_row < tile_col)
        def _():
            put(jnp.zeros((NB, NB), jnp.float32))

        @pl.when((tile_row >= tile_col) & (tile_col >= 2))
        def _():
            put(
                tile_from(own, 2 * b, stride)
                - (mm(prow0, q0[b][...], HIGH) + mm(prow1, q1[b][...], HIGH))
            )

        if b == 0:

            @pl.when((tile_row > 0) & (tile_col == 0))
            def _():
                put(prow0)

            @pl.when((tile_row > 1) & (tile_col == 1))
            def _():
                put(prow1)

            if a == 0:

                @pl.when((tile_row == 0) & (tile_col == 0))
                def _():
                    put(u0[...].T)

                @pl.when((tile_row == 1) & (tile_col == 1))
                def _():
                    put(u1[...].T)


def panel_row(pos, left, right, x0, x1, w):
    even_col = pos[1] % 2 == 0
    l, r = left[...], right[...]
    b0, b1 = jnp.where(even_col, l, r), jnp.where(even_col, r, l)
    return mm_t(b0, x0[...], HIGH), mm_t(b0, w[...], HIGH) + mm_t(b1, x1[...], HIGH)


def columns_kernel(
    loc_cols, pos, own, left, right, mine_a, mine_b, other_a, other_b, u0, x0, u1, x1, w, out, *q
):
    stride = 2 * loc_cols
    even = pos[0] % 2 == 0

    def top_tile(a, b, start):
        halves = [
            jnp.concatenate(
                [ref[pl.ds(start + k, HALF, stride=stride), :] for k in (0, 1)], axis=1
            )
            for ref in (a, b)
        ]
        return jnp.concatenate(halves, axis=0)

    q0, q1 = q[:loc_cols], q[loc_cols:]
    for b in range(loc_cols):
        e, o = top_tile(mine_a, mine_b, 2 * b), top_tile(other_a, other_b, 2 * b)
        d0, d1 = jnp.where(even, e, o), jnp.where(even, o, e)
        q0[b][...] = mm(x0[...], d0, HIGH)
        q1[b][...] = mm(w[...], d0, HIGH) + mm(x1[...], d1, HIGH)
    prow0, prow1 = panel_row(pos, left, right, x0, x1, w)
    store_row(0, loc_cols, pos, prow0, prow1, q0, q1, u0, u1, own, out)


def later_kernel(a, loc_cols, pos, own, left, right, x0, x1, w, *rest):
    q, out = rest[: 2 * loc_cols], rest[-1]
    prow0, prow1 = panel_row(pos, left, right, x0, x1, w)
    store_row(
        a, loc_cols, pos, prow0, prow1, q[:loc_cols], q[loc_cols:], None, None, own, out
    )


VMEM = pl.BlockSpec(memory_space=pltpu.VMEM)
SMEM = pl.BlockSpec(memory_space=pltpu.SMEM)


def shape(*dims):
    return jax.ShapeDtypeStruct(dims, jnp.float32)


def call(
    kernel, out_shape, flops, *args, smem=0, vmem=16, specs=None, out_specs=None, aliases=None, grid=()
):
    return pl.pallas_call(
        kernel,
        grid=grid,
        out_shape=out_shape,
        in_specs=specs or [SMEM] * smem + [VMEM] * (len(args) - smem),
        out_specs=out_specs or jax.tree.map(lambda _: VMEM, out_shape),
        input_output_aliases=aliases or {},
        compiler_params=pltpu.CompilerParams(vmem_limit_bytes=vmem * 2**20),
        cost_estimate=pl.CostEstimate(flops=flops, bytes_accessed=2**22, transcendentals=0),
    )(*args)


def on_device(n_row, n_col, trailing_in):
    row = lax.axis_index("row")
    col = lax.axis_index("col")
    loc_rows, _, _, loc_cols, _, _ = trailing_in.shape
    stride = 2 * loc_cols
    chips = n_row // 2
    chip = row // 2
    own = trailing_in.reshape(loc_rows * NB * stride, HALF)
    pos = jnp.stack([row, col, jnp.int32(n_row), jnp.int32(n_col)]).astype(jnp.int32)
    row_bits = [1 << k for k in range(1, (n_row - 1).bit_length())]
    col_bits = [1 << k for k in range(1, (n_col - 1).bit_length())][::-1]
    after = lax.optimization_barrier

    def swap(value, axis, bits):
        size = n_row if axis == "row" else n_col
        return lax.ppermute(value, axis, [(i, i ^ bits) for i in range(size)])

    def pick(index, values):
        out = values[0]
        for k, value in enumerate(values[1:], 1):
            out = jnp.where(index == k, value, out)
        return out

    def settle(value, axis, bit, got):
        return jnp.where((row if axis == "row" else col) & bit != 0, got, value)

    half = HALF * stride
    top_a, top_b, *left = call(
        functools.partial(pack_kernel, loc_rows, loc_cols),
        [shape(half, HALF), shape(half, HALF)] + [shape(NB, NB)] * loc_rows,
        10**8,
        own,
    )

    size = NB // chips
    pieces = [left[0][k * size : (k + 1) * size] for k in range(chips)]
    got = [swap(pieces[k], "row", 2 * k) for k in range(1, chips)]
    top_a, top_b, got = after((top_a, top_b, got))
    got_a, got_b = swap(top_a, "row", row_bits[0]), swap(top_b, "row", row_bits[-1])
    piece = pick(chip, [pieces[0]] + got)
    along = [piece] + [swap(piece, "col", k) for k in range(1, n_col)]
    got_a, got_b, along = after((got_a, got_b, along))
    pair = jnp.concatenate([pick(col, along), pick(col ^ 1, along)], axis=0)
    left[0], pair = after((left[0], pair))
    got_left = [swap(left[0], "col", col_bits[0])]
    got = [pair] + [swap(pair, "row", 2 * k) for k in range(1, chips)]
    lead = [
        jnp.concatenate(
            [pick(chip ^ k, got)[j * size : (j + 1) * size] for k in range(chips)], axis=0
        )
        for j in (0, 1)
    ]
    lead_other = swap(jnp.where(row % 2 == 0, lead[0], lead[1]), "row", 1)

    def columns(a):
        value = settle(left[a], "col", col_bits[0], got_left[a])
        for bit in col_bits[1:]:
            value = settle(value, "col", bit, swap(value, "col", bit))
        return value, swap(value, "col", 1)

    top_a, top_b, lead[0] = after((top_a, top_b, lead[0]))
    top_a = settle(top_a, "row", row_bits[0], got_a)
    top_b = settle(top_b, "row", row_bits[-1], got_b)
    for first, second in zip(row_bits[1:-1], row_bits[-2:0:-1]):
        top_a = settle(top_a, "row", first, swap(top_a, "row", first))
        top_b = settle(top_b, "row", second, swap(top_b, "row", second))
    got_a, got_b = swap(top_a, "row", row_bits[-1]), swap(top_b, "row", row_bits[0])
    u0, x0 = call(first_kernel, [shape(NB, NB)] * 2, 10**10, pos, lead[0], lead_other, smem=1)

    got_left, left[1:], lead[1], x0 = after((got_left, left[1:], lead[1], x0))
    lead_next = swap(lead[1], "row", 1)
    got_left += [swap(value, "col", col_bits[0]) for value in left[1:]]
    both = [columns(0)]
    u1, x1, w = call(
        second_kernel,
        [shape(NB, NB)] * 3,
        10**10,
        pos, x0, lead[0], lead[1], lead_other, lead_next,
        smem=1,
    )
    got_a, got_b, got_left[1:], both[0], x1 = after((got_a, got_b, got_left[1:], both[0], x1))
    top_a = settle(top_a, "row", row_bits[-1], got_a)
    top_b = settle(top_b, "row", row_bits[0], got_b)
    other_a, other_b = swap(top_a, "row", 1), swap(top_b, "row", 1)
    both += [columns(a) for a in range(1, loc_rows)]

    def block(a):
        return pl.BlockSpec((NB * stride, HALF), lambda i: (a, 0))

    out, *q = call(
        functools.partial(columns_kernel, loc_cols),
        [shape(*own.shape)] + [shape(NB, NB)] * (2 * loc_cols),
        10**9,
        pos, own, *both[0], top_a, top_b, other_a, other_b, u0, x0, u1, x1, w,
        specs=[SMEM, block(0)] + [VMEM] * 11,
        out_specs=[block(0)] + [VMEM] * (2 * loc_cols),
        grid=(1,),
        vmem=24,
    )
    for a in range(1, loc_rows):
        out = call(
            functools.partial(later_kernel, a, loc_cols),
            shape(*own.shape),
            10**7,
            pos, own, *both[a], x0, x1, w, *q, out,
            specs=[SMEM, block(a)] + [VMEM] * (5 + 2 * loc_cols) + [pl.BlockSpec(memory_space=pl.ANY)],
            out_specs=block(a),
            aliases={7 + 2 * loc_cols: 0},
            grid=(1,),
        )
    return out.reshape(trailing_in.shape)


def solution(mesh):
    return jax.shard_map(
        functools.partial(on_device, mesh.shape["row"], mesh.shape["col"]),
        mesh=mesh,
        in_specs=(P(None, "row", None, None, "col", None),),
        out_specs=P(None, "row", None, None, "col", None),
        check_vma=False,
    )
```

```python
import functools

import jax
import jax.numpy as jnp
from jax import lax
from jax.experimental import pallas as pl
from jax.experimental.pallas import tpu as pltpu
from jax.sharding import PartitionSpec as P

NB = 256
HALF = 128
SUB = 8
HIGHEST = lax.Precision.HIGHEST
HIGH = lax.Precision.HIGH


def mm(a, b, precision=HIGHEST):
    return lax.dot_general(
        a, b, (((1,), (0,)), ((), ())), precision=precision, preferred_element_type=jnp.float32
    )


def mm_t(a, b, precision=HIGHEST):
    return lax.dot_general(
        a, b, (((1,), (1,)), ((), ())), precision=precision, preferred_element_type=jnp.float32
    )


def t_mm(a, b, precision=HIGHEST):
    return lax.dot_general(
        a, b, (((0,), (0,)), ((), ())), precision=precision, preferred_element_type=jnp.float32
    )


def spread(x):
    return jnp.broadcast_to(x, (SUB, HALF))


def factor_half(s):
    groups = HALF // SUB
    lane = lax.broadcasted_iota(jnp.int32, (SUB, HALF), 1)
    sub = lax.broadcasted_iota(jnp.int32, (SUB, HALF), 0)
    rows = [s[SUB * g : SUB * (g + 1), :] for g in range(groups)]
    own_diagonal = [jnp.where(lane == sub + SUB * g, rows[g], 0.0) for g in range(groups)]
    diagonal = spread(jnp.sum(sum(own_diagonal), axis=0, keepdims=True))
    scale = lax.rsqrt(diagonal)
    unscale = diagonal * scale
    eyes = []
    for g in range(groups):
        down = spread(lax.rsqrt(jnp.sum(own_diagonal[g], axis=1, keepdims=True)))
        rows[g] = (rows[g] * scale) * down
        eyes.append(jnp.where(lane == sub + SUB * g, 1.0, 0.0).astype(jnp.float32))
    out_u, out_x = [], []
    for g in range(groups):
        base = SUB * g
        own = rows[g]
        own_x = eyes[g]
        a = {}
        for j in range(SUB):
            column = spread(own[:, base + j : base + j + 1])
            for i in range(j + 1):
                a[i, j] = spread(column[i : i + 1, :])
        near = None
        if g + 1 < groups:
            near = [spread(rows[g + 1][:, base + j : base + j + 1]) for j in range(SUB)]
        u = [spread(own[i : i + 1, :]) for i in range(SUB)]
        x = [spread(own_x[i : i + 1, :]) for i in range(SUB)]
        r = [None] * SUB
        l = {}
        for k in range(0, SUB, 2):
            p, q, t = a[k, k], a[k, k + 1], a[k + 1, k + 1]
            r[k] = lax.rsqrt(p)
            root = lax.rsqrt(p * t - q * q)
            both = r[k] * root
            r[k + 1] = (p * r[k]) * root
            l[k, k + 1] = q * r[k]
            for j in range(k + 2, SUB):
                l[k, j] = a[k, j] * r[k]
                l[k + 1, j] = (p * a[k + 1, j] - q * a[k, j]) * both
            for i in range(k + 2, SUB):
                for j in range(i, SUB):
                    a[i, j] = (a[i, j] - l[k, i] * l[k, j]) - l[k + 1, i] * l[k + 1, j]
            for m in (k, k + 1):
                u[m] = u[m] * r[m]
                x[m] = x[m] * r[m]
                if near is not None:
                    near[m] = near[m] * r[m]
                for i in range(m + 1, SUB):
                    u[i] = u[i] - l[m, i] * u[m]
                    x[i] = x[i] - l[m, i] * x[m]
                    if near is not None:
                        near[i] = near[i] - l[m, i] * near[m]
        final_u, final_x = u[0], x[0]
        for i in range(1, SUB):
            final_u = jnp.where(sub == i, u[i], final_u)
            final_x = jnp.where(sub == i, x[i], final_x)
        out_u.append(jnp.where(lane >= sub + base, final_u * unscale, 0.0))
        out_x.append(final_x * scale)
        if near is not None:
            nxt, nxt_x = rows[g + 1], eyes[g + 1]
            for k in range(SUB):
                nxt = nxt - near[k] * u[k]
                nxt_x = nxt_x - near[k] * x[k]
        if g + 2 < groups:
            v, vx = list(u), list(x)
            for i in reversed(range(SUB)):
                for j in range(i + 1, SUB):
                    v[i] = v[i] - l[i, j] * v[j]
                    vx[i] = vx[i] - l[i, j] * vx[j]
                v[i] = v[i] * r[i]
                vx[i] = vx[i] * r[i]
            for h in range(g + 2, groups):
                far, far_x = rows[h], eyes[h]
                for j in range(SUB):
                    c = spread(rows[h][:, base + j : base + j + 1])
                    far = far - c * v[j]
                    far_x = far_x - c * vx[j]
                rows[h], eyes[h] = far, far_x
        if near is not None:
            rows[g + 1], eyes[g + 1] = nxt, nxt_x
    return jnp.concatenate(out_u, axis=0), jnp.concatenate(out_x, axis=0)


def finish_blocks(u11, u12, x11, rest, u_ref, x_ref):
    zero = jnp.zeros((HALF, HALF), jnp.float32)
    u22, x22 = factor_half(rest)
    u_ref[:HALF, :HALF] = u11
    u_ref[:HALF, HALF:] = u12
    u_ref[HALF:, :HALF] = zero
    u_ref[HALF:, HALF:] = u22
    x_ref[:HALF, :HALF] = x11
    x_ref[:HALF, HALF:] = zero
    x_ref[HALF:, :HALF] = -mm(x22, t_mm(u12, x11))
    x_ref[HALF:, HALF:] = x22


def factor_blocks(s11, s12, s22, u_ref, x_ref):
    u11, x11 = factor_half(s11)
    u12 = mm(x11, s12)
    finish_blocks(u11, u12, x11, s22 - t_mm(u12, u12), u_ref, x_ref)


def tile_from(ref, start, stride):
    return jnp.concatenate(
        [ref[pl.ds(start, NB, stride=stride), :], ref[pl.ds(start + 1, NB, stride=stride), :]], axis=1
    )


def pack_kernel(loc_rows, loc_cols, own, top_a, top_b, *left):
    stride = 2 * loc_cols
    for a in range(loc_rows):
        left[a][...] = tile_from(own, a * NB * stride, stride)
    half = HALF * stride
    top_a[...] = own[:half, :]
    top_b[...] = own[half : 2 * half, :]


def first_kernel(pos, mine, other, u_ref, x_ref):
    s = jnp.where(pos[0] % 2 == 0, mine[...], other[...])
    factor_blocks(s[:HALF, :HALF], s[:HALF, HALF:], s[HALF:, HALF:], u_ref, x_ref)


def second_kernel(pos, x0, mine0, mine1, other0, other1, u_ref, x_ref, w_ref):
    even = pos[0] % 2 == 0
    u01 = mm(x0[...], jnp.where(even, mine1[...], other1[...]))
    s = jnp.where(even, other0[...], mine1[...]) - t_mm(u01, u01)
    factor_blocks(s[:HALF, :HALF], s[:HALF, HALF:], s[HALF:, HALF:], u_ref, x_ref)
    w_ref[...] = -mm(x_ref[...], t_mm(u01, x0[...]))


def store_row(a, loc_cols, pos, prow0, prow1, q0, q1, u0, u1, own, out):
    stride = 2 * loc_cols
    tile_row = pos[0] + a * pos[2]
    for b in range(loc_cols):
        tile_col = pos[1] + b * pos[3]

        def put(value, start=2 * b):
            out[pl.ds(start, NB, stride=stride), :] = value[:, :HALF]
            out[pl.ds(start + 1, NB, stride=stride), :] = value[:, HALF:]

        @pl.when(tile_row < tile_col)
        def _():
            put(jnp.zeros((NB, NB), jnp.float32))

        @pl.when((tile_row >= tile_col) & (tile_col >= 2))
        def _():
            put(
                tile_from(own, 2 * b, stride)
                - (mm(prow0, q0[b][...], HIGH) + mm(prow1, q1[b][...], HIGH))
            )

        if b == 0:

            @pl.when((tile_row > 0) & (tile_col == 0))
            def _():
                put(prow0)

            @pl.when((tile_row > 1) & (tile_col == 1))
            def _():
                put(prow1)

            if a == 0:

                @pl.when((tile_row == 0) & (tile_col == 0))
                def _():
                    put(u0[...].T)

                @pl.when((tile_row == 1) & (tile_col == 1))
                def _():
                    put(u1[...].T)


def panel_row(pos, left, right, x0, x1, w):
    even_col = pos[1] % 2 == 0
    l, r = left[...], right[...]
    b0, b1 = jnp.where(even_col, l, r), jnp.where(even_col, r, l)
    return mm_t(b0, x0[...], HIGH), mm_t(b0, w[...], HIGH) + mm_t(b1, x1[...], HIGH)


def columns_kernel(
    loc_cols, pos, own, left, right, mine_a, mine_b, other_a, other_b, u0, x0, u1, x1, w, out, *q
):
    stride = 2 * loc_cols
    even = pos[0] % 2 == 0

    def top_tile(a, b, start):
        halves = [
            jnp.concatenate(
                [ref[pl.ds(start + k, HALF, stride=stride), :] for k in (0, 1)], axis=1
            )
            for ref in (a, b)
        ]
        return jnp.concatenate(halves, axis=0)

    q0, q1 = q[:loc_cols], q[loc_cols:]
    for b in range(loc_cols):
        e, o = top_tile(mine_a, mine_b, 2 * b), top_tile(other_a, other_b, 2 * b)
        d0, d1 = jnp.where(even, e, o), jnp.where(even, o, e)
        q0[b][...] = mm(x0[...], d0, HIGH)
        q1[b][...] = mm(w[...], d0, HIGH) + mm(x1[...], d1, HIGH)
    prow0, prow1 = panel_row(pos, left, right, x0, x1, w)
    store_row(0, loc_cols, pos, prow0, prow1, q0, q1, u0, u1, own, out)


def later_kernel(a, loc_cols, pos, own, left, right, x0, x1, w, *rest):
    q, out = rest[: 2 * loc_cols], rest[-1]
    prow0, prow1 = panel_row(pos, left, right, x0, x1, w)
    store_row(
        a, loc_cols, pos, prow0, prow1, q[:loc_cols], q[loc_cols:], None, None, own, out
    )


VMEM = pl.BlockSpec(memory_space=pltpu.VMEM)
SMEM = pl.BlockSpec(memory_space=pltpu.SMEM)


def shape(*dims):
    return jax.ShapeDtypeStruct(dims, jnp.float32)


def call(
    kernel, out_shape, flops, *args, smem=0, vmem=16, specs=None, out_specs=None, aliases=None, grid=()
):
    return pl.pallas_call(
        kernel,
        grid=grid,
        out_shape=out_shape,
        in_specs=specs or [SMEM] * smem + [VMEM] * (len(args) - smem),
        out_specs=out_specs or jax.tree.map(lambda _: VMEM, out_shape),
        input_output_aliases=aliases or {},
        compiler_params=pltpu.CompilerParams(vmem_limit_bytes=vmem * 2**20),
        cost_estimate=pl.CostEstimate(flops=flops, bytes_accessed=2**22, transcendentals=0),
    )(*args)


def on_device(n_row, n_col, trailing_in):
    row = lax.axis_index("row")
    col = lax.axis_index("col")
    loc_rows, _, _, loc_cols, _, _ = trailing_in.shape
    stride = 2 * loc_cols
    chips = n_row // 2
    chip = row // 2
    own = trailing_in.reshape(loc_rows * NB * stride, HALF)
    pos = jnp.stack([row, col, jnp.int32(n_row), jnp.int32(n_col)]).astype(jnp.int32)
    row_bits = [1 << k for k in range(1, (n_row - 1).bit_length())]
    col_bits = [1 << k for k in range(1, (n_col - 1).bit_length())][::-1]
    after = lax.optimization_barrier

    def swap(value, axis, bits):
        size = n_row if axis == "row" else n_col
        return lax.ppermute(value, axis, [(i, i ^ bits) for i in range(size)])

    def pick(index, values):
        out = values[0]
        for k, value in enumerate(values[1:], 1):
            out = jnp.where(index == k, value, out)
        return out

    def settle(value, axis, bit, got):
        return jnp.where((row if axis == "row" else col) & bit != 0, got, value)

    half = HALF * stride
    top_a, top_b, *left = call(
        functools.partial(pack_kernel, loc_rows, loc_cols),
        [shape(half, HALF), shape(half, HALF)] + [shape(NB, NB)] * loc_rows,
        10**8,
        own,
    )

    size = NB // chips
    pieces = [left[0][k * size : (k + 1) * size] for k in range(chips)]
    got = [swap(pieces[k], "row", 2 * k) for k in range(1, chips)]
    piece = pick(chip, [pieces[0]] + got)
    along = [piece] + [swap(piece, "col", k) for k in range(1, n_col)]
    pair = jnp.concatenate([pick(col, along), pick(col ^ 1, along)], axis=0)
    left[0], top_a, top_b, pair = after((left[0], top_a, top_b, pair))
    got_left = [swap(left[0], "col", col_bits[0])]
    got_a, got_b = swap(top_a, "row", row_bits[0]), swap(top_b, "row", row_bits[-1])
    got = [pair] + [swap(pair, "row", 2 * k) for k in range(1, chips)]
    lead = [
        jnp.concatenate(
            [pick(chip ^ k, got)[j * size : (j + 1) * size] for k in range(chips)], axis=0
        )
        for j in (0, 1)
    ]
    lead_other = swap(jnp.where(row % 2 == 0, lead[0], lead[1]), "row", 1)

    def columns(a):
        value = settle(left[a], "col", col_bits[0], got_left[a])
        for bit in col_bits[1:]:
            value = settle(value, "col", bit, swap(value, "col", bit))
        return value, swap(value, "col", 1)

    u0, x0 = call(first_kernel, [shape(NB, NB)] * 2, 10**10, pos, lead[0], lead_other, smem=1)

    got_a, got_b, got_left, left[1:], lead[1], x0 = after(
        (got_a, got_b, got_left, left[1:], lead[1], x0)
    )
    lead_next = swap(lead[1], "row", 1)
    top_a = settle(top_a, "row", row_bits[0], got_a)
    top_b = settle(top_b, "row", row_bits[-1], got_b)
    for first, second in zip(row_bits[1:-1], row_bits[-2:0:-1]):
        top_a = settle(top_a, "row", first, swap(top_a, "row", first))
        top_b = settle(top_b, "row", second, swap(top_b, "row", second))
    got_a, got_b = swap(top_a, "row", row_bits[-1]), swap(top_b, "row", row_bits[0])
    got_left += [swap(value, "col", col_bits[0]) for value in left[1:]]
    both = [columns(0)]
    u1, x1, w = call(
        second_kernel,
        [shape(NB, NB)] * 3,
        10**10,
        pos, x0, lead[0], lead[1], lead_other, lead_next,
        smem=1,
    )
    got_a, got_b, both[0], x1 = after((got_a, got_b, both[0], x1))
    top_a = settle(top_a, "row", row_bits[-1], got_a)
    top_b = settle(top_b, "row", row_bits[0], got_b)
    other_a, other_b = swap(top_a, "row", 1), swap(top_b, "row", 1)
    got_left[1:], x1 = after((got_left[1:], x1))
    both += [columns(a) for a in range(1, loc_rows)]

    def block(a):
        return pl.BlockSpec((NB * stride, HALF), lambda i: (a, 0))

    out, *q = call(
        functools.partial(columns_kernel, loc_cols),
        [shape(*own.shape)] + [shape(NB, NB)] * (2 * loc_cols),
        10**9,
        pos, own, *both[0], top_a, top_b, other_a, other_b, u0, x0, u1, x1, w,
        specs=[SMEM, block(0)] + [VMEM] * 11,
        out_specs=[block(0)] + [VMEM] * (2 * loc_cols),
        grid=(1,),
        vmem=24,
    )
    for a in range(1, loc_rows):
        out = call(
            functools.partial(later_kernel, a, loc_cols),
            shape(*own.shape),
            10**7,
            pos, own, *both[a], x0, x1, w, *q, out,
            specs=[SMEM, block(a)] + [VMEM] * (5 + 2 * loc_cols) + [pl.BlockSpec(memory_space=pl.ANY)],
            out_specs=block(a),
            aliases={7 + 2 * loc_cols: 0},
            grid=(1,),
        )
    return out.reshape(trailing_in.shape)


def solution(mesh):
    return jax.shard_map(
        functools.partial(on_device, mesh.shape["row"], mesh.shape["col"]),
        mesh=mesh,
        in_specs=(P(None, "row", None, None, "col", None),),
        out_specs=P(None, "row", None, None, "col", None),
        check_vma=False,
    )
```

```python
import functools

import jax
import jax.numpy as jnp
from jax import lax
from jax.experimental import pallas as pl
from jax.experimental.pallas import tpu as pltpu
from jax.sharding import PartitionSpec as P

NB = 256
HALF = 128
SUB = 8
HIGHEST = lax.Precision.HIGHEST
HIGH = lax.Precision.HIGH


def mm(a, b, precision=HIGHEST):
    return lax.dot_general(
        a, b, (((1,), (0,)), ((), ())), precision=precision, preferred_element_type=jnp.float32
    )


def mm_t(a, b, precision=HIGHEST):
    return lax.dot_general(
        a, b, (((1,), (1,)), ((), ())), precision=precision, preferred_element_type=jnp.float32
    )


def t_mm(a, b, precision=HIGHEST):
    return lax.dot_general(
        a, b, (((0,), (0,)), ((), ())), precision=precision, preferred_element_type=jnp.float32
    )


def spread(x):
    return jnp.broadcast_to(x, (SUB, HALF))


def factor_half(s):
    groups = HALF // SUB
    lane = lax.broadcasted_iota(jnp.int32, (SUB, HALF), 1)
    sub = lax.broadcasted_iota(jnp.int32, (SUB, HALF), 0)
    rows = [s[SUB * g : SUB * (g + 1), :] for g in range(groups)]
    own_diagonal = [jnp.where(lane == sub + SUB * g, rows[g], 0.0) for g in range(groups)]
    diagonal = spread(jnp.sum(sum(own_diagonal), axis=0, keepdims=True))
    scale = lax.rsqrt(diagonal)
    unscale = diagonal * scale
    eyes = []
    for g in range(groups):
        down = spread(lax.rsqrt(jnp.sum(own_diagonal[g], axis=1, keepdims=True)))
        rows[g] = (rows[g] * scale) * down
        eyes.append(jnp.where(lane == sub + SUB * g, 1.0, 0.0).astype(jnp.float32))
    out_u, out_x = [], []
    for g in range(groups):
        base = SUB * g
        own = rows[g]
        own_x = eyes[g]
        a = {}
        for j in range(SUB):
            column = spread(own[:, base + j : base + j + 1])
            for i in range(j + 1):
                a[i, j] = spread(column[i : i + 1, :])
        near = None
        if g + 1 < groups:
            near = [spread(rows[g + 1][:, base + j : base + j + 1]) for j in range(SUB)]
        u = [spread(own[i : i + 1, :]) for i in range(SUB)]
        x = [spread(own_x[i : i + 1, :]) for i in range(SUB)]
        r = [None] * SUB
        l = {}
        for k in range(0, SUB, 2):
            p, q, t = a[k, k], a[k, k + 1], a[k + 1, k + 1]
            r[k] = lax.rsqrt(p)
            root = lax.rsqrt(p * t - q * q)
            both = r[k] * root
            r[k + 1] = (p * r[k]) * root
            l[k, k + 1] = q * r[k]
            for j in range(k + 2, SUB):
                l[k, j] = a[k, j] * r[k]
                l[k + 1, j] = (p * a[k + 1, j] - q * a[k, j]) * both
            for i in range(k + 2, SUB):
                for j in range(i, SUB):
                    a[i, j] = (a[i, j] - l[k, i] * l[k, j]) - l[k + 1, i] * l[k + 1, j]
            for m in (k, k + 1):
                u[m] = u[m] * r[m]
                x[m] = x[m] * r[m]
                if near is not None:
                    near[m] = near[m] * r[m]
                for i in range(m + 1, SUB):
                    u[i] = u[i] - l[m, i] * u[m]
                    x[i] = x[i] - l[m, i] * x[m]
                    if near is not None:
                        near[i] = near[i] - l[m, i] * near[m]
        final_u, final_x = u[0], x[0]
        for i in range(1, SUB):
            final_u = jnp.where(sub == i, u[i], final_u)
            final_x = jnp.where(sub == i, x[i], final_x)
        out_u.append(jnp.where(lane >= sub + base, final_u * unscale, 0.0))
        out_x.append(final_x * scale)
        if near is not None:
            nxt, nxt_x = rows[g + 1], eyes[g + 1]
            for k in range(SUB):
                nxt = nxt - near[k] * u[k]
                nxt_x = nxt_x - near[k] * x[k]
        if g + 2 < groups:
            v, vx = list(u), list(x)
            for i in reversed(range(SUB)):
                for j in range(i + 1, SUB):
                    v[i] = v[i] - l[i, j] * v[j]
                    vx[i] = vx[i] - l[i, j] * vx[j]
                v[i] = v[i] * r[i]
                vx[i] = vx[i] * r[i]
            for h in range(g + 2, groups):
                far, far_x = rows[h], eyes[h]
                for j in range(SUB):
                    c = spread(rows[h][:, base + j : base + j + 1])
                    far = far - c * v[j]
                    far_x = far_x - c * vx[j]
                rows[h], eyes[h] = far, far_x
        if near is not None:
            rows[g + 1], eyes[g + 1] = nxt, nxt_x
    return jnp.concatenate(out_u, axis=0), jnp.concatenate(out_x, axis=0)


def finish_blocks(u11, u12, x11, rest, u_ref, x_ref):
    zero = jnp.zeros((HALF, HALF), jnp.float32)
    u22, x22 = factor_half(rest)
    u_ref[:HALF, :HALF] = u11
    u_ref[:HALF, HALF:] = u12
    u_ref[HALF:, :HALF] = zero
    u_ref[HALF:, HALF:] = u22
    x_ref[:HALF, :HALF] = x11
    x_ref[:HALF, HALF:] = zero
    x_ref[HALF:, :HALF] = -mm(x22, t_mm(u12, x11))
    x_ref[HALF:, HALF:] = x22


def factor_blocks(s11, s12, s22, u_ref, x_ref):
    u11, x11 = factor_half(s11)
    u12 = mm(x11, s12)
    finish_blocks(u11, u12, x11, s22 - t_mm(u12, u12), u_ref, x_ref)


def tile_from(ref, start, stride):
    return jnp.concatenate(
        [ref[pl.ds(start, NB, stride=stride), :], ref[pl.ds(start + 1, NB, stride=stride), :]], axis=1
    )


def pack_kernel(loc_rows, loc_cols, own, top_a, top_b, *left):
    stride = 2 * loc_cols
    for a in range(loc_rows):
        left[a][...] = tile_from(own, a * NB * stride, stride)
    half = HALF * stride
    top_a[...] = own[:half, :]
    top_b[...] = own[half : 2 * half, :]


def first_kernel(pos, mine, other, u_ref, x_ref):
    s = jnp.where(pos[0] % 2 == 0, mine[...], other[...])
    factor_blocks(s[:HALF, :HALF], s[:HALF, HALF:], s[HALF:, HALF:], u_ref, x_ref)


def second_kernel(pos, x0, mine0, mine1, other0, other1, u_ref, x_ref, w_ref):
    even = pos[0] % 2 == 0
    u01 = mm(x0[...], jnp.where(even, mine1[...], other1[...]))
    s = jnp.where(even, other0[...], mine1[...]) - t_mm(u01, u01)
    factor_blocks(s[:HALF, :HALF], s[:HALF, HALF:], s[HALF:, HALF:], u_ref, x_ref)
    w_ref[...] = -mm(x_ref[...], t_mm(u01, x0[...]))


def store_row(a, loc_cols, pos, prow0, prow1, q0, q1, u0, u1, own, out):
    stride = 2 * loc_cols
    tile_row = pos[0] + a * pos[2]
    for b in range(loc_cols):
        tile_col = pos[1] + b * pos[3]

        def put(value, start=2 * b):
            out[pl.ds(start, NB, stride=stride), :] = value[:, :HALF]
            out[pl.ds(start + 1, NB, stride=stride), :] = value[:, HALF:]

        @pl.when(tile_row < tile_col)
        def _():
            put(jnp.zeros((NB, NB), jnp.float32))

        @pl.when((tile_row >= tile_col) & (tile_col >= 2))
        def _():
            put(
                tile_from(own, 2 * b, stride)
                - (mm(prow0, q0[b][...], HIGH) + mm(prow1, q1[b][...], HIGH))
            )

        if b == 0:

            @pl.when((tile_row > 0) & (tile_col == 0))
            def _():
                put(prow0)

            @pl.when((tile_row > 1) & (tile_col == 1))
            def _():
                put(prow1)

            if a == 0:

                @pl.when((tile_row == 0) & (tile_col == 0))
                def _():
                    put(u0[...].T)

                @pl.when((tile_row == 1) & (tile_col == 1))
                def _():
                    put(u1[...].T)


def panel_row(pos, left, right, x0, x1, w):
    even_col = pos[1] % 2 == 0
    l, r = left[...], right[...]
    b0, b1 = jnp.where(even_col, l, r), jnp.where(even_col, r, l)
    return mm_t(b0, x0[...], HIGH), mm_t(b0, w[...], HIGH) + mm_t(b1, x1[...], HIGH)


def columns_kernel(
    loc_cols, pos, own, left, right, mine_a, mine_b, other_a, other_b, u0, x0, u1, x1, w, out, *q
):
    stride = 2 * loc_cols
    even = pos[0] % 2 == 0

    def top_tile(a, b, start):
        halves = [
            jnp.concatenate(
                [ref[pl.ds(start + k, HALF, stride=stride), :] for k in (0, 1)], axis=1
            )
            for ref in (a, b)
        ]
        return jnp.concatenate(halves, axis=0)

    q0, q1 = q[:loc_cols], q[loc_cols:]
    for b in range(loc_cols):
        e, o = top_tile(mine_a, mine_b, 2 * b), top_tile(other_a, other_b, 2 * b)
        d0, d1 = jnp.where(even, e, o), jnp.where(even, o, e)
        q0[b][...] = mm(x0[...], d0, HIGH)
        q1[b][...] = mm(w[...], d0, HIGH) + mm(x1[...], d1, HIGH)
    prow0, prow1 = panel_row(pos, left, right, x0, x1, w)
    store_row(0, loc_cols, pos, prow0, prow1, q0, q1, u0, u1, own, out)


def later_kernel(a, loc_cols, pos, own, left, right, x0, x1, w, *rest):
    q, out = rest[: 2 * loc_cols], rest[-1]
    prow0, prow1 = panel_row(pos, left, right, x0, x1, w)
    store_row(
        a, loc_cols, pos, prow0, prow1, q[:loc_cols], q[loc_cols:], None, None, own, out
    )


VMEM = pl.BlockSpec(memory_space=pltpu.VMEM)
SMEM = pl.BlockSpec(memory_space=pltpu.SMEM)


def shape(*dims):
    return jax.ShapeDtypeStruct(dims, jnp.float32)


def call(
    kernel, out_shape, flops, *args, smem=0, vmem=16, specs=None, out_specs=None, aliases=None, grid=()
):
    return pl.pallas_call(
        kernel,
        grid=grid,
        out_shape=out_shape,
        in_specs=specs or [SMEM] * smem + [VMEM] * (len(args) - smem),
        out_specs=out_specs or jax.tree.map(lambda _: VMEM, out_shape),
        input_output_aliases=aliases or {},
        compiler_params=pltpu.CompilerParams(vmem_limit_bytes=vmem * 2**20),
        cost_estimate=pl.CostEstimate(flops=flops, bytes_accessed=2**22, transcendentals=0),
    )(*args)


def on_device(n_row, n_col, trailing_in):
    row = lax.axis_index("row")
    col = lax.axis_index("col")
    loc_rows, _, _, loc_cols, _, _ = trailing_in.shape
    stride = 2 * loc_cols
    chips = n_row // 2
    chip = row // 2
    own = trailing_in.reshape(loc_rows * NB * stride, HALF)
    pos = jnp.stack([row, col, jnp.int32(n_row), jnp.int32(n_col)]).astype(jnp.int32)
    row_bits = [1 << k for k in range(1, (n_row - 1).bit_length())]
    col_bits = [1 << k for k in range(1, (n_col - 1).bit_length())][::-1]
    after = lax.optimization_barrier

    def swap(value, axis, bits):
        size = n_row if axis == "row" else n_col
        return lax.ppermute(value, axis, [(i, i ^ bits) for i in range(size)])

    def pick(index, values):
        out = values[0]
        for k, value in enumerate(values[1:], 1):
            out = jnp.where(index == k, value, out)
        return out

    def settle(value, axis, bit, got):
        return jnp.where((row if axis == "row" else col) & bit != 0, got, value)

    half = HALF * stride
    top_a, top_b, *left = call(
        functools.partial(pack_kernel, loc_rows, loc_cols),
        [shape(half, HALF), shape(half, HALF)] + [shape(NB, NB)] * loc_rows,
        10**8,
        own,
    )

    size = NB // chips
    pieces = [left[0][k * size : (k + 1) * size] for k in range(chips)]
    got = [swap(pieces[k], "row", 2 * k) for k in range(1, chips)]
    top_a, top_b, got = after((top_a, top_b, got))
    got_a, got_b = swap(top_a, "row", row_bits[0]), swap(top_b, "row", row_bits[-1])
    piece = pick(chip, [pieces[0]] + got)
    along = [piece] + [swap(piece, "col", k) for k in range(1, n_col)]
    got_a, got_b, along = after((got_a, got_b, along))
    pair = jnp.concatenate([pick(col, along), pick(col ^ 1, along)], axis=0)
    left[0], pair = after((left[0], pair))
    got_left = [swap(left[0], "col", col_bits[0])]
    got = [pair] + [swap(pair, "row", 2 * k) for k in range(1, chips)]
    lead = [
        jnp.concatenate(
            [pick(chip ^ k, got)[j * size : (j + 1) * size] for k in range(chips)], axis=0
        )
        for j in (0, 1)
    ]
    lead_other = swap(jnp.where(row % 2 == 0, lead[0], lead[1]), "row", 1)

    def columns(a):
        value = settle(left[a], "col", col_bits[0], got_left[a])
        for bit in col_bits[1:]:
            value = settle(value, "col", bit, swap(value, "col", bit))
        return value, swap(value, "col", 1)

    top_a, top_b, lead[0] = after((top_a, top_b, lead[0]))
    top_a = settle(top_a, "row", row_bits[0], got_a)
    top_b = settle(top_b, "row", row_bits[-1], got_b)
    for first, second in zip(row_bits[1:-1], row_bits[-2:0:-1]):
        top_a = settle(top_a, "row", first, swap(top_a, "row", first))
        top_b = settle(top_b, "row", second, swap(top_b, "row", second))
    got_a, got_b = swap(top_a, "row", row_bits[-1]), swap(top_b, "row", row_bits[0])
    u0, x0 = call(first_kernel, [shape(NB, NB)] * 2, 10**10, pos, lead[0], lead_other, smem=1)

    got_left, left[1:], lead[1], x0 = after((got_left, left[1:], lead[1], x0))
    lead_next = swap(lead[1], "row", 1)
    got_left += [swap(value, "col", col_bits[0]) for value in left[1:]]
    both = [columns(0)]
    u1, x1, w = call(
        second_kernel,
        [shape(NB, NB)] * 3,
        10**10,
        pos, x0, lead[0], lead[1], lead_other, lead_next,
        smem=1,
    )
    got_a, got_b, both[0], x1 = after((got_a, got_b, both[0], x1))
    top_a = settle(top_a, "row", row_bits[-1], got_a)
    top_b = settle(top_b, "row", row_bits[0], got_b)
    other_a, other_b = swap(top_a, "row", 1), swap(top_b, "row", 1)
    got_left[1:], x1 = after((got_left[1:], x1))
    both += [columns(a) for a in range(1, loc_rows)]

    def block(a):
        return pl.BlockSpec((NB * stride, HALF), lambda i: (a, 0))

    out, *q = call(
        functools.partial(columns_kernel, loc_cols),
        [shape(*own.shape)] + [shape(NB, NB)] * (2 * loc_cols),
        10**9,
        pos, own, *both[0], top_a, top_b, other_a, other_b, u0, x0, u1, x1, w,
        specs=[SMEM, block(0)] + [VMEM] * 11,
        out_specs=[block(0)] + [VMEM] * (2 * loc_cols),
        grid=(1,),
        vmem=24,
    )
    for a in range(1, loc_rows):
        out = call(
            functools.partial(later_kernel, a, loc_cols),
            shape(*own.shape),
            10**7,
            pos, own, *both[a], x0, x1, w, *q, out,
            specs=[SMEM, block(a)] + [VMEM] * (5 + 2 * loc_cols) + [pl.BlockSpec(memory_space=pl.ANY)],
            out_specs=block(a),
            aliases={7 + 2 * loc_cols: 0},
            grid=(1,),
        )
    return out.reshape(trailing_in.shape)


def solution(mesh):
    return jax.shard_map(
        functools.partial(on_device, mesh.shape["row"], mesh.shape["col"]),
        mesh=mesh,
        in_specs=(P(None, "row", None, None, "col", None),),
        out_specs=P(None, "row", None, None, "col", None),
        check_vma=False,
    )
```
